32 devices in a mesh: groups: 2 (over x), wide: 8 (over z, y), narrow: 2 (over core).
Axes of the slice: x: 2, y: 2, z: 4, core: 2. Of those that a mesh axis runs over, the one named last changes fastest.
Arguments:
- context_symbol_ids: int32 [2, 16, 16], P('narrow', 'groups'), parts along dimension 1, may hold values from 0 to 32767
- context_symbol_spans: int32 [2, 16], P('narrow', 'groups'), parts along dimension 1, may hold values from 1 to 16, as said below
- symbol_vector_lookup: bfloat16 [4096, 32768], P('wide'), may hold values from -6 to 6
- opening_lagged_blend: float32 [4096], replicated, may hold values from 0 to 1
- lagged_blend_weights: float32 [3, 4096], replicated, may hold values from 0 to 1
- blending_left_operand: bfloat16 [4096, 192], replicated, may hold values from -0.09375 to 0.09375
- blending_right_operands: bfloat16 [3, 64, 4096], replicated, may hold values from -0.375 to 0.375
- fixed_fading_scores: float32 [4096], P('wide'), may hold values from -6 to -1
- fading_left_operand: bfloat16 [4096, 128], replicated, may hold values from -0.09375 to 0.09375
- fading_right_operand: bfloat16 [128, 4096], P(None, 'wide'), may hold values from -0.5 to 0.5
- address_projector: bfloat16 [4096, 4096], P('wide'), may hold values from -0.09375 to 0.09375
- payload_projector: bfloat16 [4096, 4096], P('wide'), may hold values from -0.09375 to 0.09375
- present_symbol_reward: float32 [64, 64], replicated, may hold values from -1 to 1
- cluster_scaling_weight: float32 [4096], replicated, may hold values from 0.5 to 1.5
- cluster_scaling_offset: float32 [4096], replicated, may hold values from -3 to 3
- generated_acceptance: bfloat16 [2, 16, 4, 4096], P(None, ('groups', 'wide'), None, 'narrow'), parts along dimension 1, may hold values from -6 to 6
- generated_addresses: bfloat16 [2, 16, 4, 4096], P(None, ('groups', 'wide'), None, 'narrow'), parts along dimension 1, may hold values from -6 to 6
- generated_payloads: bfloat16 [2, 16, 4, 4096], P(None, ('groups', 'wide'), None, 'narrow'), parts along dimension 1, may hold values from -6 to 6
- generated_fading_scores: bfloat16 [2, 16, 4, 4096], P(None, ('groups', 'wide'), None, 'narrow'), parts along dimension 1, may hold values from -6 to -1
- generated_valve_scores: bfloat16 [2, 16, 4, 4096], P(None, ('groups', 'wide'), None, 'narrow'), parts along dimension 1, may hold values from -6 to 6
Outputs:
- dec_out: bfloat16 [2, 16, 4, 4096], P(None, ('groups', 'wide'), None, 'narrow'), parts along dimension 1
The draws below stay inside these ranges and needn't reach their ends.
There are 2 independent parts, one for each index of `groups`. The reference program is written for one: setup_inputs(seed, part) draws one part's arguments, and reference() takes and returns one part's arrays. A program takes and returns all parts, laid end to end along the dimension named above; an argument that names none is the same for every part. Nothing has to cross between parts.
Inputs may be any that keep to these rules, and one draw needn't show every extreme that they name: `context_symbol_spans`: positions at or past a prompt's length are padding. In every draw one of the 2 banks, chosen by the draw, holds only prompts of exactly 16 tokens, and every other bank holds at least one prompt of 16 tokens.
All inputs are finite; a program needn't handle non-finite values.
Results may differ from the reference program's by a relative error of at most 0.0095.
Values may be sent and summed in bfloat16 or wider, within the bound.
A program may use at most 128 MiB of HBM per device.

```python
import jax
import jax.numpy as jnp
from jax import lax

ATTENDER_SUM = 64
WIDTH_OF_UNIT = 64
MIX = 64
DLORA = 128
V = 32768
L = 16
STEPS = 4
D = 4096
BANKS = 2
BANK_ROWS = 8


def full_bank(key):
    return jax.random.randint(jax.random.fold_in(key, 7), (), 0, BANKS)


def draw_context_symbol_spans(key, part):
    first_key, second_key = jax.random.split(jax.random.fold_in(key, 11))
    random_lengths = jax.random.randint(first_key, (BANKS, BANK_ROWS), 1, L + 1)
    chosen = jax.random.randint(second_key, (BANKS, 1), 0, BANK_ROWS)
    places = lax.broadcasted_iota(jnp.int32, (BANKS, BANK_ROWS), 1)
    ragged = jnp.where(places == chosen, L, random_lengths)
    banks = lax.broadcasted_iota(jnp.int32, (BANKS, BANK_ROWS), 0)
    return jnp.where(banks == full_bank(key), L, ragged).astype(jnp.int32)


def draw_context_symbol_ids(key, part):
    keys = jax.random.split(jax.random.fold_in(key, 23), 5)
    shape = (BANKS, BANK_ROWS, L)
    ceiling = jax.random.randint(keys[0], shape, 1, V + 1)
    ranks = jax.random.randint(keys[1], shape, 0, ceiling)
    common = jax.random.permutation(keys[2], jnp.arange(V, dtype=jnp.int32))[ranks]
    count = BANK_ROWS * L
    middle = jax.random.permutation(keys[3], jnp.arange(1, V - 1, dtype=jnp.int32))[:count - 2]
    ends = jnp.array([0, V - 1], jnp.int32)
    distinct = jax.random.permutation(keys[4], jnp.concatenate([ends, middle])).reshape(1, BANK_ROWS, L)
    banks = lax.broadcasted_iota(jnp.int32, (BANKS, 1, 1), 0)
    return jnp.where(banks == full_bank(key), distinct, common).astype(jnp.int32)


def block_scale(stream_key, dims, shards, low, top_value):
    def one(dim, blocks):
        heights = jax.random.uniform(jax.random.fold_in(jax.random.fold_in(stream_key, 6), dim), (blocks,), jnp.float32, low / len(shards), top_value / len(shards))
        return jnp.repeat(jnp.exp(heights), dims[dim] // blocks).reshape((-1,) + (1,) * (len(dims) - dim - 1))

    level = one(*shards[0])
    for cut in shards[1:]:
        level = level * one(*cut)
    return level


def noise(own_key, extent, scale, most, shards=(), held_as=jnp.bfloat16):
    factor_of = block_scale(own_key, extent, shards, -0.22, 0.18) if shards else 1.0
    values = jax.random.normal(own_key, extent, jnp.float32) * scale * factor_of
    return jnp.minimum(jnp.maximum(values, -most), most).astype(held_as)


def setup_inputs(seed: int = 0, part: int = 0) -> dict:
    key_list = jax.random.split(jax.random.key(seed), 21)
    own_keys = jax.random.split(jax.random.fold_in(key_list[20], part), 21)
    return {
        "context_symbol_ids": draw_context_symbol_ids(jax.random.fold_in(jax.random.fold_in(key_list[20], part), 71), part),
        "context_symbol_spans": draw_context_symbol_spans(jax.random.fold_in(jax.random.fold_in(key_list[20], part), 71), part),
        "symbol_vector_lookup": noise(key_list[2], (D, V), 1.0, 6.0, ((0, 8),)),
        "opening_lagged_blend": jnp.clip(jax.random.uniform(key_list[3], (D,), jnp.float32, 0.0, 1.0), 0.0, 1.0),
        "lagged_blend_weights": jnp.clip(jax.random.uniform(key_list[4], (3, D), jnp.float32, 0.0, 1.0), 0.0, 1.0),
        "blending_left_operand": noise(key_list[5], (D, 3 * MIX), D ** -0.5, 0.09375),
        "blending_right_operands": noise(key_list[6], (3, MIX, D), (4 * MIX) ** -0.5, 0.375),
        "fixed_fading_scores": jnp.clip(-6.0 + 5.0 * jax.random.uniform(key_list[7], (D,), jnp.float32) ** block_scale(key_list[7], (D,), ((0, 8),), -0.2, 0.2), -6.0, -1.0),
        "fading_left_operand": noise(key_list[8], (D, DLORA), D ** -0.5, 0.09375),
        "fading_right_operand": noise(key_list[9], (DLORA, D), DLORA ** -0.5, 0.5, ((1, 8),)),
        "address_projector": noise(key_list[10], (D, D), D ** -0.5, 0.09375, ((0, 8),)),
        "payload_projector": noise(key_list[11], (D, D), D ** -0.5, 0.09375, ((0, 8),)),
        "present_symbol_reward": jnp.clip(jax.random.uniform(key_list[12], (ATTENDER_SUM, WIDTH_OF_UNIT), jnp.float32, -1.0, 1.0), -1.0, 1.0),
        "cluster_scaling_weight": jnp.clip(jax.random.uniform(key_list[13], (D,), jnp.float32, 0.5, 1.5), 0.5, 1.5),
        "cluster_scaling_offset": noise(key_list[14], (D,), 0.5, 3.0, (), jnp.float32),
        "generated_acceptance": noise(own_keys[15], (BANKS, BANK_ROWS, STEPS, D), 1.0, 6.0, ((1, 8), (3, 2))),
        "generated_addresses": noise(own_keys[16], (BANKS, BANK_ROWS, STEPS, D), 1.0, 6.0, ((1, 8), (3, 2))),
        "generated_payloads": noise(own_keys[17], (BANKS, BANK_ROWS, STEPS, D), 1.0, 6.0, ((1, 8), (3, 2))),
        "generated_fading_scores": jnp.clip(-6.0 + 5.0 * jax.random.uniform(own_keys[18], (BANKS, BANK_ROWS, STEPS, D), jnp.float32) ** block_scale(own_keys[18], (BANKS, BANK_ROWS, STEPS, D), ((1, 8), (3, 2)), -0.2, 0.2), -6.0, -1.0).astype(jnp.bfloat16),
        "generated_valve_scores": noise(own_keys[19], (BANKS, BANK_ROWS, STEPS, D), 1.0, 6.0, ((1, 8), (3, 2))),
    }


norm_eps = 0.00064

def mix_project(embedded, opening_lagged_blend, lagged_blend_weights, blending_left_operand, blending_right_operands, fixed_fading_scores, fading_left_operand, fading_right_operand, address_projector, payload_projector):
    features = embedded.shape[2]
    previous = jnp.pad(embedded, ((0, 0), (1, 0), (0, 0)))[:, :-1, :]
    current = embedded.reshape(-1, features).astype(jnp.float32)
    difference = previous.reshape(-1, features).astype(jnp.float32) - current
    mixed_in = (current + difference * opening_lagged_blend).astype(jnp.bfloat16)
    hidden = jnp.tanh(jnp.dot(mixed_in, blending_left_operand, preferred_element_type=jnp.float32)).astype(jnp.bfloat16)
    rank_size = blending_right_operands.shape[1]
    branches = []
    for branch in range(3):
        shift_term = jnp.dot(hidden[:, branch * rank_size:(branch + 1) * rank_size], blending_right_operands[branch], preferred_element_type=jnp.float32)
        branches.append((current + difference * (lagged_blend_weights[branch] + shift_term)).astype(jnp.bfloat16))
    decay_hidden = jnp.tanh(jnp.dot(branches[0], fading_left_operand, preferred_element_type=jnp.float32)).astype(jnp.bfloat16)
    decay_log = fixed_fading_scores + jnp.dot(decay_hidden, fading_right_operand, preferred_element_type=jnp.float32)
    key_proj = jnp.dot(branches[1], address_projector.T, preferred_element_type=jnp.float32).astype(jnp.bfloat16)
    value_proj = jnp.dot(branches[2], payload_projector.T, preferred_element_type=jnp.float32).astype(jnp.bfloat16)
    return (key_proj, value_proj, decay_log)

def prefill_states(key_proj, value_proj, decay_log, lengths, attender_ordinal, attender_width):
    bank_count, bank_rows, length, features = key_proj.shape
    split_shape = (bank_count, bank_rows, length, attender_ordinal, attender_width)
    key_split = jnp.moveaxis(key_proj.astype(jnp.float32).reshape(split_shape), 2, 0)
    valued = jnp.moveaxis(value_proj.astype(jnp.float32).reshape(split_shape), 2, 0)
    factors = jnp.moveaxis(jnp.exp(-jnp.exp(decay_log)).reshape(split_shape), 2, 0)
    places = lax.iota(jnp.int32, length)
    live_mask = places[:, None, None] < lengths[None, :, :]

    def advance(recurrent_memories, inputs):
        present_address, present_payload, factor_now, live_now = inputs
        updated = factor_now[..., :, None] * recurrent_memories + present_address[..., :, None] * present_payload[..., None, :]
        return (jnp.where(live_now[:, :, None, None, None], updated, recurrent_memories), None)
    initial = jnp.zeros((bank_count, bank_rows, attender_ordinal, attender_width, attender_width), jnp.float32)
    recurrent_memories, unused = lax.scan(advance, initial, (key_split, valued, factors, live_mask))
    return recurrent_memories

def generation_iterations(recurrent_memories, acceptance_lines, address_source, payload_source, fading_source, valve_source, shard_reward, shard_scaling_weight, shard_scaling_offset):
    attender_ordinal = recurrent_memories.shape[-3]
    attender_width = recurrent_memories.shape[-1]
    leading = acceptance_lines.shape[:-2]
    step_count = acceptance_lines.shape[-2]
    split_shape = leading + (step_count, attender_ordinal, attender_width)
    receptance = acceptance_lines.astype(jnp.float32).reshape(split_shape)
    key_split = address_source.astype(jnp.float32).reshape(split_shape)
    valued = payload_source.astype(jnp.float32).reshape(split_shape)
    factors = jnp.exp(-jnp.exp(fading_source.astype(jnp.float32))).reshape(split_shape)
    results = []
    for position in range(step_count):
        present_acceptance = receptance[..., position, :, :]
        present_address = key_split[..., position, :, :]
        present_payload = valued[..., position, :, :]
        immediate_summand = lax.optimization_barrier(jnp.sum(present_acceptance * shard_reward * present_address, axis=-1, keepdims=True)) * present_payload
        carried = jnp.einsum('...hi,...hij->...hj', present_acceptance, recurrent_memories, precision=lax.Precision.HIGHEST)
        results.append(carried + immediate_summand)
        if position + 1 < step_count:
            recurrent_memories = factors[..., position, :, :][..., :, None] * recurrent_memories + present_address[..., :, None] * present_payload[..., None, :]
    mixed_out = jnp.stack(results, axis=-3)
    average = lax.optimization_barrier(jnp.mean(mixed_out, axis=-1, keepdims=True))
    centred = mixed_out - average
    spread = lax.optimization_barrier(jnp.mean(centred * centred, axis=-1, keepdims=True))
    normed = (centred * lax.rsqrt(spread + norm_eps)).reshape(leading + (step_count, attender_ordinal * attender_width))
    return ((normed * shard_scaling_weight + shard_scaling_offset) * jax.nn.silu(valve_source.astype(jnp.float32))).astype(jnp.bfloat16)

def reference(context_symbol_ids, context_symbol_spans, symbol_vector_lookup, opening_lagged_blend, lagged_blend_weights, blending_left_operand, blending_right_operands, fixed_fading_scores, fading_left_operand, fading_right_operand, address_projector, payload_projector, present_symbol_reward, cluster_scaling_weight, cluster_scaling_offset, generated_acceptance, generated_addresses, generated_payloads, generated_fading_scores, generated_valve_scores):
    bank_count, bank_rows, length = context_symbol_ids.shape
    features = symbol_vector_lookup.shape[0]
    attender_ordinal, attender_width = present_symbol_reward.shape
    picked = jnp.take(symbol_vector_lookup, context_symbol_ids.reshape(-1), axis=1)
    embedded = picked.T.reshape(bank_count * bank_rows, length, features)
    key_proj, value_proj, decay_log = mix_project(embedded, opening_lagged_blend, lagged_blend_weights, blending_left_operand, blending_right_operands, fixed_fading_scores, fading_left_operand, fading_right_operand, address_projector, payload_projector)
    shaped = (bank_count, bank_rows, length, features)
    recurrent_memories = prefill_states(key_proj.reshape(shaped), value_proj.reshape(shaped), decay_log.reshape(shaped), context_symbol_spans, attender_ordinal, attender_width)
    return generation_iterations(recurrent_memories, generated_acceptance, generated_addresses, generated_payloads, generated_fading_scores, generated_valve_scores, present_symbol_reward, cluster_scaling_weight, cluster_scaling_offset)
```

```python
import functools

import jax
import jax.numpy as jnp
from jax import lax
from jax.experimental import pallas as pl
from jax.experimental.pallas import tpu as pltpu
from jax.sharding import PartitionSpec as P

norm_eps = 0.00064
lane_count = 128


def mix_project(
    embedded,
    opening_lagged_blend,
    lagged_blend_weights,
    blending_left_operand,
    blending_right_operands,
    fixed_fading_scores,
    fading_left_operand,
    fading_right_operand,
    address_projector,
    payload_projector,
):
    features = embedded.shape[2]
    previous = jnp.pad(embedded, ((0, 0), (1, 0), (0, 0)))[:, :-1, :]
    current = embedded.reshape(-1, features).astype(jnp.float32)
    difference = previous.reshape(-1, features).astype(jnp.float32) - current
    mixed_in = (current + difference * opening_lagged_blend).astype(jnp.bfloat16)
    hidden = jnp.tanh(
        jnp.dot(mixed_in, blending_left_operand, preferred_element_type=jnp.float32)
    ).astype(jnp.bfloat16)
    rank_size = blending_right_operands.shape[1]
    branches = []
    for branch in range(3):
        shift_term = jnp.dot(
            hidden[:, branch * rank_size : (branch + 1) * rank_size],
            blending_right_operands[branch],
            preferred_element_type=jnp.float32,
        )
        branches.append(
            (current + difference * (lagged_blend_weights[branch] + shift_term)).astype(
                jnp.bfloat16
            )
        )
    decay_hidden = jnp.tanh(
        jnp.dot(branches[0], fading_left_operand, preferred_element_type=jnp.float32)
    ).astype(jnp.bfloat16)
    decay_log = fixed_fading_scores + jnp.dot(
        decay_hidden, fading_right_operand, preferred_element_type=jnp.float32
    )
    key_proj = jnp.dot(branches[1], address_projector.T, preferred_element_type=jnp.float32).astype(
        jnp.bfloat16
    )
    value_proj = jnp.dot(
        branches[2], payload_projector.T, preferred_element_type=jnp.float32
    ).astype(jnp.bfloat16)
    return (key_proj, value_proj, decay_log)


def final_states(key_proj, value_proj, decay_log, lengths, attender_width):
    bank_rows, length, columns = key_proj.shape
    attender_ordinal = columns // attender_width
    decay_rates = jnp.exp(decay_log)
    places = lax.broadcasted_iota(jnp.int32, (bank_rows, length), 1)
    live_mask = (places < lengths[:, None])[:, :, None]
    running = jnp.cumsum(jnp.where(live_mask, decay_rates, 0.0), axis=1)
    remaining = running[:, -1:, :] - running
    weights = jnp.where(live_mask, jnp.exp(-remaining), 0.0)
    weighted = (key_proj.astype(jnp.float32) * weights).reshape(
        bank_rows, length, attender_ordinal, attender_width
    )
    plain_values = value_proj.astype(jnp.float32).reshape(
        bank_rows, length, attender_ordinal, attender_width
    )
    return jnp.einsum("rlhi,rlhj->rhij", weighted, plain_values, precision=lax.Precision.HIGHEST)


def generation_iterations(
    recurrent_memories,
    acceptance_lines,
    address_source,
    payload_source,
    fading_source,
    valve_source,
    shard_reward,
    shard_scaling_weight,
    shard_scaling_offset,
):
    attender_ordinal = recurrent_memories.shape[-3]
    attender_width = recurrent_memories.shape[-1]
    leading = acceptance_lines.shape[:-2]
    step_count = acceptance_lines.shape[-2]
    split_shape = leading + (step_count, attender_ordinal, attender_width)
    receptance = acceptance_lines.astype(jnp.float32).reshape(split_shape)
    key_split = address_source.astype(jnp.float32).reshape(split_shape)
    valued = payload_source.astype(jnp.float32).reshape(split_shape)
    factors = jnp.exp(-jnp.exp(fading_source.astype(jnp.float32))).reshape(split_shape)
    results = []
    for position in range(step_count):
        present_acceptance = receptance[..., position, :, :]
        present_address = key_split[..., position, :, :]
        present_payload = valued[..., position, :, :]
        immediate_summand = (
            jnp.sum(present_acceptance * shard_reward * present_address, axis=-1, keepdims=True)
            * present_payload
        )
        carried = jnp.einsum(
            "...hi,...hij->...hj",
            present_acceptance,
            recurrent_memories,
            precision=lax.Precision.HIGHEST,
        )
        results.append(carried + immediate_summand)
        if position + 1 < step_count:
            recurrent_memories = (
                factors[..., position, :, :][..., :, None] * recurrent_memories
                + present_address[..., :, None] * present_payload[..., None, :]
            )
    mixed_out = jnp.stack(results, axis=-3)
    average = jnp.mean(mixed_out, axis=-1, keepdims=True)
    centred = mixed_out - average
    spread = jnp.mean(centred * centred, axis=-1, keepdims=True)
    normed = (centred * lax.rsqrt(spread + norm_eps)).reshape(
        leading + (step_count, attender_ordinal * attender_width)
    )
    return (
        (normed * shard_scaling_weight + shard_scaling_offset)
        * jax.nn.silu(valve_source.astype(jnp.float32))
    ).astype(jnp.bfloat16)


def gather_body(ids_ref, table_ref, out_ref, strips, sems):
    rows, length = ids_ref.shape[1], ids_ref.shape[2]
    lanes = strips.shape[2] // length

    def strip(row, place):
        tile = lax.div(ids_ref[0, row, place], lanes)
        return pltpu.make_async_copy(
            table_ref.at[:, pl.ds(pl.multiple_of(tile * lanes, lanes), lanes)],
            strips.at[row, :, pl.ds(place * lanes, lanes)],
            sems.at[row, place],
        )

    def start(row, carry):
        for place in range(length):
            strip(row, place).start()
        return carry

    lax.fori_loop(0, rows, start, 0)
    places = lax.broadcasted_iota(jnp.int32, (length, lanes), 0)
    columns = lax.broadcasted_iota(jnp.int32, (length, lanes), 1)

    def pick(row, carry):
        wanted = jnp.zeros((length, lanes), jnp.int32)
        for place in range(length):
            wanted = jnp.where(places == place, lax.rem(ids_ref[0, row, place], lanes), wanted)
        hit = jnp.where(columns == wanted, 1.0, 0.0)
        chosen = jnp.concatenate(
            [jnp.where(places == place, hit, 0.0) for place in range(length)], axis=1
        ).astype(jnp.bfloat16)
        for place in range(length):
            strip(row, place).wait()
        found = lax.dot_general(
            chosen, strips[row], (((1,), (1,)), ((), ())), preferred_element_type=jnp.float32
        )
        out_ref[pl.ds(pl.multiple_of(row * length, length), length), :] = found.astype(jnp.bfloat16)
        return carry

    lax.fori_loop(0, rows, pick, 0)


def gather_tokens(ids, table):
    rows, length = ids.shape[1], ids.shape[2]
    columns = table.shape[0]
    return pl.pallas_call(
        gather_body,
        out_shape=jax.ShapeDtypeStruct((rows * length, columns), jnp.bfloat16),
        in_specs=[
            pl.BlockSpec(memory_space=pltpu.SMEM),
            pl.BlockSpec(memory_space=pl.ANY),
        ],
        out_specs=pl.BlockSpec(memory_space=pltpu.VMEM),
        scratch_shapes=[
            pltpu.VMEM((rows, columns, length * lane_count), jnp.bfloat16),
            pltpu.SemaphoreType.DMA((rows, length)),
        ],
        compiler_params=pltpu.CompilerParams(vmem_limit_bytes=40 * 2**20),
        name="pick_tokens",
    )(ids, table)


def segment_sums(rows, ones):
    width = ones.shape[0]
    high = rows.astype(jnp.bfloat16)
    low = (rows - high.astype(jnp.float32)).astype(jnp.bfloat16)
    parts = []
    for begin in range(0, rows.shape[1], width):
        stop = begin + width
        parts.append(
            jnp.dot(high[:, begin:stop], ones, preferred_element_type=jnp.float32)
            + jnp.dot(low[:, begin:stop], ones, preferred_element_type=jnp.float32)
        )
    return jnp.concatenate(parts, axis=1)


def mixing_body(
    wide,
    narrow,
    spans_ref,
    local_ref,
    opening_ref,
    blends_ref,
    left_hbm,
    right_hbm,
    fixed_ref,
    fading_left_hbm,
    fading_right_ref,
    address_hbm,
    payload_hbm,
    reward_ref,
    scaling_ref,
    offset_ref,
    r_ref,
    k_ref,
    v_ref,
    w_ref,
    g_ref,
    out_ref,
    held,
    left,
    right,
    fading_left,
    address,
    payload,
    hidden_sum,
    key_sum,
    value_sum,
    decay_sum,
    pairs,
    own_part,
    r_send,
    r_recv,
    y_send,
    y_recv,
    weight_sems,
    ring_send,
    ring_recv,
    r_send_sems,
    r_recv_sems,
    y_send_sems,
    y_recv_sems,
    self_sems,
):
    w_me = lax.axis_index("wide")
    n_me = lax.axis_index("narrow")
    tokens, columns = local_ref.shape
    bank_rows = spans_ref.shape[1]
    length = tokens // bank_rows
    features = opening_ref.shape[1]
    head = reward_ref.shape[1]
    banks, steps, generated = r_ref.shape
    share = wide // narrow
    half_owner = lax.div(w_me, share)
    place_in_half = lax.rem(w_me, share)

    barrier = pltpu.get_barrier_semaphore()
    for other in range(1, wide * narrow):
        flat = lax.rem(w_me * narrow + n_me + other, wide * narrow)
        pl.semaphore_signal(
            barrier,
            inc=1,
            device_id={"wide": lax.div(flat, narrow), "narrow": lax.rem(flat, narrow)},
            device_id_type=pl.DeviceIdType.MESH,
        )

    loads = [
        pltpu.make_async_copy(source, target, weight_sems.at[number])
        for number, (source, target) in enumerate(
            [
                (left_hbm, left),
                (right_hbm, right),
                (fading_left_hbm, fading_left),
                (address_hbm, address),
                (payload_hbm, payload),
            ]
        )
    ]
    for load in loads:
        load.start()

    held[w_me] = local_ref[...]

    def index_at(position):
        return jnp.where(position < wide // 2, 2 * position, 2 * (wide - 1 - position) + 1)

    position = jnp.where(
        lax.rem(w_me, 2) == 0, lax.div(w_me, 2), wide - 1 - lax.div(w_me, 2)
    )
    targets = (
        index_at(lax.rem(position + 1, wide)),
        index_at(lax.rem(position + wide - 1, wide)),
    )
    half = tokens // 2
    chunk_rows = length
    chunks = half // chunk_rows

    def owner_of(direction, step):
        back = wide - step if direction == 0 else step
        return index_at(lax.rem(position + back, wide))

    def ring_copy(direction, step, chunk):
        piece = held.at[
            owner_of(direction, step), pl.ds(direction * half + chunk * chunk_rows, chunk_rows)
        ]
        return pltpu.make_async_remote_copy(
            src_ref=piece,
            dst_ref=piece,
            send_sem=ring_send.at[direction, step, chunk],
            recv_sem=ring_recv.at[direction, step, chunk],
            device_id={"wide": targets[direction]},
            device_id_type=pl.DeviceIdType.MESH,
        )

    def ring_arrival(direction, step, chunk):
        piece = held.at[
            owner_of(direction, step + 1),
            pl.ds(direction * half + chunk * chunk_rows, chunk_rows),
        ]
        return pltpu.make_async_remote_copy(
            src_ref=piece,
            dst_ref=piece,
            send_sem=ring_send.at[direction, step, chunk],
            recv_sem=ring_recv.at[direction, step, chunk],
            device_id={"wide": targets[direction]},
            device_id_type=pl.DeviceIdType.MESH,
        )

    def with_difference(block):
        current = block.astype(jnp.float32)
        places = lax.broadcasted_iota(jnp.int32, current.shape, 0) & (length - 1)
        previous = jnp.where(places == 0, 0.0, pltpu.roll(current, 1, 0))
        return current, previous - current

    def add_hidden(direction, step):
        owner = owner_of(direction, step)
        rows = pl.ds(direction * half, half)
        feature_rows = pl.ds(pl.multiple_of(owner * columns, columns), columns)
        current, difference = with_difference(held[owner, rows])
        mixed = (current + difference * opening_ref[:, feature_rows]).astype(jnp.bfloat16)
        term = jnp.dot(mixed, left[feature_rows, :], preferred_element_type=jnp.float32)
        if step == 0:
            hidden_sum[rows, :] = term
        else:
            hidden_sum[rows, :] += term

    def r_copy(bank, part):
        return pltpu.make_async_remote_copy(
            src_ref=r_send.at[bank, part],
            dst_ref=r_recv.at[w_me],
            send_sem=r_send_sems.at[bank, part],
            recv_sem=r_recv_sems.at[w_me],
            device_id={"wide": n_me * share + part, "narrow": bank},
            device_id_type=pl.DeviceIdType.MESH,
        )

    def r_self(bank, part):
        return pltpu.make_async_copy(r_send.at[bank, part], r_recv.at[w_me], self_sems.at[0])

    def r_arrival(prompt):
        return pltpu.make_async_remote_copy(
            src_ref=r_send.at[0, 0],
            dst_ref=r_recv.at[prompt],
            send_sem=r_send_sems.at[0, 0],
            recv_sem=r_recv_sems.at[prompt],
            device_id={"wide": prompt, "narrow": half_owner},
            device_id_type=pl.DeviceIdType.MESH,
        )

    def y_copy(prompt):
        return pltpu.make_async_remote_copy(
            src_ref=y_send.at[prompt],
            dst_ref=y_recv.at[n_me, place_in_half],
            send_sem=y_send_sems.at[prompt],
            recv_sem=y_recv_sems.at[n_me, place_in_half],
            device_id={"wide": prompt, "narrow": half_owner},
            device_id_type=pl.DeviceIdType.MESH,
        )

    def y_self(prompt):
        return pltpu.make_async_copy(
            y_send.at[prompt], y_recv.at[n_me, place_in_half], self_sems.at[1]
        )

    def y_arrival(bank, part):
        return pltpu.make_async_remote_copy(
            src_ref=y_send.at[0],
            dst_ref=y_recv.at[bank, part],
            send_sem=y_send_sems.at[0],
            recv_sem=y_recv_sems.at[bank, part],
            device_id={"wide": n_me * share + part, "narrow": bank},
            device_id_type=pl.DeviceIdType.MESH,
        )

    def generated_is_mine(bank, part):
        return jnp.logical_and(n_me * share + part == w_me, n_me == bank)

    def prompt_is_mine(prompt):
        return jnp.logical_and(w_me == prompt, n_me == half_owner)

    pl.semaphore_wait(barrier, wide * narrow - 1)
    for chunk in range(chunks):
        for direction in range(2):
            ring_copy(direction, 0, chunk).start()

    ones = jnp.where(
        lax.broadcasted_iota(jnp.int32, (lane_count, lane_count), 0) & -head
        == lax.broadcasted_iota(jnp.int32, (lane_count, lane_count), 1) & -head,
        1.0,
        0.0,
    ).astype(jnp.bfloat16)
    first_head = pl.multiple_of(n_me * (generated // head), generated // head)
    rewards = reward_ref[pl.ds(first_head, generated // head), :]
    reward_line = jnp.concatenate(
        [rewards[number : number + 1, :] for number in range(generated // head)], axis=1
    )
    pair_rows = {}
    for bank in range(banks):
        r_all = r_ref[bank].astype(jnp.float32)
        k_all = k_ref[bank].astype(jnp.float32)
        w_all = jnp.exp(-jnp.exp(w_ref[bank].astype(jnp.float32)))
        for step in range(steps):
            lagged = r_all[step : step + 1]
            for earlier in range(step, -1, -1):
                line = lagged * k_all[earlier : earlier + 1]
                if earlier == step:
                    line = line * reward_line
                row = len(pair_rows)
                pair_rows[bank, step, earlier] = row
                pairs[row : row + 1, :] = line
                if earlier < step:
                    lagged = lagged * w_all[earlier : earlier + 1]
            for part in range(share):
                r_send[bank, part, step : step + 1, :] = lagged[
                    :, part * columns : (part + 1) * columns
                ]
    for bank in range(banks):
        for part in range(share):

            @pl.when(generated_is_mine(bank, part))
            def _():
                r_self(bank, part).start()

            @pl.when(jnp.logical_not(generated_is_mine(bank, part)))
            def _():
                r_copy(bank, part).start()

    loads[0].wait()
    for direction in range(2):
        add_hidden(direction, 0)
    for step in range(1, wide - 1):
        for chunk in range(chunks):
            for direction in range(2):
                ring_arrival(direction, step - 1, chunk).wait_recv()
                ring_copy(direction, step, chunk).start()
        for direction in range(2):
            add_hidden(direction, step)
        if step == 1:
            sums = segment_sums(pairs[...], ones)
            for bank in range(banks):
                v_all = v_ref[bank].astype(jnp.float32)
                for now in range(steps):
                    line = None
                    for earlier in range(now + 1):
                        row = pair_rows[bank, now, earlier]
                        term = sums[row : row + 1, :] * v_all[earlier : earlier + 1]
                        line = term if line is None else line + term
                    own_part[bank * steps + now : bank * steps + now + 1, :] = line
    for load in loads[1:]:
        load.wait()
    for chunk in range(chunks):
        for direction in range(2):
            ring_arrival(direction, wide - 2, chunk).wait_recv()
    for direction in range(2):
        add_hidden(direction, wide - 1)

    hidden = jnp.tanh(hidden_sum[...]).astype(jnp.bfloat16)
    rank = right.shape[1]
    hidden_parts = [hidden[:, branch * rank : (branch + 1) * rank] for branch in range(3)]
    transposed = (((1,), (1,)), ((), ()))
    for block in range(wide):
        span = slice(block * columns, (block + 1) * columns)
        current, difference = with_difference(held[block])
        mixed = []
        for branch in range(3):
            shift = jnp.dot(
                hidden_parts[branch], right[branch, :, span], preferred_element_type=jnp.float32
            )
            mixed.append(
                (current + difference * (blends_ref[branch : branch + 1, span] + shift)).astype(
                    jnp.bfloat16
                )
            )
        decay_term = jnp.dot(mixed[0], fading_left[span, :], preferred_element_type=jnp.float32)
        key_term = lax.dot_general(
            mixed[1], address[:, span], transposed, preferred_element_type=jnp.float32
        )
        value_term = lax.dot_general(
            mixed[2], payload[:, span], transposed, preferred_element_type=jnp.float32
        )
        if block == 0:
            decay_sum[...] = decay_term
            key_sum[...] = key_term
            value_sum[...] = value_term
        else:
            decay_sum[...] += decay_term
            key_sum[...] += key_term
            value_sum[...] += value_term

    decay_hidden = jnp.tanh(decay_sum[...]).astype(jnp.bfloat16)
    rates = jnp.exp(
        fixed_ref[...]
        + jnp.dot(decay_hidden, fading_right_ref[...], preferred_element_type=jnp.float32)
    )
    row_ids = lax.broadcasted_iota(jnp.int32, (tokens, tokens), 0)
    column_ids = lax.broadcasted_iota(jnp.int32, (tokens, tokens), 1)
    row_limit = jnp.zeros((tokens, 1), jnp.int32)
    column_limit = jnp.zeros((tokens, tokens), jnp.int32)
    row_line = lax.broadcasted_iota(jnp.int32, (tokens, 1), 0)
    for prompt in range(bank_rows):
        span_now = spans_ref[0, prompt]
        row_limit = jnp.where(row_line & -length == prompt * length, span_now, row_limit)
        column_limit = jnp.where(column_ids & -length == prompt * length, span_now, column_limit)
    later = jnp.where(
        (row_ids & -length == column_ids & -length)
        & (column_ids > row_ids)
        & (column_ids & (length - 1) < column_limit),
        1.0,
        0.0,
    ).astype(jnp.bfloat16)
    high = rates.astype(jnp.bfloat16)
    low = (rates - high.astype(jnp.float32)).astype(jnp.bfloat16)
    remaining = jnp.dot(later, high, preferred_element_type=jnp.float32) + jnp.dot(
        later, low, preferred_element_type=jnp.float32
    )
    weights = jnp.where(row_line & (length - 1) < row_limit, jnp.exp(-remaining), 0.0)
    weighted = (
        key_sum[...].astype(jnp.bfloat16).astype(jnp.float32) * weights
    ).astype(jnp.bfloat16)
    values = value_sum[...].astype(jnp.bfloat16)

    for prompt in range(bank_rows):

        @pl.when(prompt_is_mine(prompt))
        def _():
            for bank in range(banks):
                for part in range(share):

                    @pl.when(generated_is_mine(bank, part))
                    def _():
                        r_self(bank, part).wait()

        @pl.when(jnp.logical_not(prompt_is_mine(prompt)))
        def _():
            r_arrival(prompt).wait_recv()

    asked = jnp.concatenate([r_recv[prompt] for prompt in range(bank_rows)], axis=0)
    asked_rows = bank_rows * steps
    lane_heads = lax.broadcasted_iota(jnp.int32, (asked_rows, columns), 1) & -head
    heads = columns // head
    spread = jnp.concatenate(
        [jnp.where(lane_heads == number * head, asked, 0.0) for number in range(heads)], axis=0
    ).astype(jnp.bfloat16)
    scores = lax.dot_general(spread, weighted, transposed, preferred_element_type=jnp.float32)
    score_rows = lax.broadcasted_iota(jnp.int32, scores.shape, 0) & (asked_rows - 1)
    score_columns = lax.broadcasted_iota(jnp.int32, scores.shape, 1)
    kept = jnp.zeros(scores.shape, jnp.float32)
    for prompt in range(bank_rows):
        kept = jnp.where(
            (score_rows & -steps == prompt * steps)
            & (score_columns & -length == prompt * length),
            scores,
            kept,
        )
    answers = jnp.dot(kept.astype(jnp.bfloat16), values, preferred_element_type=jnp.float32)
    answer = jnp.zeros((asked_rows, columns), jnp.float32)
    for number in range(heads):
        answer = jnp.where(
            lane_heads == number * head,
            answers[number * asked_rows : (number + 1) * asked_rows],
            answer,
        )
    for prompt in range(bank_rows):
        y_send[prompt] = answer[prompt * steps : (prompt + 1) * steps]
    for prompt in range(bank_rows):

        @pl.when(prompt_is_mine(prompt))
        def _():
            y_self(prompt).start()

        @pl.when(jnp.logical_not(prompt_is_mine(prompt)))
        def _():
            y_copy(prompt).start()

    gate_lines = []
    for bank in range(banks):
        gate = g_ref[bank].astype(jnp.float32)
        gate_lines.append(gate / (1.0 + jnp.exp(-gate)))
    half_columns = pl.ds(pl.multiple_of(n_me * generated, generated), generated)
    gain = scaling_ref[:, half_columns]
    bias = offset_ref[:, half_columns]

    for step in range(wide - 1):
        for chunk in range(chunks):
            for direction in range(2):
                ring_copy(direction, step, chunk).wait_send()
    for bank in range(banks):
        for part in range(share):

            @pl.when(jnp.logical_not(generated_is_mine(bank, part)))
            def _():
                r_copy(bank, part).wait_send()

    for bank in range(banks):
        for part in range(share):

            @pl.when(generated_is_mine(bank, part))
            def _():
                for prompt in range(bank_rows):

                    @pl.when(prompt_is_mine(prompt))
                    def _():
                        y_self(prompt).wait()

            @pl.when(jnp.logical_not(generated_is_mine(bank, part)))
            def _():
                y_arrival(bank, part).wait_recv()

    received = jnp.concatenate(
        [
            jnp.concatenate([y_recv[bank, part] for part in range(share)], axis=1)
            for bank in range(banks)
        ],
        axis=0,
    )
    y = received + own_part[...]
    centred = y - segment_sums(y, ones) * (1.0 / head)
    variance = segment_sums(centred * centred, ones) * (1.0 / head)
    normed = centred * lax.rsqrt(variance + norm_eps) * gain + bias
    for bank in range(banks):
        out_ref[bank] = (normed[bank * steps : (bank + 1) * steps] * gate_lines[bank]).astype(
            out_ref.dtype
        )
    for prompt in range(bank_rows):

        @pl.when(jnp.logical_not(prompt_is_mine(prompt)))
        def _():
            y_copy(prompt).wait_send()


def mixing(wide, narrow, *operands):
    spans, local = operands[0], operands[1]
    tokens, columns = local.shape
    bank_rows = spans.shape[1]
    features = operands[2].shape[1]
    left, right, fading_left = operands[4], operands[5], operands[7]
    address, payload = operands[9], operands[10]
    banks, steps, generated = operands[14].shape
    share = wide // narrow
    chunks = bank_rows // 2
    pair_count = banks * steps * (steps + 1) // 2
    vmem = pl.BlockSpec(memory_space=pltpu.VMEM)
    far = pl.BlockSpec(memory_space=pl.ANY)
    specs = [vmem] * len(operands)
    specs[0] = pl.BlockSpec(memory_space=pltpu.SMEM)
    for number in (4, 5, 7, 9, 10):
        specs[number] = far
    f32 = jnp.float32
    dma = pltpu.SemaphoreType.DMA
    return pl.pallas_call(
        functools.partial(mixing_body, wide, narrow),
        out_shape=jax.ShapeDtypeStruct((banks, steps, generated), jnp.bfloat16),
        in_specs=specs,
        out_specs=vmem,
        scratch_shapes=[
            pltpu.VMEM((wide, tokens, columns), jnp.bfloat16),
            pltpu.VMEM(left.shape, left.dtype),
            pltpu.VMEM(right.shape, right.dtype),
            pltpu.VMEM(fading_left.shape, fading_left.dtype),
            pltpu.VMEM(address.shape, address.dtype),
            pltpu.VMEM(payload.shape, payload.dtype),
            pltpu.VMEM((tokens, left.shape[1]), f32),
            pltpu.VMEM((tokens, columns), f32),
            pltpu.VMEM((tokens, columns), f32),
            pltpu.VMEM((tokens, fading_left.shape[1]), f32),
            pltpu.VMEM((pair_count, generated), f32),
            pltpu.VMEM((banks * steps, generated), f32),
            pltpu.VMEM((banks, share, steps, columns), f32),
            pltpu.VMEM((bank_rows, steps, columns), f32),
            pltpu.VMEM((bank_rows, steps, columns), f32),
            pltpu.VMEM((banks, share, steps, columns), f32),
            dma((5,)),
            dma((2, wide - 1, chunks)),
            dma((2, wide - 1, chunks)),
            dma((banks, share)),
            dma((bank_rows,)),
            dma((bank_rows,)),
            dma((banks, share)),
            dma((2,)),
        ],
        compiler_params=pltpu.CompilerParams(
            collective_id=0, has_side_effects=True, vmem_limit_bytes=40 * 2**20
        ),
        name="mix_and_generate",
    )(*operands)


def power_of_two(number):
    return number > 0 and number & (number - 1) == 0


def fits_kernels(wide, narrow, ids, table, reward, acceptance):
    bank_rows, length = ids.shape[1], ids.shape[2]
    columns = table.shape[0]
    banks, prompts, steps, generated = acceptance.shape
    return (
        prompts == 1
        and wide % 2 == 0
        and wide > 2
        and wide % narrow == 0
        and banks == narrow
        and bank_rows == wide
        and length % 16 == 0
        and columns % lane_count == 0
        and table.shape[1] % lane_count == 0
        and generated == columns * (wide // narrow)
        and lane_count % reward.shape[1] == 0
        and all(power_of_two(size) for size in (length, steps, bank_rows, reward.shape[1]))
        and columns * length * bank_rows * lane_count * 2 <= 2**25
    )


def per_device(
    context_symbol_ids,
    context_symbol_spans,
    symbol_vector_lookup,
    opening_lagged_blend,
    lagged_blend_weights,
    blending_left_operand,
    blending_right_operands,
    fixed_fading_scores,
    fading_left_operand,
    fading_right_operand,
    address_projector,
    payload_projector,
    present_symbol_reward,
    cluster_scaling_weight,
    cluster_scaling_offset,
    generated_acceptance,
    generated_addresses,
    generated_payloads,
    generated_fading_scores,
    generated_valve_scores,
):
    wide, narrow = lax.axis_size("wide"), lax.axis_size("narrow")
    if fits_kernels(
        wide,
        narrow,
        context_symbol_ids,
        symbol_vector_lookup,
        present_symbol_reward,
        generated_acceptance,
    ):
        result = mixing(
            wide,
            narrow,
            context_symbol_spans,
            gather_tokens(context_symbol_ids, symbol_vector_lookup),
            opening_lagged_blend[None],
            lagged_blend_weights,
            blending_left_operand,
            blending_right_operands,
            fixed_fading_scores[None],
            fading_left_operand,
            fading_right_operand,
            address_projector,
            payload_projector,
            present_symbol_reward,
            cluster_scaling_weight[None],
            cluster_scaling_offset[None],
            generated_acceptance[:, 0],
            generated_addresses[:, 0],
            generated_payloads[:, 0],
            generated_fading_scores[:, 0],
            generated_valve_scores[:, 0],
        )
        return result[:, None]
    bank_rows = context_symbol_ids.shape[1]
    length = context_symbol_ids.shape[2]
    columns = symbol_vector_lookup.shape[0]
    attender_width = present_symbol_reward.shape[1]
    head_local = columns // attender_width
    lengths = context_symbol_spans.reshape(-1)
    picked = jnp.take(symbol_vector_lookup, context_symbol_ids.reshape(-1), axis=1)
    gathered = lax.all_gather(picked, "wide", axis=0, tiled=True).T
    features = gathered.shape[1]
    block_rows = bank_rows
    while block_rows % 2 == 0 and block_rows * length > 1024:
        block_rows = block_rows // 2
    blocks = gathered.reshape(bank_rows // block_rows, block_rows, length, features)
    length_blocks = lengths.reshape(bank_rows // block_rows, block_rows)

    def one_block(block_item):
        key_proj, value_proj, decay_log = mix_project(
            block_item[0],
            opening_lagged_blend,
            lagged_blend_weights,
            blending_left_operand,
            blending_right_operands,
            fixed_fading_scores,
            fading_left_operand,
            fading_right_operand,
            address_projector,
            payload_projector,
        )
        block_shape = (block_rows, length, columns)
        return final_states(
            key_proj.reshape(block_shape),
            value_proj.reshape(block_shape),
            decay_log.reshape(block_shape),
            block_item[1],
            attender_width,
        )

    recurrent_memories = lax.map(one_block, (blocks, length_blocks)).reshape(
        bank_rows, head_local, attender_width, attender_width
    )
    handed = lax.all_to_all(
        lax.all_to_all(
            recurrent_memories.reshape(1, bank_rows, head_local, attender_width * attender_width),
            "wide",
            split_axis=1,
            concat_axis=2,
            tiled=True,
        ),
        "narrow",
        split_axis=2,
        concat_axis=0,
        tiled=True,
    )
    generated_by_attender = handed.shape[2]
    leading_attender_offset = lax.axis_index("narrow") * generated_by_attender
    shard_reward = lax.dynamic_slice_in_dim(
        present_symbol_reward, leading_attender_offset, generated_by_attender, 0
    )
    shard_scaling_weight = lax.dynamic_slice_in_dim(
        cluster_scaling_weight,
        leading_attender_offset * attender_width,
        generated_by_attender * attender_width,
        0,
    )
    shard_scaling_offset = lax.dynamic_slice_in_dim(
        cluster_scaling_offset,
        leading_attender_offset * attender_width,
        generated_by_attender * attender_width,
        0,
    )
    result = generation_iterations(
        handed.reshape(handed.shape[:3] + (attender_width, attender_width)),
        generated_acceptance,
        generated_addresses,
        generated_payloads,
        generated_fading_scores,
        generated_valve_scores,
        shard_reward,
        shard_scaling_weight,
        shard_scaling_offset,
    )
    return result


def solution(mesh):
    placed = (
        P("narrow", "groups", None),
        P("narrow", "groups"),
        P("wide", None),
        P(),
        P(),
        P(),
        P(),
        P("wide"),
        P(),
        P(None, "wide"),
        P("wide", None),
        P("wide", None),
        P(),
        P(),
        P(),
        P(None, ("groups", "wide"), None, "narrow"),
        P(None, ("groups", "wide"), None, "narrow"),
        P(None, ("groups", "wide"), None, "narrow"),
        P(None, ("groups", "wide"), None, "narrow"),
        P(None, ("groups", "wide"), None, "narrow"),
    )
    return jax.shard_map(
        per_device,
        mesh=mesh,
        in_specs=placed,
        out_specs=P(None, ("groups", "wide"), None, "narrow"),
        check_vma=False,
    )
```

```python
import functools

import jax
import jax.numpy as jnp
from jax import lax
from jax.experimental import pallas as pl
from jax.experimental.pallas import tpu as pltpu
from jax.sharding import PartitionSpec as P

norm_eps = 0.00064
lane_count = 128


def mix_project(
    embedded,
    opening_lagged_blend,
    lagged_blend_weights,
    blending_left_operand,
    blending_right_operands,
    fixed_fading_scores,
    fading_left_operand,
    fading_right_operand,
    address_projector,
    payload_projector,
):
    features = embedded.shape[2]
    previous = jnp.pad(embedded, ((0, 0), (1, 0), (0, 0)))[:, :-1, :]
    current = embedded.reshape(-1, features).astype(jnp.float32)
    difference = previous.reshape(-1, features).astype(jnp.float32) - current
    mixed_in = (current + difference * opening_lagged_blend).astype(jnp.bfloat16)
    hidden = jnp.tanh(
        jnp.dot(mixed_in, blending_left_operand, preferred_element_type=jnp.float32)
    ).astype(jnp.bfloat16)
    rank_size = blending_right_operands.shape[1]
    branches = []
    for branch in range(3):
        shift_term = jnp.dot(
            hidden[:, branch * rank_size : (branch + 1) * rank_size],
            blending_right_operands[branch],
            preferred_element_type=jnp.float32,
        )
        branches.append(
            (current + difference * (lagged_blend_weights[branch] + shift_term)).astype(
                jnp.bfloat16
            )
        )
    decay_hidden = jnp.tanh(
        jnp.dot(branches[0], fading_left_operand, preferred_element_type=jnp.float32)
    ).astype(jnp.bfloat16)
    decay_log = fixed_fading_scores + jnp.dot(
        decay_hidden, fading_right_operand, preferred_element_type=jnp.float32
    )
    key_proj = jnp.dot(branches[1], address_projector.T, preferred_element_type=jnp.float32).astype(
        jnp.bfloat16
    )
    value_proj = jnp.dot(
        branches[2], payload_projector.T, preferred_element_type=jnp.float32
    ).astype(jnp.bfloat16)
    return (key_proj, value_proj, decay_log)


def final_states(key_proj, value_proj, decay_log, lengths, attender_width):
    bank_rows, length, columns = key_proj.shape
    attender_ordinal = columns // attender_width
    decay_rates = jnp.exp(decay_log)
    places = lax.broadcasted_iota(jnp.int32, (bank_rows, length), 1)
    live_mask = (places < lengths[:, None])[:, :, None]
    running = jnp.cumsum(jnp.where(live_mask, decay_rates, 0.0), axis=1)
    remaining = running[:, -1:, :] - running
    weights = jnp.where(live_mask, jnp.exp(-remaining), 0.0)
    weighted = (key_proj.astype(jnp.float32) * weights).reshape(
        bank_rows, length, attender_ordinal, attender_width
    )
    plain_values = value_proj.astype(jnp.float32).reshape(
        bank_rows, length, attender_ordinal, attender_width
    )
    return jnp.einsum("rlhi,rlhj->rhij", weighted, plain_values, precision=lax.Precision.HIGHEST)


def generation_iterations(
    recurrent_memories,
    acceptance_lines,
    address_source,
    payload_source,
    fading_source,
    valve_source,
    shard_reward,
    shard_scaling_weight,
    shard_scaling_offset,
):
    attender_ordinal = recurrent_memories.shape[-3]
    attender_width = recurrent_memories.shape[-1]
    leading = acceptance_lines.shape[:-2]
    step_count = acceptance_lines.shape[-2]
    split_shape = leading + (step_count, attender_ordinal, attender_width)
    receptance = acceptance_lines.astype(jnp.float32).reshape(split_shape)
    key_split = address_source.astype(jnp.float32).reshape(split_shape)
    valued = payload_source.astype(jnp.float32).reshape(split_shape)
    factors = jnp.exp(-jnp.exp(fading_source.astype(jnp.float32))).reshape(split_shape)
    results = []
    for position in range(step_count):
        present_acceptance = receptance[..., position, :, :]
        present_address = key_split[..., position, :, :]
        present_payload = valued[..., position, :, :]
        immediate_summand = (
            jnp.sum(present_acceptance * shard_reward * present_address, axis=-1, keepdims=True)
            * present_payload
        )
        carried = jnp.einsum(
            "...hi,...hij->...hj",
            present_acceptance,
            recurrent_memories,
            precision=lax.Precision.HIGHEST,
        )
        results.append(carried + immediate_summand)
        if position + 1 < step_count:
            recurrent_memories = (
                factors[..., position, :, :][..., :, None] * recurrent_memories
                + present_address[..., :, None] * present_payload[..., None, :]
            )
    mixed_out = jnp.stack(results, axis=-3)
    average = jnp.mean(mixed_out, axis=-1, keepdims=True)
    centred = mixed_out - average
    spread = jnp.mean(centred * centred, axis=-1, keepdims=True)
    normed = (centred * lax.rsqrt(spread + norm_eps)).reshape(
        leading + (step_count, attender_ordinal * attender_width)
    )
    return (
        (normed * shard_scaling_weight + shard_scaling_offset)
        * jax.nn.silu(valve_source.astype(jnp.float32))
    ).astype(jnp.bfloat16)


def gather_body(ids_ref, table_ref, out_ref, strips, sems):
    rows, length = ids_ref.shape[1], ids_ref.shape[2]
    lanes = strips.shape[2] // length

    def strip(row, place):
        tile = lax.div(ids_ref[0, row, place], lanes)
        return pltpu.make_async_copy(
            table_ref.at[:, pl.ds(pl.multiple_of(tile * lanes, lanes), lanes)],
            strips.at[row, :, pl.ds(place * lanes, lanes)],
            sems.at[row, place],
        )

    def start(row, carry):
        for place in range(length):
            strip(row, place).start()
        return carry

    lax.fori_loop(0, rows, start, 0)
    places = lax.broadcasted_iota(jnp.int32, (length, lanes), 0)
    columns = lax.broadcasted_iota(jnp.int32, (length, lanes), 1)

    def pick(row, carry):
        wanted = jnp.zeros((length, lanes), jnp.int32)
        for place in range(length):
            wanted = jnp.where(places == place, lax.rem(ids_ref[0, row, place], lanes), wanted)
        hit = jnp.where(columns == wanted, 1.0, 0.0)
        chosen = jnp.concatenate(
            [jnp.where(places == place, hit, 0.0) for place in range(length)], axis=1
        ).astype(jnp.bfloat16)
        for place in range(length):
            strip(row, place).wait()
        found = lax.dot_general(
            chosen, strips[row], (((1,), (1,)), ((), ())), preferred_element_type=jnp.float32
        )
        out_ref[pl.ds(pl.multiple_of(row * length, length), length), :] = found.astype(jnp.bfloat16)
        return carry

    lax.fori_loop(0, rows, pick, 0)


def gather_tokens(ids, table):
    rows, length = ids.shape[1], ids.shape[2]
    columns = table.shape[0]
    return pl.pallas_call(
        gather_body,
        out_shape=jax.ShapeDtypeStruct((rows * length, columns), jnp.bfloat16),
        in_specs=[
            pl.BlockSpec(memory_space=pltpu.SMEM),
            pl.BlockSpec(memory_space=pl.ANY),
        ],
        out_specs=pl.BlockSpec(memory_space=pltpu.VMEM),
        scratch_shapes=[
            pltpu.VMEM((rows, columns, length * lane_count), jnp.bfloat16),
            pltpu.SemaphoreType.DMA((rows, length)),
        ],
        compiler_params=pltpu.CompilerParams(vmem_limit_bytes=40 * 2**20),
        name="pick_tokens",
    )(ids, table)


def segment_sums(rows, ones):
    width = ones.shape[0]
    high = rows.astype(jnp.bfloat16)
    low = (rows - high.astype(jnp.float32)).astype(jnp.bfloat16)
    parts = []
    for begin in range(0, rows.shape[1], width):
        stop = begin + width
        parts.append(
            jnp.dot(high[:, begin:stop], ones, preferred_element_type=jnp.float32)
            + jnp.dot(low[:, begin:stop], ones, preferred_element_type=jnp.float32)
        )
    return jnp.concatenate(parts, axis=1)


def mixing_body(wide, narrow, local_ref, *refs):
    sources, out_ref, loaded = refs[:18], refs[18], refs[19:37]
    (
        left,
        r_ref,
        w_ref,
        opening_ref,
        right,
        blends_ref,
        fading_left,
        address,
        payload,
        fixed_ref,
        fading_right_ref,
        spans_ref,
        k_ref,
        v_ref,
        g_ref,
        reward_ref,
        scaling_ref,
        offset_ref,
    ) = loaded
    (
        held,
        hidden_sum,
        key_sum,
        value_sum,
        decay_sum,
        pairs,
        own_part,
        r_send,
        r_recv,
        y_send,
        y_recv,
        load_sems,
        ring_send,
        ring_recv,
        r_send_sems,
        r_recv_sems,
        y_send_sems,
        y_recv_sems,
        self_sems,
    ) = refs[37:]
    w_me = lax.axis_index("wide")
    n_me = lax.axis_index("narrow")
    tokens, columns = local_ref.shape
    bank_rows = spans_ref.shape[1]
    length = tokens // bank_rows
    features = opening_ref.shape[1]
    head = reward_ref.shape[1]
    banks, _, steps, generated = r_ref.shape
    share = wide // narrow
    half_owner = lax.div(w_me, share)
    place_in_half = lax.rem(w_me, share)

    barrier = pltpu.get_barrier_semaphore()
    for other in range(1, wide * narrow):
        flat = lax.rem(w_me * narrow + n_me + other, wide * narrow)
        pl.semaphore_signal(
            barrier,
            inc=1,
            device_id={"wide": lax.div(flat, narrow), "narrow": lax.rem(flat, narrow)},
            device_id_type=pl.DeviceIdType.MESH,
        )

    loads = [
        pltpu.make_async_copy(source, target, load_sems.at[number])
        for number, (source, target) in enumerate(zip(sources, loaded))
    ]
    for load in loads:
        load.start()

    held[w_me] = local_ref[...]

    def index_at(position):
        return jnp.where(position < wide // 2, 2 * position, 2 * (wide - 1 - position) + 1)

    position = jnp.where(
        lax.rem(w_me, 2) == 0, lax.div(w_me, 2), wide - 1 - lax.div(w_me, 2)
    )
    targets = (
        index_at(lax.rem(position + 1, wide)),
        index_at(lax.rem(position + wide - 1, wide)),
    )
    half = tokens // 2
    chunk_rows = length
    chunks = half // chunk_rows

    def owner_of(direction, step):
        back = wide - step if direction == 0 else step
        return index_at(lax.rem(position + back, wide))

    def ring_copy(direction, step, chunk):
        piece = held.at[
            owner_of(direction, step), pl.ds(direction * half + chunk * chunk_rows, chunk_rows)
        ]
        return pltpu.make_async_remote_copy(
            src_ref=piece,
            dst_ref=piece,
            send_sem=ring_send.at[direction, step, chunk],
            recv_sem=ring_recv.at[direction, step, chunk],
            device_id={"wide": targets[direction]},
            device_id_type=pl.DeviceIdType.MESH,
        )

    def ring_arrival(direction, step, chunk):
        piece = held.at[
            owner_of(direction, step + 1),
            pl.ds(direction * half + chunk * chunk_rows, chunk_rows),
        ]
        return pltpu.make_async_remote_copy(
            src_ref=piece,
            dst_ref=piece,
            send_sem=ring_send.at[direction, step, chunk],
            recv_sem=ring_recv.at[direction, step, chunk],
            device_id={"wide": targets[direction]},
            device_id_type=pl.DeviceIdType.MESH,
        )

    transposed = (((1,), (1,)), ((), ()))

    def with_difference(block):
        current = block.astype(jnp.float32)
        places = lax.broadcasted_iota(jnp.int32, current.shape, 0) & (length - 1)
        previous = jnp.where(places == 0, 0.0, pltpu.roll(current, 1, 0))
        return current, previous - current

    def add_hidden(direction, step):
        owner = owner_of(direction, step)
        rows = pl.ds(direction * half, half)
        feature_rows = pl.ds(pl.multiple_of(owner * columns, columns), columns)
        current, difference = with_difference(held[owner, rows])
        mixed = (current + difference * opening_ref[:, feature_rows]).astype(jnp.bfloat16)
        hidden_sum[rows, :] += lax.dot_general(
            mixed, left[:, feature_rows], transposed, preferred_element_type=jnp.float32
        )

    def r_copy(bank, part):
        return pltpu.make_async_remote_copy(
            src_ref=r_send.at[bank, part],
            dst_ref=r_recv.at[w_me],
            send_sem=r_send_sems.at[bank, part],
            recv_sem=r_recv_sems.at[w_me],
            device_id={"wide": n_me * share + part, "narrow": bank},
            device_id_type=pl.DeviceIdType.MESH,
        )

    def r_self(bank, part):
        return pltpu.make_async_copy(r_send.at[bank, part], r_recv.at[w_me], self_sems.at[0])

    def r_arrival(prompt):
        return pltpu.make_async_remote_copy(
            src_ref=r_send.at[0, 0],
            dst_ref=r_recv.at[prompt],
            send_sem=r_send_sems.at[0, 0],
            recv_sem=r_recv_sems.at[prompt],
            device_id={"wide": prompt, "narrow": half_owner},
            device_id_type=pl.DeviceIdType.MESH,
        )

    def y_copy(prompt):
        return pltpu.make_async_remote_copy(
            src_ref=y_send.at[prompt],
            dst_ref=y_recv.at[n_me, place_in_half],
            send_sem=y_send_sems.at[prompt],
            recv_sem=y_recv_sems.at[n_me, place_in_half],
            device_id={"wide": prompt, "narrow": half_owner},
            device_id_type=pl.DeviceIdType.MESH,
        )

    def y_self(prompt):
        return pltpu.make_async_copy(
            y_send.at[prompt], y_recv.at[n_me, place_in_half], self_sems.at[1]
        )

    def y_arrival(bank, part):
        return pltpu.make_async_remote_copy(
            src_ref=y_send.at[0],
            dst_ref=y_recv.at[bank, part],
            send_sem=y_send_sems.at[0],
            recv_sem=y_recv_sems.at[bank, part],
            device_id={"wide": n_me * share + part, "narrow": bank},
            device_id_type=pl.DeviceIdType.MESH,
        )

    def generated_is_mine(bank, part):
        return jnp.logical_and(n_me * share + part == w_me, n_me == bank)

    def prompt_is_mine(prompt):
        return jnp.logical_and(w_me == prompt, n_me == half_owner)

    pl.semaphore_wait(barrier, wide * narrow - 1)
    for chunk in range(chunks):
        for direction in range(2):
            ring_copy(direction, 0, chunk).start()

    hidden_sum[...] = jnp.zeros_like(hidden_sum)
    for load in loads[:4]:
        load.wait()
    for bank in range(banks):
        r_all = r_ref[bank, 0].astype(jnp.float32)
        w_all = jnp.exp(-jnp.exp(w_ref[bank, 0].astype(jnp.float32)))
        faded = None
        for step in range(steps):
            line = r_all[step : step + 1]
            if step > 0:
                now = w_all[step - 1 : step]
                faded = now if faded is None else faded * now
                line = line * faded
            for part in range(share):
                r_send[bank, part, step : step + 1, :] = line[
                    :, part * columns : (part + 1) * columns
                ]
    for bank in range(banks):
        for part in range(share):

            @pl.when(generated_is_mine(bank, part))
            def _():
                r_self(bank, part).start()

            @pl.when(jnp.logical_not(generated_is_mine(bank, part)))
            def _():
                r_copy(bank, part).start()

    for direction in range(2):
        add_hidden(direction, 0)

    def ring_step(step, carry):
        for chunk in range(chunks):
            for direction in range(2):
                ring_arrival(direction, step - 1, chunk).wait_recv()
                ring_copy(direction, step, chunk).start()
        for direction in range(2):
            add_hidden(direction, step)
        return carry

    lax.fori_loop(1, wide - 1, ring_step, 0)
    for load in loads[4:]:
        load.wait()
    decay_sum[...] = jnp.zeros_like(decay_sum)
    key_sum[...] = jnp.zeros_like(key_sum)
    value_sum[...] = jnp.zeros_like(value_sum)
    for chunk in range(chunks):
        for direction in range(2):
            ring_arrival(direction, wide - 2, chunk).wait_recv()
    for direction in range(2):
        add_hidden(direction, wide - 1)

    hidden = jnp.tanh(hidden_sum[...])
    rank = right.shape[0] // 3
    hidden_lanes = lax.broadcasted_iota(jnp.int32, hidden.shape, 1)
    hidden_parts = jnp.concatenate(
        [
            jnp.where(
                (hidden_lanes >= branch * rank) & (hidden_lanes < (branch + 1) * rank), hidden, 0.0
            )
            for branch in range(3)
        ],
        axis=0,
    ).astype(jnp.bfloat16)

    def project(block, carry):
        span = pl.ds(pl.multiple_of(block * columns, columns), columns)
        current, difference = with_difference(held[block])
        shifts = jnp.dot(hidden_parts, right[:, span], preferred_element_type=jnp.float32)
        mixed = [
            (
                current
                + difference
                * (
                    blends_ref[branch : branch + 1, span]
                    + shifts[branch * tokens : (branch + 1) * tokens]
                )
            ).astype(jnp.bfloat16)
            for branch in range(3)
        ]
        decay_sum[...] += jnp.dot(
            mixed[0], fading_left[span, :], preferred_element_type=jnp.float32
        )
        key_sum[...] += lax.dot_general(
            mixed[1], address[:, span], transposed, preferred_element_type=jnp.float32
        )
        value_sum[...] += lax.dot_general(
            mixed[2], payload[:, span], transposed, preferred_element_type=jnp.float32
        )
        return carry

    lax.fori_loop(0, wide, project, 0, unroll=2)

    decay_hidden = jnp.tanh(decay_sum[...]).astype(jnp.bfloat16)
    rates = jnp.exp(
        fixed_ref[...]
        + jnp.dot(decay_hidden, fading_right_ref[...], preferred_element_type=jnp.float32)
    )
    row_ids = lax.broadcasted_iota(jnp.int32, (tokens, tokens), 0)
    column_ids = lax.broadcasted_iota(jnp.int32, (tokens, tokens), 1)
    row_limit = jnp.zeros((tokens, 1), jnp.int32)
    column_limit = jnp.zeros((tokens, tokens), jnp.int32)
    row_line = lax.broadcasted_iota(jnp.int32, (tokens, 1), 0)
    for prompt in range(bank_rows):
        span_now = spans_ref[0, prompt]
        row_limit = jnp.where(row_line & -length == prompt * length, span_now, row_limit)
        column_limit = jnp.where(column_ids & -length == prompt * length, span_now, column_limit)
    later = jnp.where(
        (row_ids & -length == column_ids & -length)
        & (column_ids > row_ids)
        & (column_ids & (length - 1) < column_limit),
        1.0,
        0.0,
    ).astype(jnp.bfloat16)
    high = rates.astype(jnp.bfloat16)
    low = (rates - high.astype(jnp.float32)).astype(jnp.bfloat16)
    remaining = jnp.dot(later, high, preferred_element_type=jnp.float32) + jnp.dot(
        later, low, preferred_element_type=jnp.float32
    )
    weights = jnp.where(row_line & (length - 1) < row_limit, jnp.exp(-remaining), 0.0)
    weighted = (
        key_sum[...].astype(jnp.bfloat16).astype(jnp.float32) * weights
    ).astype(jnp.bfloat16)
    values = value_sum[...].astype(jnp.bfloat16)

    for prompt in range(bank_rows):

        @pl.when(prompt_is_mine(prompt))
        def _():
            for bank in range(banks):
                for part in range(share):

                    @pl.when(generated_is_mine(bank, part))
                    def _():
                        r_self(bank, part).wait()

        @pl.when(jnp.logical_not(prompt_is_mine(prompt)))
        def _():
            r_arrival(prompt).wait_recv()

    asked = jnp.concatenate([r_recv[prompt] for prompt in range(bank_rows)], axis=0)
    asked_rows = bank_rows * steps
    lane_heads = lax.broadcasted_iota(jnp.int32, (asked_rows, columns), 1) & -head
    heads = columns // head
    spread = jnp.concatenate(
        [jnp.where(lane_heads == number * head, asked, 0.0) for number in range(heads)], axis=0
    ).astype(jnp.bfloat16)
    scores = lax.dot_general(spread, weighted, transposed, preferred_element_type=jnp.float32)
    score_rows = lax.broadcasted_iota(jnp.int32, scores.shape, 0) & (asked_rows - 1)
    score_columns = lax.broadcasted_iota(jnp.int32, scores.shape, 1)
    kept = jnp.where(
        lax.shift_right_logical(score_rows, steps.bit_length() - 1)
        == lax.shift_right_logical(score_columns, length.bit_length() - 1),
        scores,
        0.0,
    )
    answers = jnp.dot(kept.astype(jnp.bfloat16), values, preferred_element_type=jnp.float32)
    answer = jnp.zeros((asked_rows, columns), jnp.float32)
    for number in range(heads):
        answer = jnp.where(
            lane_heads == number * head,
            answers[number * asked_rows : (number + 1) * asked_rows],
            answer,
        )
    for prompt in range(bank_rows):
        y_send[prompt] = answer[prompt * steps : (prompt + 1) * steps]
    for prompt in range(bank_rows):

        @pl.when(prompt_is_mine(prompt))
        def _():
            y_self(prompt).start()

        @pl.when(jnp.logical_not(prompt_is_mine(prompt)))
        def _():
            y_copy(prompt).start()

    ones = jnp.where(
        lax.broadcasted_iota(jnp.int32, (lane_count, lane_count), 0) & -head
        == lax.broadcasted_iota(jnp.int32, (lane_count, lane_count), 1) & -head,
        1.0,
        0.0,
    ).astype(jnp.bfloat16)
    first_head = pl.multiple_of(n_me * (generated // head), generated // head)
    rewards = reward_ref[pl.ds(first_head, generated // head), :]
    reward_line = jnp.concatenate(
        [rewards[number : number + 1, :] for number in range(generated // head)], axis=1
    )
    pair_rows = {}
    for bank in range(banks):
        r_all = r_ref[bank, 0].astype(jnp.float32)
        k_all = k_ref[bank, 0].astype(jnp.float32)
        w_all = jnp.exp(-jnp.exp(w_ref[bank, 0].astype(jnp.float32)))
        for step in range(steps):
            lagged = r_all[step : step + 1]
            for earlier in range(step, -1, -1):
                line = lagged * k_all[earlier : earlier + 1]
                if earlier == step:
                    line = line * reward_line
                elif earlier > 0:
                    lagged = lagged * w_all[earlier : earlier + 1]
                row = len(pair_rows)
                pair_rows[bank, step, earlier] = row
                pairs[row : row + 1, :] = line
    sums = segment_sums(pairs[...], ones)
    for bank in range(banks):
        v_all = v_ref[bank, 0].astype(jnp.float32)
        for now in range(steps):
            line = None
            for earlier in range(now + 1):
                row = pair_rows[bank, now, earlier]
                term = sums[row : row + 1, :] * v_all[earlier : earlier + 1]
                line = term if line is None else line + term
            own_part[bank * steps + now : bank * steps + now + 1, :] = line
    gate_lines = []
    for bank in range(banks):
        gate = g_ref[bank, 0].astype(jnp.float32)
        gate_lines.append(gate / (1.0 + jnp.exp(-gate)))
    half_columns = pl.ds(pl.multiple_of(n_me * generated, generated), generated)
    gain = scaling_ref[:, half_columns]
    bias = offset_ref[:, half_columns]

    def ring_sent(step, carry):
        for chunk in range(chunks):
            for direction in range(2):
                ring_copy(direction, step, chunk).wait_send()
        return carry

    lax.fori_loop(0, wide - 1, ring_sent, 0)
    for bank in range(banks):
        for part in range(share):

            @pl.when(jnp.logical_not(generated_is_mine(bank, part)))
            def _():
                r_copy(bank, part).wait_send()

    for bank in range(banks):
        for part in range(share):

            @pl.when(generated_is_mine(bank, part))
            def _():
                for prompt in range(bank_rows):

                    @pl.when(prompt_is_mine(prompt))
                    def _():
                        y_self(prompt).wait()

            @pl.when(jnp.logical_not(generated_is_mine(bank, part)))
            def _():
                y_arrival(bank, part).wait_recv()

    received = jnp.concatenate(
        [
            jnp.concatenate([y_recv[bank, part] for part in range(share)], axis=1)
            for bank in range(banks)
        ],
        axis=0,
    )
    y = received + own_part[...]
    centred = y - segment_sums(y, ones) * (1.0 / head)
    variance = segment_sums(centred * centred, ones) * (1.0 / head)
    normed = centred * lax.rsqrt(variance + norm_eps) * gain + bias
    for bank in range(banks):
        out_ref[bank, 0] = (normed[bank * steps : (bank + 1) * steps] * gate_lines[bank]).astype(
            out_ref.dtype
        )
    for prompt in range(bank_rows):

        @pl.when(jnp.logical_not(prompt_is_mine(prompt)))
        def _():
            y_copy(prompt).wait_send()


def mixing(wide, narrow, local, *operands):
    tokens, columns = local.shape
    left, receptance, fading_left, spans = operands[0], operands[1], operands[6], operands[11]
    bank_rows = spans.shape[1]
    banks, _, steps, generated = receptance.shape
    share = wide // narrow
    chunks = bank_rows // 2
    pair_count = banks * steps * (steps + 1) // 2
    vmem = pl.BlockSpec(memory_space=pltpu.VMEM)
    far = pl.BlockSpec(memory_space=pl.ANY)
    f32 = jnp.float32
    dma = pltpu.SemaphoreType.DMA
    return pl.pallas_call(
        functools.partial(mixing_body, wide, narrow),
        out_shape=jax.ShapeDtypeStruct(receptance.shape, jnp.bfloat16),
        in_specs=[vmem] + [far] * len(operands),
        out_specs=vmem,
        scratch_shapes=[
            pltpu.SMEM(operand.shape, operand.dtype)
            if operand is spans
            else pltpu.VMEM(operand.shape, operand.dtype)
            for operand in operands
        ]
        + [
            pltpu.VMEM((wide, tokens, columns), jnp.bfloat16),
            pltpu.VMEM((tokens, left.shape[0]), f32),
            pltpu.VMEM((tokens, columns), f32),
            pltpu.VMEM((tokens, columns), f32),
            pltpu.VMEM((tokens, fading_left.shape[1]), f32),
            pltpu.VMEM((pair_count, generated), f32),
            pltpu.VMEM((banks * steps, generated), f32),
            pltpu.VMEM((banks, share, steps, columns), f32),
            pltpu.VMEM((bank_rows, steps, columns), f32),
            pltpu.VMEM((bank_rows, steps, columns), f32),
            pltpu.VMEM((banks, share, steps, columns), f32),
            dma((len(operands),)),
            dma((2, wide - 1, chunks)),
            dma((2, wide - 1, chunks)),
            dma((banks, share)),
            dma((bank_rows,)),
            dma((bank_rows,)),
            dma((banks, share)),
            dma((2,)),
        ],
        compiler_params=pltpu.CompilerParams(
            collective_id=0, has_side_effects=True, vmem_limit_bytes=54 * 2**20
        ),
        name="mix_and_generate",
    )(local, *operands)


def power_of_two(number):
    return number > 0 and number & (number - 1) == 0


def fits_kernels(wide, narrow, ids, table, reward, acceptance):
    bank_rows, length = ids.shape[1], ids.shape[2]
    columns = table.shape[0]
    banks, prompts, steps, generated = acceptance.shape
    return (
        prompts == 1
        and wide % 2 == 0
        and wide > 2
        and wide % narrow == 0
        and banks == narrow
        and bank_rows == wide
        and length % 16 == 0
        and columns % lane_count == 0
        and table.shape[1] % lane_count == 0
        and generated == columns * (wide // narrow)
        and lane_count % reward.shape[1] == 0
        and all(power_of_two(size) for size in (length, steps, bank_rows, reward.shape[1]))
        and columns * length * bank_rows * lane_count * 2 <= 2**25
    )


def per_device(
    context_symbol_ids,
    context_symbol_spans,
    symbol_vector_lookup,
    opening_lagged_blend,
    lagged_blend_weights,
    blending_left_operand,
    blending_right_operands,
    fixed_fading_scores,
    fading_left_operand,
    fading_right_operand,
    address_projector,
    payload_projector,
    present_symbol_reward,
    cluster_scaling_weight,
    cluster_scaling_offset,
    generated_acceptance,
    generated_addresses,
    generated_payloads,
    generated_fading_scores,
    generated_valve_scores,
):
    wide, narrow = lax.axis_size("wide"), lax.axis_size("narrow")
    if fits_kernels(
        wide,
        narrow,
        context_symbol_ids,
        symbol_vector_lookup,
        present_symbol_reward,
        generated_acceptance,
    ):
        return mixing(
            wide,
            narrow,
            gather_tokens(context_symbol_ids, symbol_vector_lookup),
            blending_left_operand.T,
            generated_acceptance,
            generated_fading_scores,
            opening_lagged_blend[None],
            blending_right_operands.reshape(-1, blending_right_operands.shape[2]),
            lagged_blend_weights,
            fading_left_operand,
            address_projector,
            payload_projector,
            fixed_fading_scores[None],
            fading_right_operand,
            context_symbol_spans,
            generated_addresses,
            generated_payloads,
            generated_valve_scores,
            present_symbol_reward,
            cluster_scaling_weight[None],
            cluster_scaling_offset[None],
        )
    bank_rows = context_symbol_ids.shape[1]
    length = context_symbol_ids.shape[2]
    columns = symbol_vector_lookup.shape[0]
    attender_width = present_symbol_reward.shape[1]
    head_local = columns // attender_width
    lengths = context_symbol_spans.reshape(-1)
    picked = jnp.take(symbol_vector_lookup, context_symbol_ids.reshape(-1), axis=1)
    gathered = lax.all_gather(picked, "wide", axis=0, tiled=True).T
    features = gathered.shape[1]
    block_rows = bank_rows
    while block_rows % 2 == 0 and block_rows * length > 1024:
        block_rows = block_rows // 2
    blocks = gathered.reshape(bank_rows // block_rows, block_rows, length, features)
    length_blocks = lengths.reshape(bank_rows // block_rows, block_rows)

    def one_block(block_item):
        key_proj, value_proj, decay_log = mix_project(
            block_item[0],
            opening_lagged_blend,
            lagged_blend_weights,
            blending_left_operand,
            blending_right_operands,
            fixed_fading_scores,
            fading_left_operand,
            fading_right_operand,
            address_projector,
            payload_projector,
        )
        block_shape = (block_rows, length, columns)
        return final_states(
            key_proj.reshape(block_shape),
            value_proj.reshape(block_shape),
            decay_log.reshape(block_shape),
            block_item[1],
            attender_width,
        )

    recurrent_memories = lax.map(one_block, (blocks, length_blocks)).reshape(
        bank_rows, head_local, attender_width, attender_width
    )
    handed = lax.all_to_all(
        lax.all_to_all(
            recurrent_memories.reshape(1, bank_rows, head_local, attender_width * attender_width),
            "wide",
            split_axis=1,
            concat_axis=2,
            tiled=True,
        ),
        "narrow",
        split_axis=2,
        concat_axis=0,
        tiled=True,
    )
    generated_by_attender = handed.shape[2]
    leading_attender_offset = lax.axis_index("narrow") * generated_by_attender
    shard_reward = lax.dynamic_slice_in_dim(
        present_symbol_reward, leading_attender_offset, generated_by_attender, 0
    )
    shard_scaling_weight = lax.dynamic_slice_in_dim(
        cluster_scaling_weight,
        leading_attender_offset * attender_width,
        generated_by_attender * attender_width,
        0,
    )
    shard_scaling_offset = lax.dynamic_slice_in_dim(
        cluster_scaling_offset,
        leading_attender_offset * attender_width,
        generated_by_attender * attender_width,
        0,
    )
    result = generation_iterations(
        handed.reshape(handed.shape[:3] + (attender_width, attender_width)),
        generated_acceptance,
        generated_addresses,
        generated_payloads,
        generated_fading_scores,
        generated_valve_scores,
        shard_reward,
        shard_scaling_weight,
        shard_scaling_offset,
    )
    return result


def solution(mesh):
    placed = (
        P("narrow", "groups", None),
        P("narrow", "groups"),
        P("wide", None),
        P(),
        P(),
        P(),
        P(),
        P("wide"),
        P(),
        P(None, "wide"),
        P("wide", None),
        P("wide", None),
        P(),
        P(),
        P(),
        P(None, ("groups", "wide"), None, "narrow"),
        P(None, ("groups", "wide"), None, "narrow"),
        P(None, ("groups", "wide"), None, "narrow"),
        P(None, ("groups", "wide"), None, "narrow"),
        P(None, ("groups", "wide"), None, "narrow"),
    )
    return jax.shard_map(
        per_device,
        mesh=mesh,
        in_specs=placed,
        out_specs=P(None, ("groups", "wide"), None, "narrow"),
        check_vma=False,
    )
```

```python
import functools

import jax
import jax.numpy as jnp
from jax import lax
from jax.experimental import pallas as pl
from jax.experimental.pallas import tpu as pltpu
from jax.sharding import PartitionSpec as P

norm_eps = 0.00064
lane_count = 128


def mix_project(
    embedded,
    opening_lagged_blend,
    lagged_blend_weights,
    blending_left_operand,
    blending_right_operands,
    fixed_fading_scores,
    fading_left_operand,
    fading_right_operand,
    address_projector,
    payload_projector,
):
    features = embedded.shape[2]
    previous = jnp.pad(embedded, ((0, 0), (1, 0), (0, 0)))[:, :-1, :]
    current = embedded.reshape(-1, features).astype(jnp.float32)
    difference = previous.reshape(-1, features).astype(jnp.float32) - current
    mixed_in = (current + difference * opening_lagged_blend).astype(jnp.bfloat16)
    hidden = jnp.tanh(
        jnp.dot(mixed_in, blending_left_operand, preferred_element_type=jnp.float32)
    ).astype(jnp.bfloat16)
    rank_size = blending_right_operands.shape[1]
    branches = []
    for branch in range(3):
        shift_term = jnp.dot(
            hidden[:, branch * rank_size : (branch + 1) * rank_size],
            blending_right_operands[branch],
            preferred_element_type=jnp.float32,
        )
        branches.append(
            (current + difference * (lagged_blend_weights[branch] + shift_term)).astype(
                jnp.bfloat16
            )
        )
    decay_hidden = jnp.tanh(
        jnp.dot(branches[0], fading_left_operand, preferred_element_type=jnp.float32)
    ).astype(jnp.bfloat16)
    decay_log = fixed_fading_scores + jnp.dot(
        decay_hidden, fading_right_operand, preferred_element_type=jnp.float32
    )
    key_proj = jnp.dot(branches[1], address_projector.T, preferred_element_type=jnp.float32).astype(
        jnp.bfloat16
    )
    value_proj = jnp.dot(
        branches[2], payload_projector.T, preferred_element_type=jnp.float32
    ).astype(jnp.bfloat16)
    return (key_proj, value_proj, decay_log)


def final_states(key_proj, value_proj, decay_log, lengths, attender_width):
    bank_rows, length, columns = key_proj.shape
    attender_ordinal = columns // attender_width
    decay_rates = jnp.exp(decay_log)
    places = lax.broadcasted_iota(jnp.int32, (bank_rows, length), 1)
    live_mask = (places < lengths[:, None])[:, :, None]
    running = jnp.cumsum(jnp.where(live_mask, decay_rates, 0.0), axis=1)
    remaining = running[:, -1:, :] - running
    weights = jnp.where(live_mask, jnp.exp(-remaining), 0.0)
    weighted = (key_proj.astype(jnp.float32) * weights).reshape(
        bank_rows, length, attender_ordinal, attender_width
    )
    plain_values = value_proj.astype(jnp.float32).reshape(
        bank_rows, length, attender_ordinal, attender_width
    )
    return jnp.einsum("rlhi,rlhj->rhij", weighted, plain_values, precision=lax.Precision.HIGHEST)


def generation_iterations(
    recurrent_memories,
    acceptance_lines,
    address_source,
    payload_source,
    fading_source,
    valve_source,
    shard_reward,
    shard_scaling_weight,
    shard_scaling_offset,
):
    attender_ordinal = recurrent_memories.shape[-3]
    attender_width = recurrent_memories.shape[-1]
    leading = acceptance_lines.shape[:-2]
    step_count = acceptance_lines.shape[-2]
    split_shape = leading + (step_count, attender_ordinal, attender_width)
    receptance = acceptance_lines.astype(jnp.float32).reshape(split_shape)
    key_split = address_source.astype(jnp.float32).reshape(split_shape)
    valued = payload_source.astype(jnp.float32).reshape(split_shape)
    factors = jnp.exp(-jnp.exp(fading_source.astype(jnp.float32))).reshape(split_shape)
    results = []
    for position in range(step_count):
        present_acceptance = receptance[..., position, :, :]
        present_address = key_split[..., position, :, :]
        present_payload = valued[..., position, :, :]
        immediate_summand = (
            jnp.sum(present_acceptance * shard_reward * present_address, axis=-1, keepdims=True)
            * present_payload
        )
        carried = jnp.einsum(
            "...hi,...hij->...hj",
            present_acceptance,
            recurrent_memories,
            precision=lax.Precision.HIGHEST,
        )
        results.append(carried + immediate_summand)
        if position + 1 < step_count:
            recurrent_memories = (
                factors[..., position, :, :][..., :, None] * recurrent_memories
                + present_address[..., :, None] * present_payload[..., None, :]
            )
    mixed_out = jnp.stack(results, axis=-3)
    average = jnp.mean(mixed_out, axis=-1, keepdims=True)
    centred = mixed_out - average
    spread = jnp.mean(centred * centred, axis=-1, keepdims=True)
    normed = (centred * lax.rsqrt(spread + norm_eps)).reshape(
        leading + (step_count, attender_ordinal * attender_width)
    )
    return (
        (normed * shard_scaling_weight + shard_scaling_offset)
        * jax.nn.silu(valve_source.astype(jnp.float32))
    ).astype(jnp.bfloat16)


def gather_body(ids_ref, table_ref, out_ref, strips, found, sems):
    rows, length = ids_ref.shape[1], ids_ref.shape[2]
    lanes = strips.shape[2] // length

    def strip(row, place):
        tile = lax.div(ids_ref[0, row, place], lanes)
        return pltpu.make_async_copy(
            table_ref.at[:, pl.ds(pl.multiple_of(tile * lanes, lanes), lanes)],
            strips.at[row, :, pl.ds(place * lanes, lanes)],
            sems.at[row, place],
        )

    def start(row, carry):
        for place in range(length):
            strip(row, place).start()
        return carry

    lax.fori_loop(0, rows, start, 0)
    tokens = rows * length
    depths = lax.broadcasted_iota(jnp.int32, (lanes, tokens), 0)
    chosen_tokens = lax.broadcasted_iota(jnp.int32, (lanes, tokens), 1)
    found[...] = jnp.zeros_like(found)

    def pick(row, carry):
        chosen = jnp.concatenate(
            [
                jnp.where(
                    (depths == lax.rem(ids_ref[0, row, place], lanes))
                    & (chosen_tokens == row * length + place),
                    1.0,
                    0.0,
                ).astype(jnp.bfloat16)
                for place in range(length)
            ],
            axis=0,
        )
        for place in range(length):
            strip(row, place).wait()
        found[...] += jnp.dot(strips[row], chosen, preferred_element_type=jnp.float32)
        return carry

    lax.fori_loop(0, rows, pick, 0)
    out_ref[...] = found[...].T.astype(jnp.bfloat16)


def gather_tokens(ids, table):
    rows, length = ids.shape[1], ids.shape[2]
    columns = table.shape[0]
    return pl.pallas_call(
        gather_body,
        out_shape=jax.ShapeDtypeStruct((rows * length, columns), jnp.bfloat16),
        in_specs=[
            pl.BlockSpec(memory_space=pltpu.SMEM),
            pl.BlockSpec(memory_space=pl.ANY),
        ],
        out_specs=pl.BlockSpec(memory_space=pltpu.VMEM),
        scratch_shapes=[
            pltpu.VMEM((rows, columns, length * lane_count), jnp.bfloat16),
            pltpu.VMEM((columns, rows * length), jnp.float32),
            pltpu.SemaphoreType.DMA((rows, length)),
        ],
        compiler_params=pltpu.CompilerParams(vmem_limit_bytes=40 * 2**20),
        name="pick_tokens",
    )(ids, table)


def segment_sums(rows, ones):
    width = ones.shape[0]
    high = rows.astype(jnp.bfloat16)
    low = (rows - high.astype(jnp.float32)).astype(jnp.bfloat16)
    parts = []
    for begin in range(0, rows.shape[1], width):
        stop = begin + width
        parts.append(
            jnp.dot(high[:, begin:stop], ones, preferred_element_type=jnp.float32)
            + jnp.dot(low[:, begin:stop], ones, preferred_element_type=jnp.float32)
        )
    return jnp.concatenate(parts, axis=1)


def mixing_body(wide, narrow, chunks, local_ref, *refs):
    sources, out_ref, loaded = refs[:18], refs[18], refs[19:37]
    (
        left,
        r_ref,
        w_ref,
        opening_ref,
        right,
        blends_ref,
        fading_left,
        address,
        payload,
        fixed_ref,
        fading_right_ref,
        spans_ref,
        k_ref,
        v_ref,
        g_ref,
        reward_ref,
        scaling_ref,
        offset_ref,
    ) = loaded
    (
        held,
        hidden_sum,
        key_sum,
        value_sum,
        decay_sum,
        pairs,
        own_part,
        r_send,
        r_recv,
        y_send,
        y_recv,
        load_sems,
        line_send,
        line_recv,
        cross_send,
        cross_recv,
        r_send_sems,
        r_recv_sems,
        y_send_sems,
        y_recv_sems,
        self_sems,
    ) = refs[37:]
    w_me = lax.axis_index("wide")
    n_me = lax.axis_index("narrow")
    tokens, columns = local_ref.shape
    bank_rows = spans_ref.shape[1]
    length = tokens // bank_rows
    features = opening_ref.shape[1]
    head = reward_ref.shape[1]
    banks, _, steps, generated = r_ref.shape
    share = wide // narrow
    half_owner = lax.div(w_me, share)
    place_in_half = lax.rem(w_me, share)

    barrier = pltpu.get_barrier_semaphore()
    for other in range(1, wide * narrow):
        flat = lax.rem(w_me * narrow + n_me + other, wide * narrow)
        pl.semaphore_signal(
            barrier,
            inc=1,
            device_id={"wide": lax.div(flat, narrow), "narrow": lax.rem(flat, narrow)},
            device_id_type=pl.DeviceIdType.MESH,
        )

    loads = [
        pltpu.make_async_copy(source, target, load_sems.at[number])
        for number, (source, target) in enumerate(zip(sources, loaded))
    ]
    first_loads = 4
    for load in loads[:first_loads]:
        load.start()

    held[w_me] = local_ref[...]

    line_me, side = lax.div(w_me, 2), lax.rem(w_me, 2)
    partner = 2 * line_me + 1 - side
    lines = wide // 2
    chunk_rows = tokens // chunks

    def owner_of(offset, own_side):
        return 2 * lax.bitwise_xor(line_me, offset) + (side if own_side else 1 - side)

    def line_copy(offset, chunk, arrival=False):
        piece = held.at[
            owner_of(offset, True) if arrival else w_me, pl.ds(chunk * chunk_rows, chunk_rows)
        ]
        return pltpu.make_async_remote_copy(
            src_ref=piece,
            dst_ref=piece,
            send_sem=line_send.at[offset - 1, chunk],
            recv_sem=line_recv.at[offset - 1, chunk],
            device_id={"wide": owner_of(offset, True)},
            device_id_type=pl.DeviceIdType.MESH,
        )

    def cross_copy(offset, chunk, arrival=False):
        piece = held.at[owner_of(offset, not arrival), pl.ds(chunk * chunk_rows, chunk_rows)]
        return pltpu.make_async_remote_copy(
            src_ref=piece,
            dst_ref=piece,
            send_sem=cross_send.at[offset, chunk],
            recv_sem=cross_recv.at[offset, chunk],
            device_id={"wide": partner},
            device_id_type=pl.DeviceIdType.MESH,
        )

    transposed = (((1,), (1,)), ((), ()))

    def with_difference(block):
        current = block.astype(jnp.float32)
        places = lax.broadcasted_iota(jnp.int32, current.shape, 0) & (length - 1)
        previous = jnp.where(places == 0, 0.0, pltpu.roll(current, 1, 0))
        return current, previous - current

    def add_hidden(owner):
        feature_rows = pl.ds(pl.multiple_of(owner * columns, columns), columns)
        current, difference = with_difference(held[owner])
        mixed = (current + difference * opening_ref[:, feature_rows]).astype(jnp.bfloat16)
        hidden_sum[...] += lax.dot_general(
            mixed, left[:, feature_rows], transposed, preferred_element_type=jnp.float32
        )

    def r_copy(bank, part):
        return pltpu.make_async_remote_copy(
            src_ref=r_send.at[bank, part],
            dst_ref=r_recv.at[w_me],
            send_sem=r_send_sems.at[bank, part],
            recv_sem=r_recv_sems.at[w_me],
            device_id={"wide": n_me * share + part, "narrow": bank},
            device_id_type=pl.DeviceIdType.MESH,
        )

    def r_self(bank, part):
        return pltpu.make_async_copy(r_send.at[bank, part], r_recv.at[w_me], self_sems.at[0])

    def r_arrival(prompt):
        return pltpu.make_async_remote_copy(
            src_ref=r_send.at[0, 0],
            dst_ref=r_recv.at[prompt],
            send_sem=r_send_sems.at[0, 0],
            recv_sem=r_recv_sems.at[prompt],
            device_id={"wide": prompt, "narrow": half_owner},
            device_id_type=pl.DeviceIdType.MESH,
        )

    def y_copy(prompt):
        return pltpu.make_async_remote_copy(
            src_ref=y_send.at[prompt],
            dst_ref=y_recv.at[n_me, place_in_half],
            send_sem=y_send_sems.at[prompt],
            recv_sem=y_recv_sems.at[n_me, place_in_half],
            device_id={"wide": prompt, "narrow": half_owner},
            device_id_type=pl.DeviceIdType.MESH,
        )

    def y_self(prompt):
        return pltpu.make_async_copy(
            y_send.at[prompt], y_recv.at[n_me, place_in_half], self_sems.at[1]
        )

    def y_arrival(bank, part):
        return pltpu.make_async_remote_copy(
            src_ref=y_send.at[0],
            dst_ref=y_recv.at[bank, part],
            send_sem=y_send_sems.at[0],
            recv_sem=y_recv_sems.at[bank, part],
            device_id={"wide": n_me * share + part, "narrow": bank},
            device_id_type=pl.DeviceIdType.MESH,
        )

    def generated_is_mine(bank, part):
        return jnp.logical_and(n_me * share + part == w_me, n_me == bank)

    def prompt_is_mine(prompt):
        return jnp.logical_and(w_me == prompt, n_me == half_owner)

    pl.semaphore_wait(barrier, wide * narrow - 1)
    for chunk in range(chunks):
        for offset in range(1, lines):
            line_copy(offset, chunk).start()
        cross_copy(0, chunk).start()

    hidden_sum[...] = jnp.zeros_like(hidden_sum)
    for load in loads[:first_loads]:
        load.wait()
    for load in loads[first_loads:]:
        load.start()
    for bank in range(banks):
        r_all = r_ref[bank, 0].astype(jnp.float32)
        w_all = jnp.exp(-jnp.exp(w_ref[bank, 0].astype(jnp.float32)))
        faded = None
        for step in range(steps):
            line = r_all[step : step + 1]
            if step > 0:
                now = w_all[step - 1 : step]
                faded = now if faded is None else faded * now
                line = line * faded
            for part in range(share):
                r_send[bank, part, step : step + 1, :] = line[
                    :, part * columns : (part + 1) * columns
                ]
    for bank in range(banks):
        for part in range(share):

            @pl.when(generated_is_mine(bank, part))
            def _():
                r_self(bank, part).start()

            @pl.when(jnp.logical_not(generated_is_mine(bank, part)))
            def _():
                r_copy(bank, part).start()

    add_hidden(w_me)

    def gather_step(offset, carry):
        for chunk in range(chunks):
            line_copy(offset, chunk, True).wait_recv()
            cross_copy(offset, chunk).start()
        add_hidden(owner_of(offset, True))
        for chunk in range(chunks):
            cross_copy(offset - 1, chunk, True).wait_recv()
        add_hidden(owner_of(offset - 1, False))
        return carry

    lax.fori_loop(1, lines, gather_step, 0)
    for load in loads[first_loads:]:
        load.wait()
    decay_sum[...] = jnp.zeros_like(decay_sum)
    key_sum[...] = jnp.zeros_like(key_sum)
    value_sum[...] = jnp.zeros_like(value_sum)
    for chunk in range(chunks):
        cross_copy(lines - 1, chunk, True).wait_recv()
    add_hidden(owner_of(lines - 1, False))

    hidden = jnp.tanh(hidden_sum[...])
    rank = right.shape[0] // 3
    hidden_lanes = lax.broadcasted_iota(jnp.int32, hidden.shape, 1)
    hidden_parts = jnp.concatenate(
        [
            jnp.where(
                (hidden_lanes >= branch * rank) & (hidden_lanes < (branch + 1) * rank), hidden, 0.0
            )
            for branch in range(3)
        ],
        axis=0,
    ).astype(jnp.bfloat16)

    def project(block, carry):
        span = pl.ds(pl.multiple_of(block * columns, columns), columns)
        current, difference = with_difference(held[block])
        shifts = jnp.dot(hidden_parts, right[:, span], preferred_element_type=jnp.float32)
        mixed = [
            (
                current
                + difference
                * (
                    blends_ref[branch : branch + 1, span]
                    + shifts[branch * tokens : (branch + 1) * tokens]
                )
            ).astype(jnp.bfloat16)
            for branch in range(3)
        ]
        decay_sum[...] += jnp.dot(
            mixed[0], fading_left[span, :], preferred_element_type=jnp.float32
        )
        key_sum[...] += lax.dot_general(
            mixed[1], address[:, span], transposed, preferred_element_type=jnp.float32
        )
        value_sum[...] += lax.dot_general(
            mixed[2], payload[:, span], transposed, preferred_element_type=jnp.float32
        )
        return carry

    lax.fori_loop(0, wide, project, 0, unroll=2)

    decay_hidden = jnp.tanh(decay_sum[...]).astype(jnp.bfloat16)
    rates = jnp.exp(
        fixed_ref[...]
        + jnp.dot(decay_hidden, fading_right_ref[...], preferred_element_type=jnp.float32)
    )
    row_ids = lax.broadcasted_iota(jnp.int32, (tokens, tokens), 0)
    column_ids = lax.broadcasted_iota(jnp.int32, (tokens, tokens), 1)
    row_limit = jnp.zeros((tokens, 1), jnp.int32)
    column_limit = jnp.zeros((tokens, tokens), jnp.int32)
    row_line = lax.broadcasted_iota(jnp.int32, (tokens, 1), 0)
    for prompt in range(bank_rows):
        span_now = spans_ref[0, prompt]
        row_limit = jnp.where(row_line & -length == prompt * length, span_now, row_limit)
        column_limit = jnp.where(column_ids & -length == prompt * length, span_now, column_limit)
    later = jnp.where(
        (row_ids & -length == column_ids & -length)
        & (column_ids > row_ids)
        & (column_ids & (length - 1) < column_limit),
        1.0,
        0.0,
    ).astype(jnp.bfloat16)
    high = rates.astype(jnp.bfloat16)
    low = (rates - high.astype(jnp.float32)).astype(jnp.bfloat16)
    remaining = jnp.dot(later, high, preferred_element_type=jnp.float32) + jnp.dot(
        later, low, preferred_element_type=jnp.float32
    )
    weights = jnp.where(row_line & (length - 1) < row_limit, jnp.exp(-remaining), 0.0)
    weighted = (
        key_sum[...].astype(jnp.bfloat16).astype(jnp.float32) * weights
    ).astype(jnp.bfloat16)
    values = value_sum[...].astype(jnp.bfloat16)

    for prompt in range(bank_rows):

        @pl.when(prompt_is_mine(prompt))
        def _():
            for bank in range(banks):
                for part in range(share):

                    @pl.when(generated_is_mine(bank, part))
                    def _():
                        r_self(bank, part).wait()

        @pl.when(jnp.logical_not(prompt_is_mine(prompt)))
        def _():
            r_arrival(prompt).wait_recv()

    asked = jnp.concatenate([r_recv[prompt] for prompt in range(bank_rows)], axis=0)
    asked_rows = bank_rows * steps
    lane_heads = lax.broadcasted_iota(jnp.int32, (asked_rows, columns), 1) & -head
    heads = columns // head
    spread = jnp.concatenate(
        [jnp.where(lane_heads == number * head, asked, 0.0) for number in range(heads)], axis=0
    ).astype(jnp.bfloat16)
    scores = lax.dot_general(spread, weighted, transposed, preferred_element_type=jnp.float32)
    score_rows = lax.broadcasted_iota(jnp.int32, scores.shape, 0) & (asked_rows - 1)
    score_columns = lax.broadcasted_iota(jnp.int32, scores.shape, 1)
    kept = jnp.where(
        lax.shift_right_logical(score_rows, steps.bit_length() - 1)
        == lax.shift_right_logical(score_columns, length.bit_length() - 1),
        scores,
        0.0,
    )
    answers = jnp.dot(kept.astype(jnp.bfloat16), values, preferred_element_type=jnp.float32)
    answer = jnp.zeros((asked_rows, columns), jnp.float32)
    for number in range(heads):
        answer = jnp.where(
            lane_heads == number * head,
            answers[number * asked_rows : (number + 1) * asked_rows],
            answer,
        )
    for prompt in range(bank_rows):
        y_send[prompt] = answer[prompt * steps : (prompt + 1) * steps]
    for prompt in range(bank_rows):

        @pl.when(prompt_is_mine(prompt))
        def _():
            y_self(prompt).start()

        @pl.when(jnp.logical_not(prompt_is_mine(prompt)))
        def _():
            y_copy(prompt).start()

    ones = jnp.where(
        lax.broadcasted_iota(jnp.int32, (lane_count, lane_count), 0) & -head
        == lax.broadcasted_iota(jnp.int32, (lane_count, lane_count), 1) & -head,
        1.0,
        0.0,
    ).astype(jnp.bfloat16)
    first_head = pl.multiple_of(n_me * (generated // head), generated // head)
    rewards = reward_ref[pl.ds(first_head, generated // head), :]
    reward_line = jnp.concatenate(
        [rewards[number : number + 1, :] for number in range(generated // head)], axis=1
    )
    pair_rows = {}
    for bank in range(banks):
        r_all = r_ref[bank, 0].astype(jnp.float32)
        k_all = k_ref[bank, 0].astype(jnp.float32)
        w_all = jnp.exp(-jnp.exp(w_ref[bank, 0].astype(jnp.float32)))
        for step in range(steps):
            lagged = r_all[step : step + 1]
            for earlier in range(step, -1, -1):
                line = lagged * k_all[earlier : earlier + 1]
                if earlier == step:
                    line = line * reward_line
                elif earlier > 0:
                    lagged = lagged * w_all[earlier : earlier + 1]
                row = len(pair_rows)
                pair_rows[bank, step, earlier] = row
                pairs[row : row + 1, :] = line
    sums = segment_sums(pairs[...], ones)
    for bank in range(banks):
        v_all = v_ref[bank, 0].astype(jnp.float32)
        for now in range(steps):
            line = None
            for earlier in range(now + 1):
                row = pair_rows[bank, now, earlier]
                term = sums[row : row + 1, :] * v_all[earlier : earlier + 1]
                line = term if line is None else line + term
            own_part[bank * steps + now : bank * steps + now + 1, :] = line
    gate_lines = []
    for bank in range(banks):
        gate = g_ref[bank, 0].astype(jnp.float32)
        gate_lines.append(gate / (1.0 + jnp.exp(-gate)))
    half_columns = pl.ds(pl.multiple_of(n_me * generated, generated), generated)
    gain = scaling_ref[:, half_columns]
    bias = offset_ref[:, half_columns]

    for chunk in range(chunks):
        for offset in range(lines):
            if offset > 0:
                line_copy(offset, chunk).wait_send()
            cross_copy(offset, chunk).wait_send()
    for bank in range(banks):
        for part in range(share):

            @pl.when(jnp.logical_not(generated_is_mine(bank, part)))
            def _():
                r_copy(bank, part).wait_send()

    for bank in range(banks):
        for part in range(share):

            @pl.when(generated_is_mine(bank, part))
            def _():
                for prompt in range(bank_rows):

                    @pl.when(prompt_is_mine(prompt))
                    def _():
                        y_self(prompt).wait()

            @pl.when(jnp.logical_not(generated_is_mine(bank, part)))
            def _():
                y_arrival(bank, part).wait_recv()

    received = jnp.concatenate(
        [
            jnp.concatenate([y_recv[bank, part] for part in range(share)], axis=1)
            for bank in range(banks)
        ],
        axis=0,
    )
    y = received + own_part[...]
    centred = y - segment_sums(y, ones) * (1.0 / head)
    variance = segment_sums(centred * centred, ones) * (1.0 / head)
    normed = centred * lax.rsqrt(variance + norm_eps) * gain + bias
    for bank in range(banks):
        out_ref[bank, 0] = (normed[bank * steps : (bank + 1) * steps] * gate_lines[bank]).astype(
            out_ref.dtype
        )
    for prompt in range(bank_rows):

        @pl.when(jnp.logical_not(prompt_is_mine(prompt)))
        def _():
            y_copy(prompt).wait_send()


def mixing(wide, narrow, local, *operands):
    tokens, columns = local.shape
    left, receptance, fading_left, spans = operands[0], operands[1], operands[6], operands[11]
    bank_rows = spans.shape[1]
    banks, _, steps, generated = receptance.shape
    share = wide // narrow
    chunks = bank_rows // 2
    pair_count = banks * steps * (steps + 1) // 2
    vmem = pl.BlockSpec(memory_space=pltpu.VMEM)
    far = pl.BlockSpec(memory_space=pl.ANY)
    f32 = jnp.float32
    dma = pltpu.SemaphoreType.DMA
    return pl.pallas_call(
        functools.partial(mixing_body, wide, narrow, chunks),
        out_shape=jax.ShapeDtypeStruct(receptance.shape, jnp.bfloat16),
        in_specs=[vmem] + [far] * len(operands),
        out_specs=vmem,
        scratch_shapes=[
            pltpu.SMEM(operand.shape, operand.dtype)
            if operand is spans
            else pltpu.VMEM(operand.shape, operand.dtype)
            for operand in operands
        ]
        + [
            pltpu.VMEM((wide, tokens, columns), jnp.bfloat16),
            pltpu.VMEM((tokens, left.shape[0]), f32),
            pltpu.VMEM((tokens, columns), f32),
            pltpu.VMEM((tokens, columns), f32),
            pltpu.VMEM((tokens, fading_left.shape[1]), f32),
            pltpu.VMEM((pair_count, generated), f32),
            pltpu.VMEM((banks * steps, generated), f32),
            pltpu.VMEM((banks, share, steps, columns), f32),
            pltpu.VMEM((bank_rows, steps, columns), f32),
            pltpu.VMEM((bank_rows, steps, columns), f32),
            pltpu.VMEM((banks, share, steps, columns), f32),
            dma((len(operands),)),
            dma((wide // 2 - 1, chunks)),
            dma((wide // 2 - 1, chunks)),
            dma((wide // 2, chunks)),
            dma((wide // 2, chunks)),
            dma((banks, share)),
            dma((bank_rows,)),
            dma((bank_rows,)),
            dma((banks, share)),
            dma((2,)),
        ],
        compiler_params=pltpu.CompilerParams(
            collective_id=0, has_side_effects=True, vmem_limit_bytes=54 * 2**20
        ),
        name="mix_and_generate",
    )(local, *operands)


def power_of_two(number):
    return number > 0 and number & (number - 1) == 0


def fits_kernels(wide, narrow, ids, table, reward, acceptance):
    bank_rows, length = ids.shape[1], ids.shape[2]
    columns = table.shape[0]
    banks, prompts, steps, generated = acceptance.shape
    return (
        prompts == 1
        and wide % 2 == 0
        and wide > 2
        and wide % narrow == 0
        and banks == narrow
        and bank_rows == wide
        and length % 16 == 0
        and columns % lane_count == 0
        and table.shape[1] % lane_count == 0
        and generated == columns * (wide // narrow)
        and lane_count % reward.shape[1] == 0
        and all(power_of_two(size) for size in (length, steps, bank_rows, reward.shape[1]))
        and columns * length * bank_rows * lane_count * 2 <= 2**25
    )


def per_device(
    context_symbol_ids,
    context_symbol_spans,
    symbol_vector_lookup,
    opening_lagged_blend,
    lagged_blend_weights,
    blending_left_operand,
    blending_right_operands,
    fixed_fading_scores,
    fading_left_operand,
    fading_right_operand,
    address_projector,
    payload_projector,
    present_symbol_reward,
    cluster_scaling_weight,
    cluster_scaling_offset,
    generated_acceptance,
    generated_addresses,
    generated_payloads,
    generated_fading_scores,
    generated_valve_scores,
):
    wide, narrow = lax.axis_size("wide"), lax.axis_size("narrow")
    if fits_kernels(
        wide,
        narrow,
        context_symbol_ids,
        symbol_vector_lookup,
        present_symbol_reward,
        generated_acceptance,
    ):
        return mixing(
            wide,
            narrow,
            gather_tokens(context_symbol_ids, symbol_vector_lookup),
            blending_left_operand.T,
            generated_acceptance,
            generated_fading_scores,
            opening_lagged_blend[None],
            blending_right_operands.reshape(-1, blending_right_operands.shape[2]),
            lagged_blend_weights,
            fading_left_operand,
            address_projector,
            payload_projector,
            fixed_fading_scores[None],
            fading_right_operand,
            context_symbol_spans,
            generated_addresses,
            generated_payloads,
            generated_valve_scores,
            present_symbol_reward,
            cluster_scaling_weight[None],
            cluster_scaling_offset[None],
        )
    bank_rows = context_symbol_ids.shape[1]
    length = context_symbol_ids.shape[2]
    columns = symbol_vector_lookup.shape[0]
    attender_width = present_symbol_reward.shape[1]
    head_local = columns // attender_width
    lengths = context_symbol_spans.reshape(-1)
    picked = jnp.take(symbol_vector_lookup, context_symbol_ids.reshape(-1), axis=1)
    gathered = lax.all_gather(picked, "wide", axis=0, tiled=True).T
    features = gathered.shape[1]
    block_rows = bank_rows
    while block_rows % 2 == 0 and block_rows * length > 1024:
        block_rows = block_rows // 2
    blocks = gathered.reshape(bank_rows // block_rows, block_rows, length, features)
    length_blocks = lengths.reshape(bank_rows // block_rows, block_rows)

    def one_block(block_item):
        key_proj, value_proj, decay_log = mix_project(
            block_item[0],
            opening_lagged_blend,
            lagged_blend_weights,
            blending_left_operand,
            blending_right_operands,
            fixed_fading_scores,
            fading_left_operand,
            fading_right_operand,
            address_projector,
            payload_projector,
        )
        block_shape = (block_rows, length, columns)
        return final_states(
            key_proj.reshape(block_shape),
            value_proj.reshape(block_shape),
            decay_log.reshape(block_shape),
            block_item[1],
            attender_width,
        )

    recurrent_memories = lax.map(one_block, (blocks, length_blocks)).reshape(
        bank_rows, head_local, attender_width, attender_width
    )
    handed = lax.all_to_all(
        lax.all_to_all(
            recurrent_memories.reshape(1, bank_rows, head_local, attender_width * attender_width),
            "wide",
            split_axis=1,
            concat_axis=2,
            tiled=True,
        ),
        "narrow",
        split_axis=2,
        concat_axis=0,
        tiled=True,
    )
    generated_by_attender = handed.shape[2]
    leading_attender_offset = lax.axis_index("narrow") * generated_by_attender
    shard_reward = lax.dynamic_slice_in_dim(
        present_symbol_reward, leading_attender_offset, generated_by_attender, 0
    )
    shard_scaling_weight = lax.dynamic_slice_in_dim(
        cluster_scaling_weight,
        leading_attender_offset * attender_width,
        generated_by_attender * attender_width,
        0,
    )
    shard_scaling_offset = lax.dynamic_slice_in_dim(
        cluster_scaling_offset,
        leading_attender_offset * attender_width,
        generated_by_attender * attender_width,
        0,
    )
    result = generation_iterations(
        handed.reshape(handed.shape[:3] + (attender_width, attender_width)),
        generated_acceptance,
        generated_addresses,
        generated_payloads,
        generated_fading_scores,
        generated_valve_scores,
        shard_reward,
        shard_scaling_weight,
        shard_scaling_offset,
    )
    return result


def solution(mesh):
    placed = (
        P("narrow", "groups", None),
        P("narrow", "groups"),
        P("wide", None),
        P(),
        P(),
        P(),
        P(),
        P("wide"),
        P(),
        P(None, "wide"),
        P("wide", None),
        P("wide", None),
        P(),
        P(),
        P(),
        P(None, ("groups", "wide"), None, "narrow"),
        P(None, ("groups", "wide"), None, "narrow"),
        P(None, ("groups", "wide"), None, "narrow"),
        P(None, ("groups", "wide"), None, "narrow"),
        P(None, ("groups", "wide"), None, "narrow"),
    )
    return jax.shard_map(
        per_device,
        mesh=mesh,
        in_specs=placed,
        out_specs=P(None, ("groups", "wide"), None, "narrow"),
        check_vma=False,
    )
```

```python
import functools

import jax
import jax.numpy as jnp
from jax import lax
from jax.experimental import pallas as pl
from jax.experimental.pallas import tpu as pltpu
from jax.sharding import PartitionSpec as P

norm_eps = 0.00064
lane_count = 128


def mix_project(
    embedded,
    opening_lagged_blend,
    lagged_blend_weights,
    blending_left_operand,
    blending_right_operands,
    fixed_fading_scores,
    fading_left_operand,
    fading_right_operand,
    address_projector,
    payload_projector,
):
    features = embedded.shape[2]
    previous = jnp.pad(embedded, ((0, 0), (1, 0), (0, 0)))[:, :-1, :]
    current = embedded.reshape(-1, features).astype(jnp.float32)
    difference = previous.reshape(-1, features).astype(jnp.float32) - current
    mixed_in = (current + difference * opening_lagged_blend).astype(jnp.bfloat16)
    hidden = jnp.tanh(
        jnp.dot(mixed_in, blending_left_operand, preferred_element_type=jnp.float32)
    ).astype(jnp.bfloat16)
    rank_size = blending_right_operands.shape[1]
    branches = []
    for branch in range(3):
        shift_term = jnp.dot(
            hidden[:, branch * rank_size : (branch + 1) * rank_size],
            blending_right_operands[branch],
            preferred_element_type=jnp.float32,
        )
        branches.append(
            (current + difference * (lagged_blend_weights[branch] + shift_term)).astype(
                jnp.bfloat16
            )
        )
    decay_hidden = jnp.tanh(
        jnp.dot(branches[0], fading_left_operand, preferred_element_type=jnp.float32)
    ).astype(jnp.bfloat16)
    decay_log = fixed_fading_scores + jnp.dot(
        decay_hidden, fading_right_operand, preferred_element_type=jnp.float32
    )
    key_proj = jnp.dot(branches[1], address_projector.T, preferred_element_type=jnp.float32).astype(
        jnp.bfloat16
    )
    value_proj = jnp.dot(
        branches[2], payload_projector.T, preferred_element_type=jnp.float32
    ).astype(jnp.bfloat16)
    return (key_proj, value_proj, decay_log)


def final_states(key_proj, value_proj, decay_log, lengths, attender_width):
    bank_rows, length, columns = key_proj.shape
    attender_ordinal = columns // attender_width
    decay_rates = jnp.exp(decay_log)
    places = lax.broadcasted_iota(jnp.int32, (bank_rows, length), 1)
    live_mask = (places < lengths[:, None])[:, :, None]
    running = jnp.cumsum(jnp.where(live_mask, decay_rates, 0.0), axis=1)
    remaining = running[:, -1:, :] - running
    weights = jnp.where(live_mask, jnp.exp(-remaining), 0.0)
    weighted = (key_proj.astype(jnp.float32) * weights).reshape(
        bank_rows, length, attender_ordinal, attender_width
    )
    plain_values = value_proj.astype(jnp.float32).reshape(
        bank_rows, length, attender_ordinal, attender_width
    )
    return jnp.einsum("rlhi,rlhj->rhij", weighted, plain_values, precision=lax.Precision.HIGHEST)


def generation_iterations(
    recurrent_memories,
    acceptance_lines,
    address_source,
    payload_source,
    fading_source,
    valve_source,
    shard_reward,
    shard_scaling_weight,
    shard_scaling_offset,
):
    attender_ordinal = recurrent_memories.shape[-3]
    attender_width = recurrent_memories.shape[-1]
    leading = acceptance_lines.shape[:-2]
    step_count = acceptance_lines.shape[-2]
    split_shape = leading + (step_count, attender_ordinal, attender_width)
    receptance = acceptance_lines.astype(jnp.float32).reshape(split_shape)
    key_split = address_source.astype(jnp.float32).reshape(split_shape)
    valued = payload_source.astype(jnp.float32).reshape(split_shape)
    factors = jnp.exp(-jnp.exp(fading_source.astype(jnp.float32))).reshape(split_shape)
    results = []
    for position in range(step_count):
        present_acceptance = receptance[..., position, :, :]
        present_address = key_split[..., position, :, :]
        present_payload = valued[..., position, :, :]
        immediate_summand = (
            jnp.sum(present_acceptance * shard_reward * present_address, axis=-1, keepdims=True)
            * present_payload
        )
        carried = jnp.einsum(
            "...hi,...hij->...hj",
            present_acceptance,
            recurrent_memories,
            precision=lax.Precision.HIGHEST,
        )
        results.append(carried + immediate_summand)
        if position + 1 < step_count:
            recurrent_memories = (
                factors[..., position, :, :][..., :, None] * recurrent_memories
                + present_address[..., :, None] * present_payload[..., None, :]
            )
    mixed_out = jnp.stack(results, axis=-3)
    average = jnp.mean(mixed_out, axis=-1, keepdims=True)
    centred = mixed_out - average
    spread = jnp.mean(centred * centred, axis=-1, keepdims=True)
    normed = (centred * lax.rsqrt(spread + norm_eps)).reshape(
        leading + (step_count, attender_ordinal * attender_width)
    )
    return (
        (normed * shard_scaling_weight + shard_scaling_offset)
        * jax.nn.silu(valve_source.astype(jnp.float32))
    ).astype(jnp.bfloat16)


def gather_body(ids_ref, table_ref, out_ref, strips, sems):
    rows, length = ids_ref.shape[1], ids_ref.shape[2]
    lanes = strips.shape[2] // length

    def strip(row, place):
        tile = lax.div(ids_ref[0, row, place], lanes)
        return pltpu.make_async_copy(
            table_ref.at[:, pl.ds(pl.multiple_of(tile * lanes, lanes), lanes)],
            strips.at[row, :, pl.ds(place * lanes, lanes)],
            sems.at[row, place],
        )

    def start(row, carry):
        for place in range(length):
            strip(row, place).start()
        return carry

    lax.fori_loop(0, rows, start, 0)
    places = lax.broadcasted_iota(jnp.int32, (length, lanes), 0)
    columns = lax.broadcasted_iota(jnp.int32, (length, lanes), 1)

    def pick(row, carry):
        wanted = jnp.zeros((length, lanes), jnp.int32)
        for place in range(length):
            wanted = jnp.where(places == place, lax.rem(ids_ref[0, row, place], lanes), wanted)
        hit = jnp.where(columns == wanted, 1.0, 0.0)
        chosen = jnp.concatenate(
            [jnp.where(places == place, hit, 0.0) for place in range(length)], axis=1
        ).astype(jnp.bfloat16)
        for place in range(length):
            strip(row, place).wait()
        found = lax.dot_general(
            chosen, strips[row], (((1,), (1,)), ((), ())), preferred_element_type=jnp.float32
        )
        out_ref[pl.ds(pl.multiple_of(row * length, length), length), :] = found.astype(jnp.bfloat16)
        return carry

    lax.fori_loop(0, rows, pick, 0)


def gather_tokens(ids, table):
    rows, length = ids.shape[1], ids.shape[2]
    columns = table.shape[0]
    return pl.pallas_call(
        gather_body,
        out_shape=jax.ShapeDtypeStruct((rows * length, columns), jnp.bfloat16),
        in_specs=[
            pl.BlockSpec(memory_space=pltpu.SMEM),
            pl.BlockSpec(memory_space=pl.ANY),
        ],
        out_specs=pl.BlockSpec(memory_space=pltpu.VMEM),
        scratch_shapes=[
            pltpu.VMEM((rows, columns, length * lane_count), jnp.bfloat16),
            pltpu.SemaphoreType.DMA((rows, length)),
        ],
        compiler_params=pltpu.CompilerParams(vmem_limit_bytes=40 * 2**20),
        name="pick_tokens",
    )(ids, table)


def segment_sums(rows, ones):
    count, width = rows.shape[0], ones.shape[0]
    pieces = rows.shape[1] // width
    stacked = jnp.concatenate(
        [rows[:, piece * width : (piece + 1) * width] for piece in range(pieces)], axis=0
    )
    high = stacked.astype(jnp.bfloat16)
    low = (stacked - high.astype(jnp.float32)).astype(jnp.bfloat16)
    sums = jnp.dot(high, ones, preferred_element_type=jnp.float32) + jnp.dot(
        low, ones, preferred_element_type=jnp.float32
    )
    return jnp.concatenate(
        [sums[piece * count : (piece + 1) * count] for piece in range(pieces)], axis=1
    )


def mixing_body(wide, narrow, chunks, local_ref, *refs):
    sources, out_ref, loaded = refs[:18], refs[18], refs[19:37]
    (
        left,
        opening_ref,
        r_ref,
        w_ref,
        right,
        blends_ref,
        fading_left,
        address,
        payload,
        fixed_ref,
        fading_right_ref,
        spans_ref,
        k_ref,
        v_ref,
        g_ref,
        reward_ref,
        scaling_ref,
        offset_ref,
    ) = loaded
    (
        held,
        hidden_parts,
        partial_send,
        partial_recv,
        hidden_all,
        key_sum,
        value_sum,
        decay_sum,
        pairs,
        own_part,
        r_send,
        r_recv,
        y_send,
        y_recv,
        load_sems,
        line_send,
        line_recv,
        cross_send,
        cross_recv,
        r_send_sems,
        r_recv_sems,
        y_send_sems,
        y_recv_sems,
        partial_send_sems,
        partial_recv_sems,
        hidden_send_sems,
        hidden_recv_sems,
    ) = refs[37:]
    w_me = lax.axis_index("wide")
    n_me = lax.axis_index("narrow")
    tokens, columns = local_ref.shape
    bank_rows = spans_ref.shape[1]
    length = tokens // bank_rows
    head = reward_ref.shape[1]
    banks, _, steps, generated = r_ref.shape
    share = wide // narrow
    half_owner = lax.div(w_me, share)
    place_in_half = lax.rem(w_me, share)

    barrier = pltpu.get_barrier_semaphore()
    for other in range(1, wide * narrow):
        flat = lax.rem(w_me * narrow + n_me + other, wide * narrow)
        pl.semaphore_signal(
            barrier,
            inc=1,
            device_id={"wide": lax.div(flat, narrow), "narrow": lax.rem(flat, narrow)},
            device_id_type=pl.DeviceIdType.MESH,
        )

    own_columns = pl.ds(pl.multiple_of(w_me * columns, columns), columns)
    loads = [
        pltpu.make_async_copy(
            source.at[:, own_columns] if number < 2 else source, target, load_sems.at[number]
        )
        for number, (source, target) in enumerate(zip(sources, loaded))
    ]
    first_loads = 4
    for load in loads[:first_loads]:
        load.start()

    held[w_me] = local_ref[...]

    line_me, side = lax.div(w_me, 2), lax.rem(w_me, 2)
    partner = 2 * line_me + 1 - side
    lines = wide // 2
    chunk_rows = tokens // chunks

    def owner_of(offset, own_side):
        return 2 * lax.bitwise_xor(line_me, offset) + (side if own_side else 1 - side)

    def line_copy(offset, chunk, arrival=False):
        piece = held.at[
            owner_of(offset, True) if arrival else w_me, pl.ds(chunk * chunk_rows, chunk_rows)
        ]
        return pltpu.make_async_remote_copy(
            src_ref=piece,
            dst_ref=piece,
            send_sem=line_send.at[offset - 1, chunk],
            recv_sem=line_recv.at[offset - 1, chunk],
            device_id={"wide": owner_of(offset, True)},
            device_id_type=pl.DeviceIdType.MESH,
        )

    def cross_copy(offset, chunk, arrival=False):
        piece = held.at[owner_of(offset, not arrival), pl.ds(chunk * chunk_rows, chunk_rows)]
        return pltpu.make_async_remote_copy(
            src_ref=piece,
            dst_ref=piece,
            send_sem=cross_send.at[offset, chunk],
            recv_sem=cross_recv.at[offset, chunk],
            device_id={"wide": partner},
            device_id_type=pl.DeviceIdType.MESH,
        )

    transposed = (((1,), (1,)), ((), ()))

    def with_difference(block):
        current = block.astype(jnp.float32)
        places = lax.broadcasted_iota(jnp.int32, current.shape, 0) & (length - 1)
        previous = jnp.where(places == 0, 0.0, pltpu.roll(current, 1, 0))
        return current, previous - current

    def partial_copy(offset):
        other = lax.bitwise_xor(w_me, offset)
        return pltpu.make_async_remote_copy(
            src_ref=partial_send.at[other],
            dst_ref=partial_recv.at[w_me],
            send_sem=partial_send_sems.at[offset - 1],
            recv_sem=partial_recv_sems.at[offset - 1],
            device_id={"wide": other},
            device_id_type=pl.DeviceIdType.MESH,
        )

    def partial_arrival(offset):
        other = lax.bitwise_xor(w_me, offset)
        return pltpu.make_async_remote_copy(
            src_ref=partial_send.at[other],
            dst_ref=partial_recv.at[other],
            send_sem=partial_send_sems.at[offset - 1],
            recv_sem=partial_recv_sems.at[offset - 1],
            device_id={"wide": other},
            device_id_type=pl.DeviceIdType.MESH,
        )

    def hidden_copy(offset, arrival=False):
        other = lax.bitwise_xor(w_me, offset)
        piece = hidden_all.at[other if arrival else w_me]
        return pltpu.make_async_remote_copy(
            src_ref=piece,
            dst_ref=piece,
            send_sem=hidden_send_sems.at[offset - 1],
            recv_sem=hidden_recv_sems.at[offset - 1],
            device_id={"wide": other},
            device_id_type=pl.DeviceIdType.MESH,
        )

    def r_copy(bank, part):
        return pltpu.make_async_remote_copy(
            src_ref=r_send.at[bank, part],
            dst_ref=r_recv.at[w_me],
            send_sem=r_send_sems.at[bank, part],
            recv_sem=r_recv_sems.at[w_me],
            device_id={"wide": n_me * share + part, "narrow": bank},
            device_id_type=pl.DeviceIdType.MESH,
        )

    def r_arrival(prompt):
        return pltpu.make_async_remote_copy(
            src_ref=r_send.at[0, 0],
            dst_ref=r_recv.at[prompt],
            send_sem=r_send_sems.at[0, 0],
            recv_sem=r_recv_sems.at[prompt],
            device_id={"wide": prompt, "narrow": half_owner},
            device_id_type=pl.DeviceIdType.MESH,
        )

    def y_copy(prompt):
        return pltpu.make_async_remote_copy(
            src_ref=y_send.at[prompt],
            dst_ref=y_recv.at[n_me, place_in_half],
            send_sem=y_send_sems.at[prompt],
            recv_sem=y_recv_sems.at[n_me, place_in_half],
            device_id={"wide": prompt, "narrow": half_owner},
            device_id_type=pl.DeviceIdType.MESH,
        )

    def y_arrival(bank, part):
        return pltpu.make_async_remote_copy(
            src_ref=y_send.at[0],
            dst_ref=y_recv.at[bank, part],
            send_sem=y_send_sems.at[0],
            recv_sem=y_recv_sems.at[bank, part],
            device_id={"wide": n_me * share + part, "narrow": bank},
            device_id_type=pl.DeviceIdType.MESH,
        )

    def generated_is_mine(bank, part):
        return jnp.logical_and(n_me * share + part == w_me, n_me == bank)

    def prompt_is_mine(prompt):
        return jnp.logical_and(w_me == prompt, n_me == half_owner)

    loads[0].wait()
    loads[1].wait()
    current, difference = with_difference(local_ref[...])
    own_mixed = (current + difference * opening_ref[...]).astype(jnp.bfloat16)
    own_share = lax.dot_general(
        own_mixed, left[...], transposed, preferred_element_type=jnp.float32
    )
    for prompt in range(wide):
        partial_send[prompt] = own_share[prompt * length : (prompt + 1) * length]
    pl.semaphore_wait(barrier, wide * narrow - 1)
    for offset in range(1, wide):
        partial_copy(offset).start()
    for chunk in range(chunks // 2):
        for offset in range(lines - 1, 0, -1):
            line_copy(offset, chunk).start()
        cross_copy(0, chunk).start()

    for load in loads[2:first_loads]:
        load.wait()
    for load in loads[first_loads:]:
        load.start()
    for bank in range(banks):
        r_all = r_ref[bank, 0].astype(jnp.float32)
        w_all = jnp.exp(-jnp.exp(w_ref[bank, 0].astype(jnp.float32)))
        faded = None
        for step in range(steps):
            line = r_all[step : step + 1]
            if step > 0:
                now = w_all[step - 1 : step]
                faded = now if faded is None else faded * now
                line = line * faded
            for part in range(share):
                r_send[bank, part, step : step + 1, :] = line[
                    :, part * columns : (part + 1) * columns
                ]
    for bank in range(banks):
        for part in range(share):

            @pl.when(jnp.logical_not(generated_is_mine(bank, part)))
            def _():
                r_copy(bank, part).start()

    @pl.when(n_me == half_owner)
    def _():
        r_recv[w_me] = r_send[n_me, place_in_half]

    total = partial_send[w_me]
    for offset in range(1, wide):
        partial_arrival(offset).wait_recv()
        total = total + partial_recv[lax.bitwise_xor(w_me, offset)]
    hidden_all[w_me] = jnp.tanh(total).astype(jnp.bfloat16)
    for offset in range(1, wide):
        hidden_copy(offset).start()
    for chunk in range(chunks // 2, chunks):
        for offset in range(lines - 1, 0, -1):
            line_copy(offset, chunk).start()
        cross_copy(0, chunk).start()
    decay_sum[...] = jnp.zeros_like(decay_sum)
    key_sum[...] = jnp.zeros_like(key_sum)
    value_sum[...] = jnp.zeros_like(value_sum)
    for load in loads[first_loads:]:
        load.wait()
    for offset in range(1, wide):
        hidden_copy(offset, True).wait_recv()
    hidden = jnp.concatenate([hidden_all[prompt] for prompt in range(wide)], axis=0).astype(
        jnp.float32
    )
    rank = right.shape[0] // 3
    hidden_lanes = lax.broadcasted_iota(jnp.int32, hidden.shape, 1)
    hidden_parts[...] = jnp.concatenate(
        [
            jnp.where(
                (hidden_lanes >= branch * rank) & (hidden_lanes < (branch + 1) * rank), hidden, 0.0
            )
            for branch in range(3)
        ],
        axis=0,
    ).astype(jnp.bfloat16)

    def project(block):
        span = pl.ds(pl.multiple_of(block * columns, columns), columns)
        current, difference = with_difference(held[block])
        shifts = jnp.dot(hidden_parts[...], right[:, span], preferred_element_type=jnp.float32)
        mixed = [
            (
                current
                + difference
                * (
                    blends_ref[branch : branch + 1, span]
                    + shifts[branch * tokens : (branch + 1) * tokens]
                )
            ).astype(jnp.bfloat16)
            for branch in range(3)
        ]
        decay_sum[...] += jnp.dot(
            mixed[0], fading_left[span, :], preferred_element_type=jnp.float32
        )
        key_sum[...] += lax.dot_general(
            mixed[1], address[:, span], transposed, preferred_element_type=jnp.float32
        )
        value_sum[...] += lax.dot_general(
            mixed[2], payload[:, span], transposed, preferred_element_type=jnp.float32
        )

    def gather_step(offset, carry):
        for chunk in range(chunks):
            line_copy(offset, chunk, True).wait_recv()
            cross_copy(offset, chunk).start()
        project(owner_of(offset - 1, True))
        for chunk in range(chunks):
            cross_copy(offset - 1, chunk, True).wait_recv()
        project(owner_of(offset - 1, False))
        return carry

    lax.fori_loop(1, lines, gather_step, 0)
    project(owner_of(lines - 1, True))
    for chunk in range(chunks):
        cross_copy(lines - 1, chunk, True).wait_recv()
    project(owner_of(lines - 1, False))

    decay_hidden = jnp.tanh(decay_sum[...]).astype(jnp.bfloat16)
    rates = jnp.exp(
        fixed_ref[...]
        + jnp.dot(decay_hidden, fading_right_ref[...], preferred_element_type=jnp.float32)
    )
    row_ids = lax.broadcasted_iota(jnp.int32, (tokens, tokens), 0)
    column_ids = lax.broadcasted_iota(jnp.int32, (tokens, tokens), 1)
    row_limit = jnp.zeros((tokens, 1), jnp.int32)
    column_limit = jnp.zeros((tokens, tokens), jnp.int32)
    row_line = lax.broadcasted_iota(jnp.int32, (tokens, 1), 0)
    for prompt in range(bank_rows):
        span_now = spans_ref[0, prompt]
        row_limit = jnp.where(row_line & -length == prompt * length, span_now, row_limit)
        column_limit = jnp.where(column_ids & -length == prompt * length, span_now, column_limit)
    later = jnp.where(
        (row_ids & -length == column_ids & -length)
        & (column_ids > row_ids)
        & (column_ids & (length - 1) < column_limit),
        1.0,
        0.0,
    ).astype(jnp.bfloat16)
    high = rates.astype(jnp.bfloat16)
    low = (rates - high.astype(jnp.float32)).astype(jnp.bfloat16)
    remaining = jnp.dot(later, high, preferred_element_type=jnp.float32) + jnp.dot(
        later, low, preferred_element_type=jnp.float32
    )
    weights = jnp.where(row_line & (length - 1) < row_limit, jnp.exp(-remaining), 0.0)
    weighted = (
        key_sum[...].astype(jnp.bfloat16).astype(jnp.float32) * weights
    ).astype(jnp.bfloat16)
    values = value_sum[...].astype(jnp.bfloat16)

    for prompt in range(bank_rows):

        @pl.when(jnp.logical_not(prompt_is_mine(prompt)))
        def _():
            r_arrival(prompt).wait_recv()

    asked = jnp.concatenate([r_recv[prompt] for prompt in range(bank_rows)], axis=0)
    asked_rows = bank_rows * steps
    lane_heads = lax.broadcasted_iota(jnp.int32, (asked_rows, columns), 1) & -head
    heads = columns // head
    spread = jnp.concatenate(
        [jnp.where(lane_heads == number * head, asked, 0.0) for number in range(heads)], axis=0
    ).astype(jnp.bfloat16)
    scores = lax.dot_general(spread, weighted, transposed, preferred_element_type=jnp.float32)
    score_rows = lax.broadcasted_iota(jnp.int32, scores.shape, 0) & (asked_rows - 1)
    score_columns = lax.broadcasted_iota(jnp.int32, scores.shape, 1)
    kept = jnp.where(
        lax.shift_right_logical(score_rows, steps.bit_length() - 1)
        == lax.shift_right_logical(score_columns, length.bit_length() - 1),
        scores,
        0.0,
    )
    answers = jnp.dot(kept.astype(jnp.bfloat16), values, preferred_element_type=jnp.float32)
    answer = jnp.zeros((asked_rows, columns), jnp.float32)
    for number in range(heads):
        answer = jnp.where(
            lane_heads == number * head,
            answers[number * asked_rows : (number + 1) * asked_rows],
            answer,
        )
    for prompt in range(bank_rows):
        y_send[prompt] = answer[prompt * steps : (prompt + 1) * steps]
    for prompt in range(bank_rows):

        @pl.when(jnp.logical_not(prompt_is_mine(prompt)))
        def _():
            y_copy(prompt).start()

    @pl.when(n_me == half_owner)
    def _():
        y_recv[n_me, place_in_half] = y_send[w_me]

    ones = jnp.where(
        lax.broadcasted_iota(jnp.int32, (lane_count, lane_count), 0) & -head
        == lax.broadcasted_iota(jnp.int32, (lane_count, lane_count), 1) & -head,
        1.0,
        0.0,
    ).astype(jnp.bfloat16)
    first_head = pl.multiple_of(n_me * (generated // head), generated // head)
    rewards = reward_ref[pl.ds(first_head, generated // head), :]
    reward_line = jnp.concatenate(
        [rewards[number : number + 1, :] for number in range(generated // head)], axis=1
    )
    pair_rows = {}
    for bank in range(banks):
        r_all = r_ref[bank, 0].astype(jnp.float32)
        k_all = k_ref[bank, 0].astype(jnp.float32)
        w_all = jnp.exp(-jnp.exp(w_ref[bank, 0].astype(jnp.float32)))
        for step in range(steps):
            lagged = r_all[step : step + 1]
            for earlier in range(step, -1, -1):
                line = lagged * k_all[earlier : earlier + 1]
                if earlier == step:
                    line = line * reward_line
                elif earlier > 0:
                    lagged = lagged * w_all[earlier : earlier + 1]
                row = len(pair_rows)
                pair_rows[bank, step, earlier] = row
                pairs[row : row + 1, :] = line
    for row in range(len(pair_rows), pairs.shape[0]):
        pairs[row : row + 1, :] = jnp.zeros((1, generated), jnp.float32)
    sums = segment_sums(pairs[...], ones)
    for bank in range(banks):
        v_all = v_ref[bank, 0].astype(jnp.float32)
        for now in range(steps):
            line = None
            for earlier in range(now + 1):
                row = pair_rows[bank, now, earlier]
                term = sums[row : row + 1, :] * v_all[earlier : earlier + 1]
                line = term if line is None else line + term
            own_part[bank * steps + now : bank * steps + now + 1, :] = line
    gate_lines = []
    for bank in range(banks):
        gate = g_ref[bank, 0].astype(jnp.float32)
        gate_lines.append(gate / (1.0 + jnp.exp(-gate)))
    half_columns = pl.ds(pl.multiple_of(n_me * generated, generated), generated)
    gain = scaling_ref[:, half_columns]
    bias = offset_ref[:, half_columns]

    for chunk in range(chunks):
        for offset in range(lines):
            if offset > 0:
                line_copy(offset, chunk).wait_send()
            cross_copy(offset, chunk).wait_send()
    for offset in range(1, wide):
        partial_copy(offset).wait_send()
        hidden_copy(offset).wait_send()
    for bank in range(banks):
        for part in range(share):

            @pl.when(jnp.logical_not(generated_is_mine(bank, part)))
            def _():
                r_copy(bank, part).wait_send()

    for bank in range(banks):
        for part in range(share):

            @pl.when(jnp.logical_not(generated_is_mine(bank, part)))
            def _():
                y_arrival(bank, part).wait_recv()

    received = jnp.concatenate(
        [
            jnp.concatenate([y_recv[bank, part] for part in range(share)], axis=1)
            for bank in range(banks)
        ],
        axis=0,
    )
    y = received + own_part[...]
    centred = y - segment_sums(y, ones) * (1.0 / head)
    variance = segment_sums(centred * centred, ones) * (1.0 / head)
    normed = centred * lax.rsqrt(variance + norm_eps) * gain + bias
    for bank in range(banks):
        out_ref[bank, 0] = (normed[bank * steps : (bank + 1) * steps] * gate_lines[bank]).astype(
            out_ref.dtype
        )
    for prompt in range(bank_rows):

        @pl.when(jnp.logical_not(prompt_is_mine(prompt)))
        def _():
            y_copy(prompt).wait_send()


def mixing(wide, narrow, local, *operands):
    tokens, columns = local.shape
    left, receptance, fading_left, spans = operands[0], operands[2], operands[6], operands[11]
    bank_rows = spans.shape[1]
    banks, _, steps, generated = receptance.shape
    share = wide // narrow
    chunks = bank_rows // 2
    pair_count = -(-(banks * steps * (steps + 1) // 2) // 8) * 8
    vmem = pl.BlockSpec(memory_space=pltpu.VMEM)
    far = pl.BlockSpec(memory_space=pl.ANY)
    f32 = jnp.float32
    dma = pltpu.SemaphoreType.DMA
    return pl.pallas_call(
        functools.partial(mixing_body, wide, narrow, chunks),
        out_shape=jax.ShapeDtypeStruct(receptance.shape, jnp.bfloat16),
        in_specs=[vmem] + [far] * len(operands),
        out_specs=vmem,
        scratch_shapes=[
            pltpu.SMEM(operand.shape, operand.dtype)
            if operand is spans
            else pltpu.VMEM(
                (operand.shape[0], columns) if number < 2 else operand.shape, operand.dtype
            )
            for number, operand in enumerate(operands)
        ]
        + [
            pltpu.VMEM((wide, tokens, columns), jnp.bfloat16),
            pltpu.VMEM((3 * tokens, left.shape[0]), jnp.bfloat16),
            pltpu.VMEM((wide, tokens // wide, left.shape[0]), f32),
            pltpu.VMEM((wide, tokens // wide, left.shape[0]), f32),
            pltpu.VMEM((wide, tokens // wide, left.shape[0]), jnp.bfloat16),
            pltpu.VMEM((tokens, columns), f32),
            pltpu.VMEM((tokens, columns), f32),
            pltpu.VMEM((tokens, fading_left.shape[1]), f32),
            pltpu.VMEM((pair_count, generated), f32),
            pltpu.VMEM((banks * steps, generated), f32),
            pltpu.VMEM((banks, share, steps, columns), f32),
            pltpu.VMEM((bank_rows, steps, columns), f32),
            pltpu.VMEM((bank_rows, steps, columns), f32),
            pltpu.VMEM((banks, share, steps, columns), f32),
            dma((len(operands),)),
            dma((wide // 2 - 1, chunks)),
            dma((wide // 2 - 1, chunks)),
            dma((wide // 2, chunks)),
            dma((wide // 2, chunks)),
            dma((banks, share)),
            dma((bank_rows,)),
            dma((bank_rows,)),
            dma((banks, share)),
            dma((wide - 1,)),
            dma((wide - 1,)),
            dma((wide - 1,)),
            dma((wide - 1,)),
        ],
        compiler_params=pltpu.CompilerParams(
            collective_id=0, has_side_effects=True, vmem_limit_bytes=54 * 2**20
        ),
        name="mix_and_generate",
    )(local, *operands)


def power_of_two(number):
    return number > 0 and number & (number - 1) == 0


def fits_kernels(wide, narrow, ids, table, reward, acceptance):
    bank_rows, length = ids.shape[1], ids.shape[2]
    columns = table.shape[0]
    banks, prompts, steps, generated = acceptance.shape
    return (
        prompts == 1
        and wide % 2 == 0
        and wide > 2
        and wide % narrow == 0
        and banks == narrow
        and bank_rows == wide
        and length % 16 == 0
        and columns % lane_count == 0
        and table.shape[1] % lane_count == 0
        and generated == columns * (wide // narrow)
        and lane_count % reward.shape[1] == 0
        and all(power_of_two(size) for size in (length, steps, bank_rows, reward.shape[1]))
        and columns * length * bank_rows * lane_count * 2 <= 2**25
    )


def per_device(
    context_symbol_ids,
    context_symbol_spans,
    symbol_vector_lookup,
    opening_lagged_blend,
    lagged_blend_weights,
    blending_left_operand,
    blending_right_operands,
    fixed_fading_scores,
    fading_left_operand,
    fading_right_operand,
    address_projector,
    payload_projector,
    present_symbol_reward,
    cluster_scaling_weight,
    cluster_scaling_offset,
    generated_acceptance,
    generated_addresses,
    generated_payloads,
    generated_fading_scores,
    generated_valve_scores,
):
    wide, narrow = lax.axis_size("wide"), lax.axis_size("narrow")
    if fits_kernels(
        wide,
        narrow,
        context_symbol_ids,
        symbol_vector_lookup,
        present_symbol_reward,
        generated_acceptance,
    ):
        return mixing(
            wide,
            narrow,
            gather_tokens(context_symbol_ids, symbol_vector_lookup),
            blending_left_operand.T,
            opening_lagged_blend[None],
            generated_acceptance,
            generated_fading_scores,
            blending_right_operands.reshape(-1, blending_right_operands.shape[2]),
            lagged_blend_weights,
            fading_left_operand,
            address_projector,
            payload_projector,
            fixed_fading_scores[None],
            fading_right_operand,
            context_symbol_spans,
            generated_addresses,
            generated_payloads,
            generated_valve_scores,
            present_symbol_reward,
            cluster_scaling_weight[None],
            cluster_scaling_offset[None],
        )
    bank_rows = context_symbol_ids.shape[1]
    length = context_symbol_ids.shape[2]
    columns = symbol_vector_lookup.shape[0]
    attender_width = present_symbol_reward.shape[1]
    head_local = columns // attender_width
    lengths = context_symbol_spans.reshape(-1)
    picked = jnp.take(symbol_vector_lookup, context_symbol_ids.reshape(-1), axis=1)
    gathered = lax.all_gather(picked, "wide", axis=0, tiled=True).T
    features = gathered.shape[1]
    block_rows = bank_rows
    while block_rows % 2 == 0 and block_rows * length > 1024:
        block_rows = block_rows // 2
    blocks = gathered.reshape(bank_rows // block_rows, block_rows, length, features)
    length_blocks = lengths.reshape(bank_rows // block_rows, block_rows)

    def one_block(block_item):
        key_proj, value_proj, decay_log = mix_project(
            block_item[0],
            opening_lagged_blend,
            lagged_blend_weights,
            blending_left_operand,
            blending_right_operands,
            fixed_fading_scores,
            fading_left_operand,
            fading_right_operand,
            address_projector,
            payload_projector,
        )
        block_shape = (block_rows, length, columns)
        return final_states(
            key_proj.reshape(block_shape),
            value_proj.reshape(block_shape),
            decay_log.reshape(block_shape),
            block_item[1],
            attender_width,
        )

    recurrent_memories = lax.map(one_block, (blocks, length_blocks)).reshape(
        bank_rows, head_local, attender_width, attender_width
    )
    handed = lax.all_to_all(
        lax.all_to_all(
            recurrent_memories.reshape(1, bank_rows, head_local, attender_width * attender_width),
            "wide",
            split_axis=1,
            concat_axis=2,
            tiled=True,
        ),
        "narrow",
        split_axis=2,
        concat_axis=0,
        tiled=True,
    )
    generated_by_attender = handed.shape[2]
    leading_attender_offset = lax.axis_index("narrow") * generated_by_attender
    shard_reward = lax.dynamic_slice_in_dim(
        present_symbol_reward, leading_attender_offset, generated_by_attender, 0
    )
    shard_scaling_weight = lax.dynamic_slice_in_dim(
        cluster_scaling_weight,
        leading_attender_offset * attender_width,
        generated_by_attender * attender_width,
        0,
    )
    shard_scaling_offset = lax.dynamic_slice_in_dim(
        cluster_scaling_offset,
        leading_attender_offset * attender_width,
        generated_by_attender * attender_width,
        0,
    )
    result = generation_iterations(
        handed.reshape(handed.shape[:3] + (attender_width, attender_width)),
        generated_acceptance,
        generated_addresses,
        generated_payloads,
        generated_fading_scores,
        generated_valve_scores,
        shard_reward,
        shard_scaling_weight,
        shard_scaling_offset,
    )
    return result


def solution(mesh):
    placed = (
        P("narrow", "groups", None),
        P("narrow", "groups"),
        P("wide", None),
        P(),
        P(),
        P(),
        P(),
        P("wide"),
        P(),
        P(None, "wide"),
        P("wide", None),
        P("wide", None),
        P(),
        P(),
        P(),
        P(None, ("groups", "wide"), None, "narrow"),
        P(None, ("groups", "wide"), None, "narrow"),
        P(None, ("groups", "wide"), None, "narrow"),
        P(None, ("groups", "wide"), None, "narrow"),
        P(None, ("groups", "wide"), None, "narrow"),
    )
    return jax.shard_map(
        per_device,
        mesh=mesh,
        in_specs=placed,
        out_specs=P(None, ("groups", "wide"), None, "narrow"),
        check_vma=False,
    )
```

```python
import functools

import jax
import jax.numpy as jnp
from jax import lax
from jax.experimental import pallas as pl
from jax.experimental.pallas import tpu as pltpu
from jax.sharding import PartitionSpec as P

norm_eps = 0.00064
lane_count = 128


def mix_project(
    embedded,
    opening_lagged_blend,
    lagged_blend_weights,
    blending_left_operand,
    blending_right_operands,
    fixed_fading_scores,
    fading_left_operand,
    fading_right_operand,
    address_projector,
    payload_projector,
):
    features = embedded.shape[2]
    previous = jnp.pad(embedded, ((0, 0), (1, 0), (0, 0)))[:, :-1, :]
    current = embedded.reshape(-1, features).astype(jnp.float32)
    difference = previous.reshape(-1, features).astype(jnp.float32) - current
    mixed_in = (current + difference * opening_lagged_blend).astype(jnp.bfloat16)
    hidden = jnp.tanh(
        jnp.dot(mixed_in, blending_left_operand, preferred_element_type=jnp.float32)
    ).astype(jnp.bfloat16)
    rank_size = blending_right_operands.shape[1]
    branches = []
    for branch in range(3):
        shift_term = jnp.dot(
            hidden[:, branch * rank_size : (branch + 1) * rank_size],
            blending_right_operands[branch],
            preferred_element_type=jnp.float32,
        )
        branches.append(
            (current + difference * (lagged_blend_weights[branch] + shift_term)).astype(
                jnp.bfloat16
            )
        )
    decay_hidden = jnp.tanh(
        jnp.dot(branches[0], fading_left_operand, preferred_element_type=jnp.float32)
    ).astype(jnp.bfloat16)
    decay_log = fixed_fading_scores + jnp.dot(
        decay_hidden, fading_right_operand, preferred_element_type=jnp.float32
    )
    key_proj = jnp.dot(branches[1], address_projector.T, preferred_element_type=jnp.float32).astype(
        jnp.bfloat16
    )
    value_proj = jnp.dot(
        branches[2], payload_projector.T, preferred_element_type=jnp.float32
    ).astype(jnp.bfloat16)
    return (key_proj, value_proj, decay_log)


def final_states(key_proj, value_proj, decay_log, lengths, attender_width):
    bank_rows, length, columns = key_proj.shape
    attender_ordinal = columns // attender_width
    decay_rates = jnp.exp(decay_log)
    places = lax.broadcasted_iota(jnp.int32, (bank_rows, length), 1)
    live_mask = (places < lengths[:, None])[:, :, None]
    running = jnp.cumsum(jnp.where(live_mask, decay_rates, 0.0), axis=1)
    remaining = running[:, -1:, :] - running
    weights = jnp.where(live_mask, jnp.exp(-remaining), 0.0)
    weighted = (key_proj.astype(jnp.float32) * weights).reshape(
        bank_rows, length, attender_ordinal, attender_width
    )
    plain_values = value_proj.astype(jnp.float32).reshape(
        bank_rows, length, attender_ordinal, attender_width
    )
    return jnp.einsum("rlhi,rlhj->rhij", weighted, plain_values, precision=lax.Precision.HIGHEST)


def generation_iterations(
    recurrent_memories,
    acceptance_lines,
    address_source,
    payload_source,
    fading_source,
    valve_source,
    shard_reward,
    shard_scaling_weight,
    shard_scaling_offset,
):
    attender_ordinal = recurrent_memories.shape[-3]
    attender_width = recurrent_memories.shape[-1]
    leading = acceptance_lines.shape[:-2]
    step_count = acceptance_lines.shape[-2]
    split_shape = leading + (step_count, attender_ordinal, attender_width)
    receptance = acceptance_lines.astype(jnp.float32).reshape(split_shape)
    key_split = address_source.astype(jnp.float32).reshape(split_shape)
    valued = payload_source.astype(jnp.float32).reshape(split_shape)
    factors = jnp.exp(-jnp.exp(fading_source.astype(jnp.float32))).reshape(split_shape)
    results = []
    for position in range(step_count):
        present_acceptance = receptance[..., position, :, :]
        present_address = key_split[..., position, :, :]
        present_payload = valued[..., position, :, :]
        immediate_summand = (
            jnp.sum(present_acceptance * shard_reward * present_address, axis=-1, keepdims=True)
            * present_payload
        )
        carried = jnp.einsum(
            "...hi,...hij->...hj",
            present_acceptance,
            recurrent_memories,
            precision=lax.Precision.HIGHEST,
        )
        results.append(carried + immediate_summand)
        if position + 1 < step_count:
            recurrent_memories = (
                factors[..., position, :, :][..., :, None] * recurrent_memories
                + present_address[..., :, None] * present_payload[..., None, :]
            )
    mixed_out = jnp.stack(results, axis=-3)
    average = jnp.mean(mixed_out, axis=-1, keepdims=True)
    centred = mixed_out - average
    spread = jnp.mean(centred * centred, axis=-1, keepdims=True)
    normed = (centred * lax.rsqrt(spread + norm_eps)).reshape(
        leading + (step_count, attender_ordinal * attender_width)
    )
    return (
        (normed * shard_scaling_weight + shard_scaling_offset)
        * jax.nn.silu(valve_source.astype(jnp.float32))
    ).astype(jnp.bfloat16)


def gather_body(ids_ref, table_ref, out_ref, strips, sems):
    rows, length = ids_ref.shape[1], ids_ref.shape[2]
    lanes = strips.shape[2] // length

    def strip(row, place):
        tile = lax.div(ids_ref[0, row, place], lanes)
        return pltpu.make_async_copy(
            table_ref.at[:, pl.ds(pl.multiple_of(tile * lanes, lanes), lanes)],
            strips.at[row, :, pl.ds(place * lanes, lanes)],
            sems.at[row, place],
        )

    def start(row, carry):
        for place in range(length):
            strip(row, place).start()
        return carry

    lax.fori_loop(0, rows, start, 0)
    places = lax.broadcasted_iota(jnp.int32, (length, lanes), 0)
    columns = lax.broadcasted_iota(jnp.int32, (length, lanes), 1)

    def pick(row, carry):
        wanted = jnp.zeros((length, lanes), jnp.int32)
        for place in range(length):
            wanted = jnp.where(places == place, lax.rem(ids_ref[0, row, place], lanes), wanted)
        hit = jnp.where(columns == wanted, 1.0, 0.0)
        chosen = jnp.concatenate(
            [jnp.where(places == place, hit, 0.0) for place in range(length)], axis=1
        ).astype(jnp.bfloat16)
        for place in range(length):
            strip(row, place).wait()
        found = lax.dot_general(
            chosen, strips[row], (((1,), (1,)), ((), ())), preferred_element_type=jnp.float32
        )
        out_ref[pl.ds(pl.multiple_of(row * length, length), length), :] = found.astype(jnp.bfloat16)
        return carry

    lax.fori_loop(0, rows, pick, 0)


def gather_tokens(ids, table):
    rows, length = ids.shape[1], ids.shape[2]
    columns = table.shape[0]
    return pl.pallas_call(
        gather_body,
        out_shape=jax.ShapeDtypeStruct((rows * length, columns), jnp.bfloat16),
        in_specs=[
            pl.BlockSpec(memory_space=pltpu.SMEM),
            pl.BlockSpec(memory_space=pl.ANY),
        ],
        out_specs=pl.BlockSpec(memory_space=pltpu.VMEM),
        scratch_shapes=[
            pltpu.VMEM((rows, columns, length * lane_count), jnp.bfloat16),
            pltpu.SemaphoreType.DMA((rows, length)),
        ],
        compiler_params=pltpu.CompilerParams(vmem_limit_bytes=40 * 2**20),
        name="pick_tokens",
    )(ids, table)


def segment_sums(rows, ones):
    count, width = rows.shape[0], ones.shape[0]
    pieces = rows.shape[1] // width
    stacked = jnp.concatenate(
        [rows[:, piece * width : (piece + 1) * width] for piece in range(pieces)], axis=0
    )
    high = stacked.astype(jnp.bfloat16)
    low = (stacked - high.astype(jnp.float32)).astype(jnp.bfloat16)
    sums = jnp.dot(high, ones, preferred_element_type=jnp.float32) + jnp.dot(
        low, ones, preferred_element_type=jnp.float32
    )
    return jnp.concatenate(
        [sums[piece * count : (piece + 1) * count] for piece in range(pieces)], axis=1
    )


def mixing_body(wide, narrow, chunks, local_ref, *refs):
    sources, out_ref, loaded = refs[:18], refs[18], refs[19:37]
    (
        left,
        opening_ref,
        r_ref,
        w_ref,
        right,
        blends_ref,
        fading_left,
        address,
        payload,
        fixed_ref,
        fading_right_ref,
        spans_ref,
        k_ref,
        v_ref,
        g_ref,
        reward_ref,
        scaling_ref,
        offset_ref,
    ) = loaded
    (
        held,
        hidden_parts,
        hidden_sum,
        key_sum,
        value_sum,
        decay_sum,
        pairs,
        own_part,
        r_send,
        r_recv,
        y_send,
        y_recv,
        load_sems,
        line_send,
        line_recv,
        cross_send,
        cross_recv,
        r_send_sems,
        r_recv_sems,
        y_send_sems,
        y_recv_sems,
    ) = refs[37:]
    w_me = lax.axis_index("wide")
    n_me = lax.axis_index("narrow")
    tokens, columns = local_ref.shape
    bank_rows = spans_ref.shape[1]
    length = tokens // bank_rows
    head = reward_ref.shape[1]
    banks, _, steps, generated = r_ref.shape
    share = wide // narrow
    half_owner = lax.div(w_me, share)
    place_in_half = lax.rem(w_me, share)

    barrier = pltpu.get_barrier_semaphore()
    for other in range(1, wide * narrow):
        flat = lax.rem(w_me * narrow + n_me + other, wide * narrow)
        pl.semaphore_signal(
            barrier,
            inc=1,
            device_id={"wide": lax.div(flat, narrow), "narrow": lax.rem(flat, narrow)},
            device_id_type=pl.DeviceIdType.MESH,
        )

    loads = [
        pltpu.make_async_copy(source, target, load_sems.at[number])
        for number, (source, target) in enumerate(zip(sources, loaded))
    ]
    first_loads = 4
    for load in loads[:first_loads]:
        load.start()

    held[w_me] = local_ref[...]

    line_me, side = lax.div(w_me, 2), lax.rem(w_me, 2)
    partner = 2 * line_me + 1 - side
    lines = wide // 2
    chunk_rows = tokens // chunks

    def owner_of(offset, own_side):
        return 2 * lax.bitwise_xor(line_me, offset) + (side if own_side else 1 - side)

    def line_copy(offset, chunk, arrival=False):
        piece = held.at[
            owner_of(offset, True) if arrival else w_me, pl.ds(chunk * chunk_rows, chunk_rows)
        ]
        return pltpu.make_async_remote_copy(
            src_ref=piece,
            dst_ref=piece,
            send_sem=line_send.at[offset - 1, chunk],
            recv_sem=line_recv.at[offset - 1, chunk],
            device_id={"wide": owner_of(offset, True)},
            device_id_type=pl.DeviceIdType.MESH,
        )

    def cross_copy(offset, chunk, arrival=False):
        piece = held.at[owner_of(offset, not arrival), pl.ds(chunk * chunk_rows, chunk_rows)]
        return pltpu.make_async_remote_copy(
            src_ref=piece,
            dst_ref=piece,
            send_sem=cross_send.at[offset, chunk],
            recv_sem=cross_recv.at[offset, chunk],
            device_id={"wide": partner},
            device_id_type=pl.DeviceIdType.MESH,
        )

    transposed = (((1,), (1,)), ((), ()))

    def with_difference(block):
        current = block.astype(jnp.float32)
        places = lax.broadcasted_iota(jnp.int32, current.shape, 0) & (length - 1)
        previous = jnp.where(places == 0, 0.0, pltpu.roll(current, 1, 0))
        return current, previous - current

    def add_hidden(owner):
        feature_rows = pl.ds(pl.multiple_of(owner * columns, columns), columns)
        current, difference = with_difference(held[owner])
        mixed = (current + difference * opening_ref[:, feature_rows]).astype(jnp.bfloat16)
        hidden_sum[...] += lax.dot_general(
            mixed, left[:, feature_rows], transposed, preferred_element_type=jnp.float32
        )

    def r_copy(bank, part):
        return pltpu.make_async_remote_copy(
            src_ref=r_send.at[bank, part],
            dst_ref=r_recv.at[w_me],
            send_sem=r_send_sems.at[bank, part],
            recv_sem=r_recv_sems.at[w_me],
            device_id={"wide": n_me * share + part, "narrow": bank},
            device_id_type=pl.DeviceIdType.MESH,
        )

    def r_arrival(prompt):
        return pltpu.make_async_remote_copy(
            src_ref=r_send.at[0, 0],
            dst_ref=r_recv.at[prompt],
            send_sem=r_send_sems.at[0, 0],
            recv_sem=r_recv_sems.at[prompt],
            device_id={"wide": prompt, "narrow": half_owner},
            device_id_type=pl.DeviceIdType.MESH,
        )

    def y_copy(prompt):
        return pltpu.make_async_remote_copy(
            src_ref=y_send.at[prompt],
            dst_ref=y_recv.at[n_me, place_in_half],
            send_sem=y_send_sems.at[prompt],
            recv_sem=y_recv_sems.at[n_me, place_in_half],
            device_id={"wide": prompt, "narrow": half_owner},
            device_id_type=pl.DeviceIdType.MESH,
        )

    def y_arrival(bank, part):
        return pltpu.make_async_remote_copy(
            src_ref=y_send.at[0],
            dst_ref=y_recv.at[bank, part],
            send_sem=y_send_sems.at[0],
            recv_sem=y_recv_sems.at[bank, part],
            device_id={"wide": n_me * share + part, "narrow": bank},
            device_id_type=pl.DeviceIdType.MESH,
        )

    def generated_is_mine(bank, part):
        return jnp.logical_and(n_me * share + part == w_me, n_me == bank)

    def prompt_is_mine(prompt):
        return jnp.logical_and(w_me == prompt, n_me == half_owner)

    pl.semaphore_wait(barrier, wide * narrow - 1)
    for chunk in range(chunks):
        cross_copy(0, chunk).start()
        for offset in range(1, lines):
            line_copy(offset, chunk).start()

    for load in loads[2:first_loads]:
        load.wait()
    hidden_sum[...] = jnp.zeros_like(hidden_sum)
    decay_sum[...] = jnp.zeros_like(decay_sum)
    key_sum[...] = jnp.zeros_like(key_sum)
    value_sum[...] = jnp.zeros_like(value_sum)
    for bank in range(banks):
        r_all = r_ref[bank, 0].astype(jnp.float32)
        w_all = jnp.exp(-jnp.exp(w_ref[bank, 0].astype(jnp.float32)))
        faded = None
        for step in range(steps):
            line = r_all[step : step + 1]
            if step > 0:
                now = w_all[step - 1 : step]
                faded = now if faded is None else faded * now
                line = line * faded
            for part in range(share):
                r_send[bank, part, step : step + 1, :] = line[
                    :, part * columns : (part + 1) * columns
                ]
    for bank in range(banks):
        for part in range(share):

            @pl.when(jnp.logical_not(generated_is_mine(bank, part)))
            def _():
                r_copy(bank, part).start()

    @pl.when(n_me == half_owner)
    def _():
        r_recv[w_me] = r_send[n_me, place_in_half]

    for load in loads[first_loads:]:
        load.start()
    for load in loads[:2]:
        load.wait()
    add_hidden(w_me)

    def gather_step(offset, carry):
        for chunk in range(chunks):
            line_copy(offset, chunk, True).wait_recv()
            cross_copy(offset, chunk).start()
        add_hidden(owner_of(offset, True))
        for chunk in range(chunks):
            cross_copy(offset - 1, chunk, True).wait_recv()
        add_hidden(owner_of(offset - 1, False))
        return carry

    lax.fori_loop(1, lines, gather_step, 0)
    for load in loads[first_loads:]:
        load.wait()
    for chunk in range(chunks):
        cross_copy(lines - 1, chunk, True).wait_recv()
    add_hidden(owner_of(lines - 1, False))

    hidden = jnp.tanh(hidden_sum[...])
    rank = right.shape[0] // 3
    hidden_lanes = lax.broadcasted_iota(jnp.int32, hidden.shape, 1)
    hidden_parts[...] = jnp.concatenate(
        [
            jnp.where(
                (hidden_lanes >= branch * rank) & (hidden_lanes < (branch + 1) * rank), hidden, 0.0
            )
            for branch in range(3)
        ],
        axis=0,
    ).astype(jnp.bfloat16)

    def project(pair, carry):
        span = pl.ds(pl.multiple_of(pair * 2 * columns, 2 * columns), 2 * columns)
        mixed = [[], [], []]
        for member in range(2):
            block = pair * 2 + member
            part = pl.ds(pl.multiple_of(block * columns, columns), columns)
            current, difference = with_difference(held[block])
            shifts = jnp.dot(
                hidden_parts[...], right[:, part], preferred_element_type=jnp.float32
            )
            for branch in range(3):
                blend = (
                    blends_ref[branch : branch + 1, part]
                    + shifts[branch * tokens : (branch + 1) * tokens]
                )
                mixed[branch].append((current + difference * blend).astype(jnp.bfloat16))
        decayed, keyed, valued = (jnp.concatenate(parts, axis=1) for parts in mixed)
        decay_sum[...] += jnp.dot(
            decayed, fading_left[span, :], preferred_element_type=jnp.float32
        )
        key_sum[...] += lax.dot_general(
            keyed, address[:, span], transposed, preferred_element_type=jnp.float32
        )
        value_sum[...] += lax.dot_general(
            valued, payload[:, span], transposed, preferred_element_type=jnp.float32
        )
        return carry

    lax.fori_loop(0, lines, project, 0)

    decay_hidden = jnp.tanh(decay_sum[...]).astype(jnp.bfloat16)
    rates = jnp.exp(
        fixed_ref[...]
        + jnp.dot(decay_hidden, fading_right_ref[...], preferred_element_type=jnp.float32)
    )
    row_ids = lax.broadcasted_iota(jnp.int32, (tokens, tokens), 0)
    column_ids = lax.broadcasted_iota(jnp.int32, (tokens, tokens), 1)
    row_limit = jnp.zeros((tokens, 1), jnp.int32)
    column_limit = jnp.zeros((tokens, tokens), jnp.int32)
    row_line = lax.broadcasted_iota(jnp.int32, (tokens, 1), 0)
    for prompt in range(bank_rows):
        span_now = spans_ref[0, prompt]
        row_limit = jnp.where(row_line & -length == prompt * length, span_now, row_limit)
        column_limit = jnp.where(column_ids & -length == prompt * length, span_now, column_limit)
    later = jnp.where(
        (row_ids & -length == column_ids & -length)
        & (column_ids > row_ids)
        & (column_ids & (length - 1) < column_limit),
        1.0,
        0.0,
    ).astype(jnp.bfloat16)
    high = rates.astype(jnp.bfloat16)
    low = (rates - high.astype(jnp.float32)).astype(jnp.bfloat16)
    remaining = jnp.dot(later, high, preferred_element_type=jnp.float32) + jnp.dot(
        later, low, preferred_element_type=jnp.float32
    )
    weights = jnp.where(row_line & (length - 1) < row_limit, jnp.exp(-remaining), 0.0)
    weighted = (
        key_sum[...].astype(jnp.bfloat16).astype(jnp.float32) * weights
    ).astype(jnp.bfloat16)
    values = value_sum[...].astype(jnp.bfloat16)

    for prompt in range(bank_rows):

        @pl.when(jnp.logical_not(prompt_is_mine(prompt)))
        def _():
            r_arrival(prompt).wait_recv()

    asked = jnp.concatenate([r_recv[prompt] for prompt in range(bank_rows)], axis=0)
    asked_rows = bank_rows * steps
    lane_heads = lax.broadcasted_iota(jnp.int32, (asked_rows, columns), 1) & -head
    heads = columns // head
    spread = jnp.concatenate(
        [jnp.where(lane_heads == number * head, asked, 0.0) for number in range(heads)], axis=0
    ).astype(jnp.bfloat16)
    scores = lax.dot_general(spread, weighted, transposed, preferred_element_type=jnp.float32)
    score_rows = lax.broadcasted_iota(jnp.int32, scores.shape, 0) & (asked_rows - 1)
    score_columns = lax.broadcasted_iota(jnp.int32, scores.shape, 1)
    kept = jnp.where(
        lax.shift_right_logical(score_rows, steps.bit_length() - 1)
        == lax.shift_right_logical(score_columns, length.bit_length() - 1),
        scores,
        0.0,
    )
    answers = jnp.dot(kept.astype(jnp.bfloat16), values, preferred_element_type=jnp.float32)
    answer = jnp.zeros((asked_rows, columns), jnp.float32)
    for number in range(heads):
        answer = jnp.where(
            lane_heads == number * head,
            answers[number * asked_rows : (number + 1) * asked_rows],
            answer,
        )
    for prompt in range(bank_rows):
        y_send[prompt] = answer[prompt * steps : (prompt + 1) * steps]
    for prompt in range(bank_rows):

        @pl.when(jnp.logical_not(prompt_is_mine(prompt)))
        def _():
            y_copy(prompt).start()

    @pl.when(n_me == half_owner)
    def _():
        y_recv[n_me, place_in_half] = y_send[w_me]

    ones = jnp.where(
        lax.broadcasted_iota(jnp.int32, (lane_count, lane_count), 0) & -head
        == lax.broadcasted_iota(jnp.int32, (lane_count, lane_count), 1) & -head,
        1.0,
        0.0,
    ).astype(jnp.bfloat16)
    first_head = pl.multiple_of(n_me * (generated // head), generated // head)
    rewards = reward_ref[pl.ds(first_head, generated // head), :]
    reward_line = jnp.concatenate(
        [rewards[number : number + 1, :] for number in range(generated // head)], axis=1
    )
    pair_rows = {}
    for bank in range(banks):
        r_all = r_ref[bank, 0].astype(jnp.float32)
        k_all = k_ref[bank, 0].astype(jnp.float32)
        w_all = jnp.exp(-jnp.exp(w_ref[bank, 0].astype(jnp.float32)))
        for step in range(steps):
            lagged = r_all[step : step + 1]
            for earlier in range(step, -1, -1):
                line = lagged * k_all[earlier : earlier + 1]
                if earlier == step:
                    line = line * reward_line
                elif earlier > 0:
                    lagged = lagged * w_all[earlier : earlier + 1]
                row = len(pair_rows)
                pair_rows[bank, step, earlier] = row
                pairs[row : row + 1, :] = line
    for row in range(len(pair_rows), pairs.shape[0]):
        pairs[row : row + 1, :] = jnp.zeros((1, generated), jnp.float32)
    sums = segment_sums(pairs[...], ones)
    for bank in range(banks):
        v_all = v_ref[bank, 0].astype(jnp.float32)
        for now in range(steps):
            line = None
            for earlier in range(now + 1):
                row = pair_rows[bank, now, earlier]
                term = sums[row : row + 1, :] * v_all[earlier : earlier + 1]
                line = term if line is None else line + term
            own_part[bank * steps + now : bank * steps + now + 1, :] = line
    gate_lines = []
    for bank in range(banks):
        gate = g_ref[bank, 0].astype(jnp.float32)
        gate_lines.append(gate / (1.0 + jnp.exp(-gate)))
    half_columns = pl.ds(pl.multiple_of(n_me * generated, generated), generated)
    gain = scaling_ref[:, half_columns]
    bias = offset_ref[:, half_columns]

    for chunk in range(chunks):
        for offset in range(lines):
            if offset > 0:
                line_copy(offset, chunk).wait_send()
            cross_copy(offset, chunk).wait_send()
    for bank in range(banks):
        for part in range(share):

            @pl.when(jnp.logical_not(generated_is_mine(bank, part)))
            def _():
                r_copy(bank, part).wait_send()

    for bank in range(banks):
        for part in range(share):

            @pl.when(jnp.logical_not(generated_is_mine(bank, part)))
            def _():
                y_arrival(bank, part).wait_recv()

    received = jnp.concatenate(
        [
            jnp.concatenate([y_recv[bank, part] for part in range(share)], axis=1)
            for bank in range(banks)
        ],
        axis=0,
    )
    y = received + own_part[...]
    centred = y - segment_sums(y, ones) * (1.0 / head)
    variance = segment_sums(centred * centred, ones) * (1.0 / head)
    normed = centred * lax.rsqrt(variance + norm_eps) * gain + bias
    for bank in range(banks):
        out_ref[bank, 0] = (normed[bank * steps : (bank + 1) * steps] * gate_lines[bank]).astype(
            out_ref.dtype
        )
    for prompt in range(bank_rows):

        @pl.when(jnp.logical_not(prompt_is_mine(prompt)))
        def _():
            y_copy(prompt).wait_send()


def mixing(wide, narrow, local, *operands):
    tokens, columns = local.shape
    left, receptance, fading_left, spans = operands[0], operands[2], operands[6], operands[11]
    bank_rows = spans.shape[1]
    banks, _, steps, generated = receptance.shape
    share = wide // narrow
    chunks = bank_rows // 2
    pair_count = -(-(banks * steps * (steps + 1) // 2) // 8) * 8
    vmem = pl.BlockSpec(memory_space=pltpu.VMEM)
    far = pl.BlockSpec(memory_space=pl.ANY)
    f32 = jnp.float32
    dma = pltpu.SemaphoreType.DMA
    return pl.pallas_call(
        functools.partial(mixing_body, wide, narrow, chunks),
        out_shape=jax.ShapeDtypeStruct(receptance.shape, jnp.bfloat16),
        in_specs=[vmem] + [far] * len(operands),
        out_specs=vmem,
        scratch_shapes=[
            pltpu.SMEM(operand.shape, operand.dtype)
            if operand is spans
            else pltpu.VMEM(operand.shape, operand.dtype)
            for operand in operands
        ]
        + [
            pltpu.VMEM((wide, tokens, columns), jnp.bfloat16),
            pltpu.VMEM((3 * tokens, left.shape[0]), jnp.bfloat16),
            pltpu.VMEM((tokens, left.shape[0]), f32),
            pltpu.VMEM((tokens, columns), f32),
            pltpu.VMEM((tokens, columns), f32),
            pltpu.VMEM((tokens, fading_left.shape[1]), f32),
            pltpu.VMEM((pair_count, generated), f32),
            pltpu.VMEM((banks * steps, generated), f32),
            pltpu.VMEM((banks, share, steps, columns), f32),
            pltpu.VMEM((bank_rows, steps, columns), f32),
            pltpu.VMEM((bank_rows, steps, columns), f32),
            pltpu.VMEM((banks, share, steps, columns), f32),
            dma((len(operands),)),
            dma((wide // 2 - 1, chunks)),
            dma((wide // 2 - 1, chunks)),
            dma((wide // 2, chunks)),
            dma((wide // 2, chunks)),
            dma((banks, share)),
            dma((bank_rows,)),
            dma((bank_rows,)),
            dma((banks, share)),
        ],
        compiler_params=pltpu.CompilerParams(
            collective_id=0, has_side_effects=True, vmem_limit_bytes=54 * 2**20
        ),
        name="mix_and_generate",
    )(local, *operands)


def power_of_two(number):
    return number > 0 and number & (number - 1) == 0


def fits_kernels(wide, narrow, ids, table, reward, acceptance):
    bank_rows, length = ids.shape[1], ids.shape[2]
    columns = table.shape[0]
    banks, prompts, steps, generated = acceptance.shape
    return (
        prompts == 1
        and wide % 2 == 0
        and wide > 2
        and wide % narrow == 0
        and banks == narrow
        and bank_rows == wide
        and length % 16 == 0
        and columns % lane_count == 0
        and table.shape[1] % lane_count == 0
        and generated == columns * (wide // narrow)
        and lane_count % reward.shape[1] == 0
        and all(power_of_two(size) for size in (length, steps, bank_rows, reward.shape[1]))
        and columns * length * bank_rows * lane_count * 2 <= 2**25
    )


def per_device(
    context_symbol_ids,
    context_symbol_spans,
    symbol_vector_lookup,
    opening_lagged_blend,
    lagged_blend_weights,
    blending_left_operand,
    blending_right_operands,
    fixed_fading_scores,
    fading_left_operand,
    fading_right_operand,
    address_projector,
    payload_projector,
    present_symbol_reward,
    cluster_scaling_weight,
    cluster_scaling_offset,
    generated_acceptance,
    generated_addresses,
    generated_payloads,
    generated_fading_scores,
    generated_valve_scores,
):
    wide, narrow = lax.axis_size("wide"), lax.axis_size("narrow")
    if fits_kernels(
        wide,
        narrow,
        context_symbol_ids,
        symbol_vector_lookup,
        present_symbol_reward,
        generated_acceptance,
    ):
        return mixing(
            wide,
            narrow,
            gather_tokens(context_symbol_ids, symbol_vector_lookup),
            blending_left_operand.T,
            opening_lagged_blend[None],
            generated_acceptance,
            generated_fading_scores,
            blending_right_operands.reshape(-1, blending_right_operands.shape[2]),
            lagged_blend_weights,
            fading_left_operand,
            address_projector,
            payload_projector,
            fixed_fading_scores[None],
            fading_right_operand,
            context_symbol_spans,
            generated_addresses,
            generated_payloads,
            generated_valve_scores,
            present_symbol_reward,
            cluster_scaling_weight[None],
            cluster_scaling_offset[None],
        )
    bank_rows = context_symbol_ids.shape[1]
    length = context_symbol_ids.shape[2]
    columns = symbol_vector_lookup.shape[0]
    attender_width = present_symbol_reward.shape[1]
    head_local = columns // attender_width
    lengths = context_symbol_spans.reshape(-1)
    picked = jnp.take(symbol_vector_lookup, context_symbol_ids.reshape(-1), axis=1)
    gathered = lax.all_gather(picked, "wide", axis=0, tiled=True).T
    features = gathered.shape[1]
    block_rows = bank_rows
    while block_rows % 2 == 0 and block_rows * length > 1024:
        block_rows = block_rows // 2
    blocks = gathered.reshape(bank_rows // block_rows, block_rows, length, features)
    length_blocks = lengths.reshape(bank_rows // block_rows, block_rows)

    def one_block(block_item):
        key_proj, value_proj, decay_log = mix_project(
            block_item[0],
            opening_lagged_blend,
            lagged_blend_weights,
            blending_left_operand,
            blending_right_operands,
            fixed_fading_scores,
            fading_left_operand,
            fading_right_operand,
            address_projector,
            payload_projector,
        )
        block_shape = (block_rows, length, columns)
        return final_states(
            key_proj.reshape(block_shape),
            value_proj.reshape(block_shape),
            decay_log.reshape(block_shape),
            block_item[1],
            attender_width,
        )

    recurrent_memories = lax.map(one_block, (blocks, length_blocks)).reshape(
        bank_rows, head_local, attender_width, attender_width
    )
    handed = lax.all_to_all(
        lax.all_to_all(
            recurrent_memories.reshape(1, bank_rows, head_local, attender_width * attender_width),
            "wide",
            split_axis=1,
            concat_axis=2,
            tiled=True,
        ),
        "narrow",
        split_axis=2,
        concat_axis=0,
        tiled=True,
    )
    generated_by_attender = handed.shape[2]
    leading_attender_offset = lax.axis_index("narrow") * generated_by_attender
    shard_reward = lax.dynamic_slice_in_dim(
        present_symbol_reward, leading_attender_offset, generated_by_attender, 0
    )
    shard_scaling_weight = lax.dynamic_slice_in_dim(
        cluster_scaling_weight,
        leading_attender_offset * attender_width,
        generated_by_attender * attender_width,
        0,
    )
    shard_scaling_offset = lax.dynamic_slice_in_dim(
        cluster_scaling_offset,
        leading_attender_offset * attender_width,
        generated_by_attender * attender_width,
        0,
    )
    result = generation_iterations(
        handed.reshape(handed.shape[:3] + (attender_width, attender_width)),
        generated_acceptance,
        generated_addresses,
        generated_payloads,
        generated_fading_scores,
        generated_valve_scores,
        shard_reward,
        shard_scaling_weight,
        shard_scaling_offset,
    )
    return result


def solution(mesh):
    placed = (
        P("narrow", "groups", None),
        P("narrow", "groups"),
        P("wide", None),
        P(),
        P(),
        P(),
        P(),
        P("wide"),
        P(),
        P(None, "wide"),
        P("wide", None),
        P("wide", None),
        P(),
        P(),
        P(),
        P(None, ("groups", "wide"), None, "narrow"),
        P(None, ("groups", "wide"), None, "narrow"),
        P(None, ("groups", "wide"), None, "narrow"),
        P(None, ("groups", "wide"), None, "narrow"),
        P(None, ("groups", "wide"), None, "narrow"),
    )
    return jax.shard_map(
        per_device,
        mesh=mesh,
        in_specs=placed,
        out_specs=P(None, ("groups", "wide"), None, "narrow"),
        check_vma=False,
    )
```

```python
import functools

import jax
import jax.numpy as jnp
from jax import lax
from jax.experimental import pallas as pl
from jax.experimental.pallas import tpu as pltpu
from jax.sharding import PartitionSpec as P

norm_eps = 0.00064
lane_count = 128


def mix_project(
    embedded,
    opening_lagged_blend,
    lagged_blend_weights,
    blending_left_operand,
    blending_right_operands,
    fixed_fading_scores,
    fading_left_operand,
    fading_right_operand,
    address_projector,
    payload_projector,
):
    features = embedded.shape[2]
    previous = jnp.pad(embedded, ((0, 0), (1, 0), (0, 0)))[:, :-1, :]
    current = embedded.reshape(-1, features).astype(jnp.float32)
    difference = previous.reshape(-1, features).astype(jnp.float32) - current
    mixed_in = (current + difference * opening_lagged_blend).astype(jnp.bfloat16)
    hidden = jnp.tanh(
        jnp.dot(mixed_in, blending_left_operand, preferred_element_type=jnp.float32)
    ).astype(jnp.bfloat16)
    rank_size = blending_right_operands.shape[1]
    branches = []
    for branch in range(3):
        shift_term = jnp.dot(
            hidden[:, branch * rank_size : (branch + 1) * rank_size],
            blending_right_operands[branch],
            preferred_element_type=jnp.float32,
        )
        branches.append(
            (current + difference * (lagged_blend_weights[branch] + shift_term)).astype(
                jnp.bfloat16
            )
        )
    decay_hidden = jnp.tanh(
        jnp.dot(branches[0], fading_left_operand, preferred_element_type=jnp.float32)
    ).astype(jnp.bfloat16)
    decay_log = fixed_fading_scores + jnp.dot(
        decay_hidden, fading_right_operand, preferred_element_type=jnp.float32
    )
    key_proj = jnp.dot(branches[1], address_projector.T, preferred_element_type=jnp.float32).astype(
        jnp.bfloat16
    )
    value_proj = jnp.dot(
        branches[2], payload_projector.T, preferred_element_type=jnp.float32
    ).astype(jnp.bfloat16)
    return (key_proj, value_proj, decay_log)


def final_states(key_proj, value_proj, decay_log, lengths, attender_width):
    bank_rows, length, columns = key_proj.shape
    attender_ordinal = columns // attender_width
    decay_rates = jnp.exp(decay_log)
    places = lax.broadcasted_iota(jnp.int32, (bank_rows, length), 1)
    live_mask = (places < lengths[:, None])[:, :, None]
    running = jnp.cumsum(jnp.where(live_mask, decay_rates, 0.0), axis=1)
    remaining = running[:, -1:, :] - running
    weights = jnp.where(live_mask, jnp.exp(-remaining), 0.0)
    weighted = (key_proj.astype(jnp.float32) * weights).reshape(
        bank_rows, length, attender_ordinal, attender_width
    )
    plain_values = value_proj.astype(jnp.float32).reshape(
        bank_rows, length, attender_ordinal, attender_width
    )
    return jnp.einsum("rlhi,rlhj->rhij", weighted, plain_values, precision=lax.Precision.HIGHEST)


def generation_iterations(
    recurrent_memories,
    acceptance_lines,
    address_source,
    payload_source,
    fading_source,
    valve_source,
    shard_reward,
    shard_scaling_weight,
    shard_scaling_offset,
):
    attender_ordinal = recurrent_memories.shape[-3]
    attender_width = recurrent_memories.shape[-1]
    leading = acceptance_lines.shape[:-2]
    step_count = acceptance_lines.shape[-2]
    split_shape = leading + (step_count, attender_ordinal, attender_width)
    receptance = acceptance_lines.astype(jnp.float32).reshape(split_shape)
    key_split = address_source.astype(jnp.float32).reshape(split_shape)
    valued = payload_source.astype(jnp.float32).reshape(split_shape)
    factors = jnp.exp(-jnp.exp(fading_source.astype(jnp.float32))).reshape(split_shape)
    results = []
    for position in range(step_count):
        present_acceptance = receptance[..., position, :, :]
        present_address = key_split[..., position, :, :]
        present_payload = valued[..., position, :, :]
        immediate_summand = (
            jnp.sum(present_acceptance * shard_reward * present_address, axis=-1, keepdims=True)
            * present_payload
        )
        carried = jnp.einsum(
            "...hi,...hij->...hj",
            present_acceptance,
            recurrent_memories,
            precision=lax.Precision.HIGHEST,
        )
        results.append(carried + immediate_summand)
        if position + 1 < step_count:
            recurrent_memories = (
                factors[..., position, :, :][..., :, None] * recurrent_memories
                + present_address[..., :, None] * present_payload[..., None, :]
            )
    mixed_out = jnp.stack(results, axis=-3)
    average = jnp.mean(mixed_out, axis=-1, keepdims=True)
    centred = mixed_out - average
    spread = jnp.mean(centred * centred, axis=-1, keepdims=True)
    normed = (centred * lax.rsqrt(spread + norm_eps)).reshape(
        leading + (step_count, attender_ordinal * attender_width)
    )
    return (
        (normed * shard_scaling_weight + shard_scaling_offset)
        * jax.nn.silu(valve_source.astype(jnp.float32))
    ).astype(jnp.bfloat16)


def gather_body(ids_ref, table_ref, out_ref, strips, sems):
    rows, length = ids_ref.shape[1], ids_ref.shape[2]
    lanes = strips.shape[2] // length

    def strip(row, place):
        tile = lax.div(ids_ref[0, row, place], lanes)
        return pltpu.make_async_copy(
            table_ref.at[:, pl.ds(pl.multiple_of(tile * lanes, lanes), lanes)],
            strips.at[row, :, pl.ds(place * lanes, lanes)],
            sems.at[row, place],
        )

    def start(row, carry):
        for place in range(length):
            strip(row, place).start()
        return carry

    lax.fori_loop(0, rows, start, 0)
    places = lax.broadcasted_iota(jnp.int32, (length, lanes), 0)
    columns = lax.broadcasted_iota(jnp.int32, (length, lanes), 1)

    def pick(row, carry):
        wanted = jnp.zeros((length, lanes), jnp.int32)
        for place in range(length):
            wanted = jnp.where(places == place, lax.rem(ids_ref[0, row, place], lanes), wanted)
        hit = jnp.where(columns == wanted, 1.0, 0.0)
        chosen = jnp.concatenate(
            [jnp.where(places == place, hit, 0.0) for place in range(length)], axis=1
        ).astype(jnp.bfloat16)
        for place in range(length):
            strip(row, place).wait()
        found = lax.dot_general(
            chosen, strips[row], (((1,), (1,)), ((), ())), preferred_element_type=jnp.float32
        )
        out_ref[pl.ds(pl.multiple_of(row * length, length), length), :] = found.astype(jnp.bfloat16)
        return carry

    lax.fori_loop(0, rows, pick, 0)


def gather_tokens(ids, table):
    rows, length = ids.shape[1], ids.shape[2]
    columns = table.shape[0]
    return pl.pallas_call(
        gather_body,
        out_shape=jax.ShapeDtypeStruct((rows * length, columns), jnp.bfloat16),
        in_specs=[
            pl.BlockSpec(memory_space=pltpu.SMEM),
            pl.BlockSpec(memory_space=pl.ANY),
        ],
        out_specs=pl.BlockSpec(memory_space=pltpu.VMEM),
        scratch_shapes=[
            pltpu.VMEM((rows, columns, length * lane_count), jnp.bfloat16),
            pltpu.SemaphoreType.DMA((rows, length)),
        ],
        compiler_params=pltpu.CompilerParams(vmem_limit_bytes=24 * 2**20),
        name="pick_tokens",
    )(ids, table)


def segment_sums(rows, ones):
    count, width = rows.shape[0], ones.shape[0]
    pieces = rows.shape[1] // width
    stacked = jnp.concatenate(
        [rows[:, piece * width : (piece + 1) * width] for piece in range(pieces)], axis=0
    )
    high = stacked.astype(jnp.bfloat16)
    low = (stacked - high.astype(jnp.float32)).astype(jnp.bfloat16)
    sums = jnp.dot(high, ones, preferred_element_type=jnp.float32) + jnp.dot(
        low, ones, preferred_element_type=jnp.float32
    )
    return jnp.concatenate(
        [sums[piece * count : (piece + 1) * count] for piece in range(pieces)], axis=1
    )


def mixing_body(wide, narrow, chunks, local_ref, *refs):
    sources, out_ref, loaded = refs[:18], refs[18], refs[19:37]
    (
        left,
        opening_ref,
        r_ref,
        w_ref,
        right,
        blends_ref,
        fading_left,
        address,
        payload,
        fixed_ref,
        fading_right_ref,
        spans_ref,
        k_ref,
        v_ref,
        g_ref,
        reward_ref,
        scaling_ref,
        offset_ref,
    ) = loaded
    (
        held,
        hidden_parts,
        hidden_sum,
        key_sum,
        value_sum,
        decay_sum,
        pairs,
        own_part,
        r_send,
        r_recv,
        y_send,
        y_recv,
        load_sems,
        line_send,
        line_recv,
        cross_send,
        cross_recv,
        r_send_sems,
        r_recv_sems,
        y_send_sems,
        y_recv_sems,
    ) = refs[37:]
    w_me = lax.axis_index("wide")
    n_me = lax.axis_index("narrow")
    tokens, columns = local_ref.shape
    bank_rows = spans_ref.shape[1]
    length = tokens // bank_rows
    head = reward_ref.shape[1]
    banks, _, steps, generated = r_ref.shape
    share = wide // narrow
    half_owner = lax.div(w_me, share)
    place_in_half = lax.rem(w_me, share)

    barrier = pltpu.get_barrier_semaphore()
    for other in range(1, wide * narrow):
        flat = lax.rem(w_me * narrow + n_me + other, wide * narrow)
        pl.semaphore_signal(
            barrier,
            inc=1,
            device_id={"wide": lax.div(flat, narrow), "narrow": lax.rem(flat, narrow)},
            device_id_type=pl.DeviceIdType.MESH,
        )

    loads = [
        pltpu.make_async_copy(source, target, load_sems.at[number])
        for number, (source, target) in enumerate(zip(sources, loaded))
    ]
    first_loads = 4
    for load in loads[:first_loads]:
        load.start()

    held[w_me] = local_ref[...]

    line_me, side = lax.div(w_me, 2), lax.rem(w_me, 2)
    partner = 2 * line_me + 1 - side
    lines = wide // 2
    chunk_rows = tokens // chunks

    def owner_of(offset, own_side):
        return 2 * lax.bitwise_xor(line_me, offset) + (side if own_side else 1 - side)

    def line_copy(offset, chunk, arrival=False):
        piece = held.at[
            owner_of(offset, True) if arrival else w_me, pl.ds(chunk * chunk_rows, chunk_rows)
        ]
        return pltpu.make_async_remote_copy(
            src_ref=piece,
            dst_ref=piece,
            send_sem=line_send.at[offset - 1, chunk],
            recv_sem=line_recv.at[offset - 1, chunk],
            device_id={"wide": owner_of(offset, True)},
            device_id_type=pl.DeviceIdType.MESH,
        )

    def cross_copy(offset, chunk, arrival=False):
        piece = held.at[owner_of(offset, not arrival), pl.ds(chunk * chunk_rows, chunk_rows)]
        return pltpu.make_async_remote_copy(
            src_ref=piece,
            dst_ref=piece,
            send_sem=cross_send.at[offset, chunk],
            recv_sem=cross_recv.at[offset, chunk],
            device_id={"wide": partner},
            device_id_type=pl.DeviceIdType.MESH,
        )

    transposed = (((1,), (1,)), ((), ()))

    def with_difference(block):
        current = block.astype(jnp.float32)
        places = lax.broadcasted_iota(jnp.int32, current.shape, 0) & (length - 1)
        previous = jnp.where(places == 0, 0.0, pltpu.roll(current, 1, 0))
        return current, previous - current

    def add_hidden(owner):
        feature_rows = pl.ds(pl.multiple_of(owner * columns, columns), columns)
        current, difference = with_difference(held[owner])
        mixed = (current + difference * opening_ref[:, feature_rows]).astype(jnp.bfloat16)
        hidden_sum[...] += lax.dot_general(
            mixed, left[:, feature_rows], transposed, preferred_element_type=jnp.float32
        )

    def r_copy(bank, part):
        return pltpu.make_async_remote_copy(
            src_ref=r_send.at[bank, part],
            dst_ref=r_recv.at[w_me],
            send_sem=r_send_sems.at[bank, part],
            recv_sem=r_recv_sems.at[w_me],
            device_id={"wide": n_me * share + part, "narrow": bank},
            device_id_type=pl.DeviceIdType.MESH,
        )

    def r_arrival(prompt):
        return pltpu.make_async_remote_copy(
            src_ref=r_send.at[0, 0],
            dst_ref=r_recv.at[prompt],
            send_sem=r_send_sems.at[0, 0],
            recv_sem=r_recv_sems.at[prompt],
            device_id={"wide": prompt, "narrow": half_owner},
            device_id_type=pl.DeviceIdType.MESH,
        )

    def y_copy(prompt):
        return pltpu.make_async_remote_copy(
            src_ref=y_send.at[prompt],
            dst_ref=y_recv.at[n_me, place_in_half],
            send_sem=y_send_sems.at[prompt],
            recv_sem=y_recv_sems.at[n_me, place_in_half],
            device_id={"wide": prompt, "narrow": half_owner},
            device_id_type=pl.DeviceIdType.MESH,
        )

    def y_arrival(bank, part):
        return pltpu.make_async_remote_copy(
            src_ref=y_send.at[0],
            dst_ref=y_recv.at[bank, part],
            send_sem=y_send_sems.at[0],
            recv_sem=y_recv_sems.at[bank, part],
            device_id={"wide": n_me * share + part, "narrow": bank},
            device_id_type=pl.DeviceIdType.MESH,
        )

    def generated_is_mine(bank, part):
        return jnp.logical_and(n_me * share + part == w_me, n_me == bank)

    def prompt_is_mine(prompt):
        return jnp.logical_and(w_me == prompt, n_me == half_owner)

    pl.semaphore_wait(barrier, wide * narrow - 1)
    for chunk in range(chunks):
        cross_copy(0, chunk).start()
        for offset in range(1, lines):
            line_copy(offset, chunk).start()

    for load in loads[2:first_loads]:
        load.wait()
    hidden_sum[...] = jnp.zeros_like(hidden_sum)
    decay_sum[...] = jnp.zeros_like(decay_sum)
    key_sum[...] = jnp.zeros_like(key_sum)
    value_sum[...] = jnp.zeros_like(value_sum)
    for bank in range(banks):
        r_all = r_ref[bank, 0].astype(jnp.float32)
        w_all = jnp.exp(-jnp.exp(w_ref[bank, 0].astype(jnp.float32)))
        faded = None
        for step in range(steps):
            line = r_all[step : step + 1]
            if step > 0:
                now = w_all[step - 1 : step]
                faded = now if faded is None else faded * now
                line = line * faded
            for part in range(share):
                r_send[bank, part, step : step + 1, :] = line[
                    :, part * columns : (part + 1) * columns
                ]
    for bank in range(banks):
        for part in range(share):

            @pl.when(jnp.logical_not(generated_is_mine(bank, part)))
            def _():
                r_copy(bank, part).start()

    @pl.when(n_me == half_owner)
    def _():
        r_recv[w_me] = r_send[n_me, place_in_half]

    for load in loads[first_loads:]:
        load.start()
    for load in loads[:2]:
        load.wait()
    add_hidden(w_me)

    def gather_step(offset, carry):
        for chunk in range(chunks):
            line_copy(offset, chunk, True).wait_recv()
            cross_copy(offset, chunk).start()
        add_hidden(owner_of(offset, True))
        for chunk in range(chunks):
            cross_copy(offset - 1, chunk, True).wait_recv()
        add_hidden(owner_of(offset - 1, False))
        return carry

    lax.fori_loop(1, lines, gather_step, 0)
    for load in loads[first_loads:]:
        load.wait()
    for chunk in range(chunks):
        cross_copy(lines - 1, chunk, True).wait_recv()
    add_hidden(owner_of(lines - 1, False))

    hidden = jnp.tanh(hidden_sum[...])
    rank = right.shape[0] // 3
    hidden_lanes = lax.broadcasted_iota(jnp.int32, hidden.shape, 1)
    hidden_parts[...] = jnp.concatenate(
        [
            jnp.where(
                (hidden_lanes >= branch * rank) & (hidden_lanes < (branch + 1) * rank), hidden, 0.0
            )
            for branch in range(3)
        ],
        axis=0,
    ).astype(jnp.bfloat16)

    def project(pair, carry):
        span = pl.ds(pl.multiple_of(pair * 2 * columns, 2 * columns), 2 * columns)
        mixed = [[], [], []]
        for member in range(2):
            block = pair * 2 + member
            part = pl.ds(pl.multiple_of(block * columns, columns), columns)
            current, difference = with_difference(held[block])
            shifts = jnp.dot(
                hidden_parts[...], right[:, part], preferred_element_type=jnp.float32
            )
            for branch in range(3):
                blend = (
                    blends_ref[branch : branch + 1, part]
                    + shifts[branch * tokens : (branch + 1) * tokens]
                )
                mixed[branch].append((current + difference * blend).astype(jnp.bfloat16))
        decayed, keyed, valued = (jnp.concatenate(parts, axis=1) for parts in mixed)
        decay_sum[...] += jnp.dot(
            decayed, fading_left[span, :], preferred_element_type=jnp.float32
        )
        key_sum[...] += lax.dot_general(
            keyed, address[:, span], transposed, preferred_element_type=jnp.float32
        )
        value_sum[...] += lax.dot_general(
            valued, payload[:, span], transposed, preferred_element_type=jnp.float32
        )
        return carry

    lax.fori_loop(0, lines, project, 0)

    decay_hidden = jnp.tanh(decay_sum[...]).astype(jnp.bfloat16)
    rates = jnp.exp(
        fixed_ref[...]
        + jnp.dot(decay_hidden, fading_right_ref[...], preferred_element_type=jnp.float32)
    )
    row_ids = lax.broadcasted_iota(jnp.int32, (tokens, tokens), 0)
    column_ids = lax.broadcasted_iota(jnp.int32, (tokens, tokens), 1)
    row_limit = jnp.zeros((tokens, 1), jnp.int32)
    column_limit = jnp.zeros((tokens, tokens), jnp.int32)
    row_line = lax.broadcasted_iota(jnp.int32, (tokens, 1), 0)
    for prompt in range(bank_rows):
        span_now = spans_ref[0, prompt]
        row_limit = jnp.where(row_line & -length == prompt * length, span_now, row_limit)
        column_limit = jnp.where(column_ids & -length == prompt * length, span_now, column_limit)
    later = jnp.where(
        (row_ids & -length == column_ids & -length)
        & (column_ids > row_ids)
        & (column_ids & (length - 1) < column_limit),
        1.0,
        0.0,
    ).astype(jnp.bfloat16)
    high = rates.astype(jnp.bfloat16)
    low = (rates - high.astype(jnp.float32)).astype(jnp.bfloat16)
    remaining = jnp.dot(later, high, preferred_element_type=jnp.float32) + jnp.dot(
        later, low, preferred_element_type=jnp.float32
    )
    weights = jnp.where(row_line & (length - 1) < row_limit, jnp.exp(-remaining), 0.0)
    weighted = (
        key_sum[...].astype(jnp.bfloat16).astype(jnp.float32) * weights
    ).astype(jnp.bfloat16)
    values = value_sum[...].astype(jnp.bfloat16)

    for prompt in range(bank_rows):

        @pl.when(jnp.logical_not(prompt_is_mine(prompt)))
        def _():
            r_arrival(prompt).wait_recv()

    asked = jnp.concatenate([r_recv[prompt] for prompt in range(bank_rows)], axis=0)
    asked_rows = bank_rows * steps
    lane_heads = lax.broadcasted_iota(jnp.int32, (asked_rows, columns), 1) & -head
    heads = columns // head
    spread = jnp.concatenate(
        [jnp.where(lane_heads == number * head, asked, 0.0) for number in range(heads)], axis=0
    ).astype(jnp.bfloat16)
    scores = lax.dot_general(spread, weighted, transposed, preferred_element_type=jnp.float32)
    score_rows = lax.broadcasted_iota(jnp.int32, scores.shape, 0) & (asked_rows - 1)
    score_columns = lax.broadcasted_iota(jnp.int32, scores.shape, 1)
    kept = jnp.where(
        lax.shift_right_logical(score_rows, steps.bit_length() - 1)
        == lax.shift_right_logical(score_columns, length.bit_length() - 1),
        scores,
        0.0,
    )
    answers = jnp.dot(kept.astype(jnp.bfloat16), values, preferred_element_type=jnp.float32)
    answer = jnp.zeros((asked_rows, columns), jnp.float32)
    for number in range(heads):
        answer = jnp.where(
            lane_heads == number * head,
            answers[number * asked_rows : (number + 1) * asked_rows],
            answer,
        )
    for prompt in range(bank_rows):
        y_send[prompt] = answer[prompt * steps : (prompt + 1) * steps]
    for prompt in range(bank_rows):

        @pl.when(jnp.logical_not(prompt_is_mine(prompt)))
        def _():
            y_copy(prompt).start()

    @pl.when(n_me == half_owner)
    def _():
        y_recv[n_me, place_in_half] = y_send[w_me]

    ones = jnp.where(
        lax.broadcasted_iota(jnp.int32, (lane_count, lane_count), 0) & -head
        == lax.broadcasted_iota(jnp.int32, (lane_count, lane_count), 1) & -head,
        1.0,
        0.0,
    ).astype(jnp.bfloat16)
    first_head = pl.multiple_of(n_me * (generated // head), generated // head)
    rewards = reward_ref[pl.ds(first_head, generated // head), :]
    reward_line = jnp.concatenate(
        [rewards[number : number + 1, :] for number in range(generated // head)], axis=1
    )
    pair_rows = {}
    for bank in range(banks):
        r_all = r_ref[bank, 0].astype(jnp.float32)
        k_all = k_ref[bank, 0].astype(jnp.float32)
        w_all = jnp.exp(-jnp.exp(w_ref[bank, 0].astype(jnp.float32)))
        for step in range(steps):
            lagged = r_all[step : step + 1]
            for earlier in range(step, -1, -1):
                line = lagged * k_all[earlier : earlier + 1]
                if earlier == step:
                    line = line * reward_line
                elif earlier > 0:
                    lagged = lagged * w_all[earlier : earlier + 1]
                row = len(pair_rows)
                pair_rows[bank, step, earlier] = row
                pairs[row : row + 1, :] = line
    for row in range(len(pair_rows), pairs.shape[0]):
        pairs[row : row + 1, :] = jnp.zeros((1, generated), jnp.float32)
    sums = segment_sums(pairs[...], ones)
    for bank in range(banks):
        v_all = v_ref[bank, 0].astype(jnp.float32)
        for now in range(steps):
            line = None
            for earlier in range(now + 1):
                row = pair_rows[bank, now, earlier]
                term = sums[row : row + 1, :] * v_all[earlier : earlier + 1]
                line = term if line is None else line + term
            own_part[bank * steps + now : bank * steps + now + 1, :] = line
    gate_lines = []
    for bank in range(banks):
        gate = g_ref[bank, 0].astype(jnp.float32)
        gate_lines.append(gate / (1.0 + jnp.exp(-gate)))
    half_columns = pl.ds(pl.multiple_of(n_me * generated, generated), generated)
    gain = scaling_ref[:, half_columns]
    bias = offset_ref[:, half_columns]

    for chunk in range(chunks):
        for offset in range(lines):
            if offset > 0:
                line_copy(offset, chunk).wait_send()
            cross_copy(offset, chunk).wait_send()
    for bank in range(banks):
        for part in range(share):

            @pl.when(jnp.logical_not(generated_is_mine(bank, part)))
            def _():
                r_copy(bank, part).wait_send()

    for bank in range(banks):
        for part in range(share):

            @pl.when(jnp.logical_not(generated_is_mine(bank, part)))
            def _():
                y_arrival(bank, part).wait_recv()

    received = jnp.concatenate(
        [
            jnp.concatenate([y_recv[bank, part] for part in range(share)], axis=1)
            for bank in range(banks)
        ],
        axis=0,
    )
    y = received + own_part[...]
    centred = y - segment_sums(y, ones) * (1.0 / head)
    variance = segment_sums(centred * centred, ones) * (1.0 / head)
    normed = centred * lax.rsqrt(variance + norm_eps) * gain + bias
    for bank in range(banks):
        out_ref[bank, 0] = (normed[bank * steps : (bank + 1) * steps] * gate_lines[bank]).astype(
            out_ref.dtype
        )
    for prompt in range(bank_rows):

        @pl.when(jnp.logical_not(prompt_is_mine(prompt)))
        def _():
            y_copy(prompt).wait_send()


def mixing(wide, narrow, local, *operands):
    tokens, columns = local.shape
    left, receptance, fading_left, spans = operands[0], operands[2], operands[6], operands[11]
    bank_rows = spans.shape[1]
    banks, _, steps, generated = receptance.shape
    share = wide // narrow
    chunks = bank_rows // 2
    pair_count = -(-(banks * steps * (steps + 1) // 2) // 8) * 8
    vmem = pl.BlockSpec(memory_space=pltpu.VMEM)
    far = pl.BlockSpec(memory_space=pl.ANY)
    f32 = jnp.float32
    dma = pltpu.SemaphoreType.DMA
    return pl.pallas_call(
        functools.partial(mixing_body, wide, narrow, chunks),
        out_shape=jax.ShapeDtypeStruct(receptance.shape, jnp.bfloat16),
        in_specs=[vmem] + [far] * len(operands),
        out_specs=vmem,
        scratch_shapes=[
            pltpu.SMEM(operand.shape, operand.dtype)
            if operand is spans
            else pltpu.VMEM(operand.shape, operand.dtype)
            for operand in operands
        ]
        + [
            pltpu.VMEM((wide, tokens, columns), jnp.bfloat16),
            pltpu.VMEM((3 * tokens, left.shape[0]), jnp.bfloat16),
            pltpu.VMEM((tokens, left.shape[0]), f32),
            pltpu.VMEM((tokens, columns), f32),
            pltpu.VMEM((tokens, columns), f32),
            pltpu.VMEM((tokens, fading_left.shape[1]), f32),
            pltpu.VMEM((pair_count, generated), f32),
            pltpu.VMEM((banks * steps, generated), f32),
            pltpu.VMEM((banks, share, steps, columns), f32),
            pltpu.VMEM((bank_rows, steps, columns), f32),
            pltpu.VMEM((bank_rows, steps, columns), f32),
            pltpu.VMEM((banks, share, steps, columns), f32),
            dma((len(operands),)),
            dma((wide // 2 - 1, chunks)),
            dma((wide // 2 - 1, chunks)),
            dma((wide // 2, chunks)),
            dma((wide // 2, chunks)),
            dma((banks, share)),
            dma((bank_rows,)),
            dma((bank_rows,)),
            dma((banks, share)),
        ],
        compiler_params=pltpu.CompilerParams(
            collective_id=0, has_side_effects=True, vmem_limit_bytes=52 * 2**20
        ),
        name="mix_and_generate",
    )(local, *operands)


def power_of_two(number):
    return number > 0 and number & (number - 1) == 0


def fits_kernels(wide, narrow, ids, table, reward, acceptance):
    bank_rows, length = ids.shape[1], ids.shape[2]
    columns = table.shape[0]
    banks, prompts, steps, generated = acceptance.shape
    return (
        prompts == 1
        and wide % 2 == 0
        and wide > 2
        and wide % narrow == 0
        and banks == narrow
        and bank_rows == wide
        and length % 16 == 0
        and columns % lane_count == 0
        and table.shape[1] % lane_count == 0
        and generated == columns * (wide // narrow)
        and lane_count % reward.shape[1] == 0
        and all(power_of_two(size) for size in (length, steps, bank_rows, reward.shape[1]))
        and columns * length * bank_rows * lane_count * 2 <= 2**25
    )


def per_device(
    context_symbol_ids,
    context_symbol_spans,
    symbol_vector_lookup,
    opening_lagged_blend,
    lagged_blend_weights,
    blending_left_operand,
    blending_right_operands,
    fixed_fading_scores,
    fading_left_operand,
    fading_right_operand,
    address_projector,
    payload_projector,
    present_symbol_reward,
    cluster_scaling_weight,
    cluster_scaling_offset,
    generated_acceptance,
    generated_addresses,
    generated_payloads,
    generated_fading_scores,
    generated_valve_scores,
):
    wide, narrow = lax.axis_size("wide"), lax.axis_size("narrow")
    if fits_kernels(
        wide,
        narrow,
        context_symbol_ids,
        symbol_vector_lookup,
        present_symbol_reward,
        generated_acceptance,
    ):
        return mixing(
            wide,
            narrow,
            gather_tokens(context_symbol_ids, symbol_vector_lookup),
            blending_left_operand.T,
            opening_lagged_blend[None],
            generated_acceptance,
            generated_fading_scores,
            blending_right_operands.reshape(-1, blending_right_operands.shape[2]),
            lagged_blend_weights,
            fading_left_operand,
            address_projector,
            payload_projector,
            fixed_fading_scores[None],
            fading_right_operand,
            context_symbol_spans,
            generated_addresses,
            generated_payloads,
            generated_valve_scores,
            present_symbol_reward,
            cluster_scaling_weight[None],
            cluster_scaling_offset[None],
        )
    bank_rows = context_symbol_ids.shape[1]
    length = context_symbol_ids.shape[2]
    columns = symbol_vector_lookup.shape[0]
    attender_width = present_symbol_reward.shape[1]
    head_local = columns // attender_width
    lengths = context_symbol_spans.reshape(-1)
    picked = jnp.take(symbol_vector_lookup, context_symbol_ids.reshape(-1), axis=1)
    gathered = lax.all_gather(picked, "wide", axis=0, tiled=True).T
    features = gathered.shape[1]
    block_rows = bank_rows
    while block_rows % 2 == 0 and block_rows * length > 1024:
        block_rows = block_rows // 2
    blocks = gathered.reshape(bank_rows // block_rows, block_rows, length, features)
    length_blocks = lengths.reshape(bank_rows // block_rows, block_rows)

    def one_block(block_item):
        key_proj, value_proj, decay_log = mix_project(
            block_item[0],
            opening_lagged_blend,
            lagged_blend_weights,
            blending_left_operand,
            blending_right_operands,
            fixed_fading_scores,
            fading_left_operand,
            fading_right_operand,
            address_projector,
            payload_projector,
        )
        block_shape = (block_rows, length, columns)
        return final_states(
            key_proj.reshape(block_shape),
            value_proj.reshape(block_shape),
            decay_log.reshape(block_shape),
            block_item[1],
            attender_width,
        )

    recurrent_memories = lax.map(one_block, (blocks, length_blocks)).reshape(
        bank_rows, head_local, attender_width, attender_width
    )
    handed = lax.all_to_all(
        lax.all_to_all(
            recurrent_memories.reshape(1, bank_rows, head_local, attender_width * attender_width),
            "wide",
            split_axis=1,
            concat_axis=2,
            tiled=True,
        ),
        "narrow",
        split_axis=2,
        concat_axis=0,
        tiled=True,
    )
    generated_by_attender = handed.shape[2]
    leading_attender_offset = lax.axis_index("narrow") * generated_by_attender
    shard_reward = lax.dynamic_slice_in_dim(
        present_symbol_reward, leading_attender_offset, generated_by_attender, 0
    )
    shard_scaling_weight = lax.dynamic_slice_in_dim(
        cluster_scaling_weight,
        leading_attender_offset * attender_width,
        generated_by_attender * attender_width,
        0,
    )
    shard_scaling_offset = lax.dynamic_slice_in_dim(
        cluster_scaling_offset,
        leading_attender_offset * attender_width,
        generated_by_attender * attender_width,
        0,
    )
    result = generation_iterations(
        handed.reshape(handed.shape[:3] + (attender_width, attender_width)),
        generated_acceptance,
        generated_addresses,
        generated_payloads,
        generated_fading_scores,
        generated_valve_scores,
        shard_reward,
        shard_scaling_weight,
        shard_scaling_offset,
    )
    return result


def solution(mesh):
    placed = (
        P("narrow", "groups", None),
        P("narrow", "groups"),
        P("wide", None),
        P(),
        P(),
        P(),
        P(),
        P("wide"),
        P(),
        P(None, "wide"),
        P("wide", None),
        P("wide", None),
        P(),
        P(),
        P(),
        P(None, ("groups", "wide"), None, "narrow"),
        P(None, ("groups", "wide"), None, "narrow"),
        P(None, ("groups", "wide"), None, "narrow"),
        P(None, ("groups", "wide"), None, "narrow"),
        P(None, ("groups", "wide"), None, "narrow"),
    )
    return jax.shard_map(
        per_device,
        mesh=mesh,
        in_specs=placed,
        out_specs=P(None, ("groups", "wide"), None, "narrow"),
        check_vma=False,
    )
```
